128 devices in a mesh: tx: 16 (over y, x), ty: 8 (over z, core).
Axes of the slice: x: 4, y: 4, z: 4, core: 2. Of those that a mesh axis runs over, the one named last changes fastest.
Arguments:
- earlier: bfloat16 [64, 32, 256, 128], P('tx', 'ty'), may hold values from -6 to 6
- innovation: bfloat16 [64, 32, 256, 128], P('tx', 'ty'), may hold values from -6 to 6
- conditioner: bfloat16 [64, 32, 1024, 128], P('tx', 'ty'), may hold values from -0.125 to 0.125
- chol_factor: bfloat16 [64, 32, 128, 128], P('tx', 'ty'), may hold values from -0.5 to 0.5
- block_level: int32 [64, 32], P('tx', 'ty'), may hold values from 0 to 3, as said below
- neighbours: int32 [64, 32, 8], P('tx', 'ty'), may hold values from 0 to 17, as said below
Outputs:
- window: bfloat16 [64, 32, 256, 128], P('tx', 'ty')
The draws below stay inside these ranges and needn't reach their ends.
Inputs may be any that keep to these rules, and one draw needn't show every extreme that they name: `block_level`: in each device's tile of 4 x 4 cells no level holds more than 8 blocks, and one level holds exactly 8. `neighbours`: A code q < 9 names the earlier-level block at cell offset (q // 3 - 1, q mod 3 - 1), with periodic wrap; a code q >= 9 names the window block at offset ((q - 9) // 3 - 1, (q - 9) mod 3 - 1), whose level is always lower than the block's own. The 8 codes of a block are distinct.
All inputs are finite; a program needn't handle non-finite values.
Results may differ from the reference program's by a relative error of at most 0.0023.
Values may be sent and summed in bfloat16 or wider, within the bound.
No kernel may reach another device: no remote copies, remote signals or barrier semaphores. Data moves between devices by JAX's collectives and lax.ppermute only.
A program may use at most 64 MiB of HBM per device.

```python
import jax
import jax.numpy as jnp
from jax import lax

BS = 128
NBR = 8
LEVELS = 4
R = 256
GX = 4
GY = 4
NGX = 64
NGY = 32


def level_map(key):
    tiles_x = NGX // GX
    tiles_y = NGY // GY
    tile_count = tiles_x * tiles_y
    tile_cells = GX * GY
    keys = jax.random.split(jax.random.fold_in(key, 11), tile_count)
    orders = jax.vmap(lambda single: jax.random.permutation(single, tile_cells))(keys)
    heavy = jax.random.randint(jax.random.fold_in(key, 12), (tile_count, 1), 0, LEVELS)
    others = jax.random.randint(jax.random.fold_in(key, 13), (tile_count, tile_cells), 0, LEVELS - 1)
    others = others + (others >= heavy).astype(jnp.int32)
    levels = jnp.where(orders < tile_cells // 2, heavy, others)
    levels = levels.reshape(tiles_x, tiles_y, GX, GY).transpose(0, 2, 1, 3).reshape(NGX, NGY)
    return levels.astype(jnp.int32)


def draw_block_level(key, part):
    return level_map(key)


def draw_neighbours(key, part):
    levels = level_map(key)
    key = jax.random.fold_in(key, 21)
    shifted = []
    for offset in range(9):
        shifted.append(jnp.roll(levels, (1 - offset // 3, 1 - offset % 3), axis=(0, 1)))
    shifted = jnp.stack(shifted, axis=-1)
    lower = shifted < levels[:, :, None]
    eligible = jnp.concatenate([jnp.ones((NGX, NGY, 9), dtype=bool), lower], axis=-1)
    scores = jax.random.randint(key, (NGX, NGY, 18), 0, 1 << 20) * 32 + jnp.arange(18, dtype=jnp.int32)
    scores = jnp.where(eligible, scores, -1)
    picked = lax.top_k(scores, NBR)[1]
    return picked.astype(jnp.int32)


def steps_of(own_key, shape, cuts, low, top_value):
    level = 1.0
    for axis_at, blocks in cuts:
        draws = jax.random.uniform(jax.random.fold_in(jax.random.fold_in(own_key, 6), axis_at), (blocks,), jnp.float32, low / len(cuts), top_value / len(cuts))
        level = level * jnp.repeat(jnp.exp(draws), shape[axis_at] // blocks).reshape((-1,) + (1,) * (len(shape) - 1 - axis_at))
    return level


def normal_values(stream_key, shape, deviation, limit, pieces=(), held_as=jnp.bfloat16):
    gain = steps_of(stream_key, shape, pieces, -0.22, 0.18) if pieces else 1.0
    array = jax.random.normal(stream_key, shape, jnp.float32) * deviation * gain
    return jnp.minimum(jnp.maximum(array, -limit), limit).astype(held_as)


def setup_inputs(seed: int = 0) -> dict:
    key_list = jax.random.split(jax.random.key(seed), 7)
    return {
        "earlier": normal_values(key_list[0], (NGX, NGY, R, BS), 1.0, 6.0, ((0, 16), (1, 8))),
        "innovation": normal_values(key_list[1], (NGX, NGY, R, BS), 1.0, 6.0, ((0, 16), (1, 8))),
        "conditioner": normal_values(key_list[2], (NGX, NGY, NBR * BS, BS), (2 * NBR * BS) ** -0.5, 0.125, ((0, 16), (1, 8))),
        "chol_factor": normal_values(key_list[3], (NGX, NGY, BS, BS), BS ** -0.5, 0.5, ((0, 16), (1, 8))),
        "block_level": draw_block_level(jax.random.fold_in(key_list[6], 71), 0),
        "neighbours": draw_neighbours(jax.random.fold_in(key_list[6], 71), 0),
    }


def reference(earlier, innovation, conditioner, chol_factor, block_level, neighbours):
    grid_x = block_level.shape[0]
    grid_y = block_level.shape[1]

    def one_level(window, section):
        lookup = jnp.stack([earlier, window])

        def block(index):
            pos_x = index // grid_y
            pos_y = index % grid_y
            near_codes = neighbours[pos_x, pos_y]
            offset = near_codes % 9
            source_kind = near_codes // 9
            row_index = (pos_x + offset // 3 - 1) % grid_x
            col_index = (pos_y + offset % 3 - 1) % grid_y

            def compute(unused):
                gathered = lookup[source_kind, row_index, col_index].astype(jnp.float32)
                matrices = conditioner[pos_x, pos_y].astype(jnp.float32).reshape(NBR, BS, BS)
                summed = jnp.einsum("krb,kbo->ro", gathered, matrices)
                summed = summed + jnp.dot(innovation[pos_x, pos_y], jnp.triu(chol_factor[pos_x, pos_y]), preferred_element_type=jnp.float32)
                return summed.astype(jnp.bfloat16)

            def keep(unused):
                return window[pos_x, pos_y]

            return lax.cond(block_level[pos_x, pos_y] == section, compute, keep, 0)

        values = lax.map(block, jnp.arange(grid_x * grid_y, dtype=jnp.int32))
        return values.reshape(window.shape)

    window = jnp.zeros(earlier.shape, jnp.bfloat16)
    for section in range(LEVELS):
        window = one_level(window, section)
    return window
```

```python
import functools

import jax
import jax.numpy as jnp
import numpy as np
from jax import lax
from jax.experimental import pallas as pl
from jax.experimental.pallas import tpu as pltpu
from jax.sharding import PartitionSpec as P

LEVELS = 4
BOTH = ("tx", "ty")
PIECES = (("ty_in", 4), ("ty_out_ends", 2), ("ty_out_mid", 2), ("tx_out", 4), ("tx_in", 4), ("tx_out_ends", 2), ("tx_in_ends", 2))
TILE = 16
HALO = 20
SLOTS = TILE + HALO


def slot_table():
    table = np.zeros((2, 2, TILE, 9), np.int32)
    for odd_x in range(2):
        for odd_y in range(2):
            in_x, out_x = (-1, 4) if odd_x else (4, -1)
            in_y, out_y = (-1, 4) if odd_y else (4, -1)
            place = {(x, y): 4 * x + y for x in range(4) for y in range(4)}
            order = [(x, in_y) for x in range(4)] + [(0, out_y), (3, out_y), (1, out_y), (2, out_y)]
            order += [(out_x, y) for y in range(4)] + [(in_x, y) for y in range(4)]
            order += [(out_x, in_y), (out_x, out_y), (in_x, in_y), (in_x, out_y)]
            for at, cell in enumerate(order):
                place[cell] = TILE + at
            for x in range(4):
                for y in range(4):
                    for j in range(9):
                        table[odd_x, odd_y, 4 * x + y, j] = place[(x + j // 3 - 1, y + j % 3 - 1)]
    return table


def send_table():
    table = np.zeros((2, 2, 16), np.int32)
    for odd_x in range(2):
        for odd_y in range(2):
            in_x, out_x = (0, 3) if odd_x else (3, 0)
            in_y, out_y = (0, 3) if odd_y else (3, 0)
            order = [(x, in_y) for x in range(4)] + [(0, out_y), (3, out_y), (1, out_y), (2, out_y)]
            order += [(out_x, y) for y in range(4)] + [(in_x, y) for y in range(4)]
            table[odd_x, odd_y] = [4 * x + y for x, y in order]
    return table


def partners(size_x, size_y, along_x, along_y):
    def other(at, size, kind):
        if kind == "in":
            return at ^ 1
        if kind == "out":
            return (((at + 1) % size) ^ 1) - 1 if at % 2 == 0 and at else (at + 1) % size if at % 2 else size - 1
        return at

    return [
        (x * size_y + y, other(x, size_x, along_x) * size_y + other(y, size_y, along_y))
        for x in range(size_x)
        for y in range(size_y)
    ]


def exchange(sends, odd_x):
    size_x, size_y = lax.axis_size("tx"), lax.axis_size("ty")
    swap = lambda value, x, y: lax.ppermute(value, BOTH, partners(size_x, size_y, x, y))
    ty_in, ty_ends, ty_mid, tx_out, tx_in = sends
    got_ty_ends = swap(ty_ends, None, "out")
    got_ty_in = swap(ty_in, None, "in")
    got_tx_out = swap(tx_out, "out", None)
    got_tx_in = swap(tx_in, "in", None)
    got_ty_mid = swap(ty_mid, None, "out")
    first = jnp.stack([got_ty_in[0], got_ty_ends[0]])
    last = jnp.stack([got_ty_in[3], got_ty_ends[1]])
    got_tx_out_ends = swap(jnp.where(odd_x, last, first), "out", None)
    got_tx_in_ends = swap(jnp.where(odd_x, first, last), "in", None)
    return got_ty_in, got_ty_ends, got_ty_mid, got_tx_out, got_tx_in, got_tx_out_ends, got_tx_in_ends


def level_kernel(section, send, level, slots, order, earlier, window, innovation, conditioner, chol_factor, *rest):
    pieces = len(PIECES)
    halos = [rest[:pieces]]
    rest = rest[pieces:]
    if section:
        halos.append(rest[:pieces])
        rest = rest[pieces:]
    result, *sends, sources = rest
    sources[0:TILE] = earlier[...]
    for half, halo in enumerate(halos):
        base = half * SLOTS + TILE
        for ref in halo:
            sources[base : base + ref.shape[0]] = ref[...]
            base += ref.shape[0]
    if section:
        sources[SLOTS : SLOTS + TILE] = window[...]
    rows = lax.broadcasted_iota(jnp.int32, (128, 128), 0)
    columns = lax.broadcasted_iota(jnp.int32, (128, 128), 1)
    upper = rows <= columns

    def one_cell(cell, carry):
        @pl.when(level[cell] == section)
        def _():
            gathered = jnp.concatenate([sources[slots[cell * 8 + k]] for k in range(8)], axis=1)
            factor = jnp.where(upper, chol_factor[cell].astype(jnp.float32), 0.0).astype(jnp.bfloat16)
            summed = jnp.dot(gathered, conditioner[cell], preferred_element_type=jnp.float32)
            summed += jnp.dot(innovation[cell], factor, preferred_element_type=jnp.float32)
            sources[SLOTS + cell] = summed.astype(jnp.bfloat16)

        return carry

    lax.fori_loop(0, TILE, one_cell, 0)
    at = 0
    for ref in sends:
        for i in range(ref.shape[0]):
            ref[i] = sources[SLOTS + order[at]]
            at += 1
    result[...] = sources[SLOTS : SLOTS + TILE]


def run_level(section, level, slots, order, earlier, window, innovation, conditioner, chol_factor, halos):
    block = earlier.shape[1:]
    send = section < LEVELS - 1
    smem = pl.BlockSpec(memory_space=pltpu.SMEM)
    vmem = pl.BlockSpec(memory_space=pltpu.VMEM)
    flat = [piece for halo in halos for piece in halo]
    shapes = [jax.ShapeDtypeStruct((TILE, *block), jnp.bfloat16)]
    if send:
        shapes += [jax.ShapeDtypeStruct((count, *block), jnp.bfloat16) for _, count in PIECES[:5]]
    return pl.pallas_call(
        functools.partial(level_kernel, section, send),
        out_shape=shapes,
        in_specs=[smem] * 3 + [vmem] * (5 + len(flat)),
        out_specs=[vmem] * len(shapes),
        scratch_shapes=[pltpu.VMEM((2 * SLOTS, *block), jnp.bfloat16)],
        compiler_params=pltpu.CompilerParams(vmem_limit_bytes=32 * 1024 * 1024),
        cost_estimate=pl.CostEstimate(flops=4 * 2 * 256 * 1152 * 128, bytes_accessed=8 << 20, transcendentals=0),
        name=f"level_{section}",
    )(level, slots, order, earlier, window, innovation, conditioner, chol_factor, *flat)


def local(earlier, innovation, conditioner, chol_factor, block_level, neighbours):
    block = earlier.shape[2:]
    odd_x = lax.axis_index("tx") % 2
    odd_y = lax.axis_index("ty") % 2
    in_x, out_x = 3 - 3 * odd_x, 3 * odd_x
    in_y, out_y = 3 - 3 * odd_y, 3 * odd_y
    out_column = lax.dynamic_index_in_dim(earlier, out_y, 1, keepdims=False)
    sends = (
        lax.dynamic_index_in_dim(earlier, in_y, 1, keepdims=False),
        jnp.stack([out_column[0], out_column[3]]),
        out_column[1:3],
        lax.dynamic_index_in_dim(earlier, out_x, 0, keepdims=False),
        lax.dynamic_index_in_dim(earlier, in_x, 0, keepdims=False),
    )
    halos = [exchange(sends, odd_x)]

    table = jnp.asarray(slot_table().reshape(4, TILE, 9))[2 * odd_x + odd_y]
    order = jnp.asarray(send_table().reshape(4, 16))[2 * odd_x + odd_y]
    codes = neighbours.reshape(TILE, 8)
    hits = (codes % 9)[:, :, None] == jnp.arange(9, dtype=jnp.int32)
    slots = jnp.sum(jnp.where(hits, table[:, None, :], 0), axis=-1) + SLOTS * (codes // 9)
    slots = slots.reshape(TILE * 8)
    level = block_level.reshape(TILE)

    own = earlier.reshape(TILE, *block)
    noise = innovation.reshape(TILE, *block)
    matrices = conditioner.reshape(TILE, *conditioner.shape[2:])
    factors = chol_factor.reshape(TILE, *chol_factor.shape[2:])
    window = own
    for section in range(LEVELS):
        window, *sends = run_level(section, level, slots, order, own, window, noise, matrices, factors, halos)
        if sends:
            halos = [halos[0], exchange(sends, odd_x)]
    return window.reshape(earlier.shape)


def solution(mesh):
    placed = (
        P("tx", "ty", None, None),
        P("tx", "ty", None, None),
        P("tx", "ty", None, None),
        P("tx", "ty", None, None),
        P("tx", "ty"),
        P("tx", "ty", None),
    )
    return jax.shard_map(
        local, mesh=mesh, in_specs=placed, out_specs=P("tx", "ty", None, None), check_vma=False
    )
```

```python
import functools

import jax
import jax.numpy as jnp
from jax import lax
from jax.experimental import pallas as pl
from jax.experimental.pallas import tpu as pltpu
from jax.sharding import PartitionSpec as P

LEVELS = 4
BOTH = ("tx", "ty")
SIDE = 4
GRID = 6
PLANE = GRID * GRID
BLANK = 2 * PLANE
CORNERS = ((0, 0), (0, 3), (3, 0), (3, 3))
VMEM = pl.BlockSpec(memory_space=pltpu.VMEM)
SMEM = pl.BlockSpec(memory_space=pltpu.SMEM)
ANY = pl.BlockSpec(memory_space=pl.ANY)
PARAMS = pltpu.CompilerParams(vmem_limit_bytes=20 * 1024 * 1024)


def partner(at, size, kind):
    if kind == "in":
        return at ^ 1
    if kind == "out":
        return (at + 1) % size if at % 2 else (at - 1) % size
    return at


def swap(value, along_x, along_y):
    size_x, size_y = lax.axis_size("tx"), lax.axis_size("ty")
    pairs = [
        (x * size_y + y, partner(x, size_x, along_x) * size_y + partner(y, size_y, along_y))
        for x in range(size_x)
        for y in range(size_y)
    ]
    return lax.ppermute(value, BOTH, pairs)


def edges():
    odd_x = lax.rem(lax.axis_index("tx"), 2)
    odd_y = lax.rem(lax.axis_index("ty"), 2)
    return 3 * odd_x, 3 - 3 * odd_x, 3 * odd_y, 3 - 3 * odd_y


def exchange_edges(sends):
    tx_out, tx_in, ty_out, ty_in = sends
    return swap(tx_out, "out", None), swap(tx_in, "in", None), swap(ty_out, None, "out"), swap(ty_in, None, "in")


def exchange_corners(halo, odd_y):
    tx_out, tx_in = halo[:2]
    first = jnp.stack([tx_out[0], tx_in[0]])
    last = jnp.stack([tx_out[3], tx_in[3]])
    return swap(jnp.where(odd_y, last, first), None, "out"), swap(jnp.where(odd_y, first, last), None, "in")


def pack_kernel(earlier, tx_out, tx_in, ty_out, ty_in, sems):
    out_x, in_x, out_y, in_y = edges()
    copies = [
        pltpu.make_async_copy(earlier.at[out_x], tx_out, sems.at[0]),
        pltpu.make_async_copy(earlier.at[in_x], tx_in, sems.at[1]),
        pltpu.make_async_copy(earlier.at[:, out_y], ty_out, sems.at[2]),
        pltpu.make_async_copy(earlier.at[:, in_y], ty_in, sems.at[3]),
    ]
    for copy in copies:
        copy.start()
    for copy in copies:
        copy.wait()


def load_kernel(earlier, innovation, conditioner, chol_factor, plane, matrices, noise, shocks, factors, sems):
    copies = [
        pltpu.make_async_copy(innovation, shocks, sems.at[0]),
        pltpu.make_async_copy(chol_factor, factors, sems.at[1]),
        pltpu.make_async_copy(conditioner, matrices, sems.at[2]),
    ]
    copies += [
        pltpu.make_async_copy(earlier.at[x], plane.at[pl.ds((x + 1) * GRID + 1, SIDE)], sems.at[3 + x])
        for x in range(SIDE)
    ]
    for copy in copies:
        copy.start()
    plane[BLANK] = jnp.zeros(plane.shape[1:], plane.dtype)
    rows = lax.broadcasted_iota(jnp.int32, factors.shape[2:], 0)
    columns = lax.broadcasted_iota(jnp.int32, factors.shape[2:], 1)
    upper = rows <= columns
    copies[0].wait()
    copies[1].wait()

    def one_cell(cell, carry):
        x, y = cell // SIDE, cell % SIDE
        factor = jnp.where(upper, factors[x, y].astype(jnp.float32), 0.0).astype(jnp.bfloat16)
        noise[cell] = jnp.dot(shocks[x, y], factor, preferred_element_type=jnp.float32)
        return carry

    lax.fori_loop(0, SIDE * SIDE, one_cell, 0)
    for copy in copies[2:]:
        copy.wait()


def slot_of(code, x, y):
    old = (code >= 9).astype(jnp.int32)
    offset = code - 9 * old
    down = (offset >= 3).astype(jnp.int32) + (offset >= 6).astype(jnp.int32)
    return (x + down) * GRID + y + (offset - 3 * down) + PLANE * old


def main_kernel(section, levels, codes, plane_in, matrices, noise, tx_out, tx_in, ty_out, ty_in, plane, partial, *rest):
    base = PLANE if section else 0
    out_x, in_x, out_y, in_y = edges()
    for i in range(SIDE):
        plane[base + (out_x // 3) * 5 * GRID + i + 1] = tx_out[i]
        plane[base + (in_x // 3) * 5 * GRID + i + 1] = tx_in[i]
        plane[base + (i + 1) * GRID + (out_y // 3) * 5] = ty_out[i]
        plane[base + (i + 1) * GRID + (in_y // 3) * 5] = ty_in[i]
    late = tuple(base + row * GRID + column for row in (0, 5) for column in (0, 5))

    def one_cell(cell, carry):
        x, y = cell // SIDE, cell % SIDE

        @pl.when(levels[x, y] == section)
        def _():
            parts = []
            for k in range(8):
                slot = slot_of(codes[x, y, k], x, y)
                for corner in late:
                    slot = jnp.where(slot == corner, BLANK, slot)
                parts.append(plane[slot])
            summed = noise[cell] + jnp.dot(
                jnp.concatenate(parts, axis=1), matrices[x, y], preferred_element_type=jnp.float32
            )
            plane[PLANE + (x + 1) * GRID + y + 1] = summed.astype(jnp.bfloat16)
            at_corner = ((x == 0) | (x == 3)) & ((y == 0) | (y == 3))

            @pl.when(at_corner)
            def _():
                partial[(x // 3) * 2 + y // 3] = summed

        return carry

    lax.fori_loop(0, SIDE * SIDE, one_cell, 0)
    if rest:
        result, sems = rest
        copies = [
            pltpu.make_async_copy(
                plane.at[pl.ds(PLANE + (x + 1) * GRID + 1, SIDE)], result.at[x], sems.at[x]
            )
            for x in range(SIDE)
        ]
        for copy in copies:
            copy.start()
        for copy in copies:
            copy.wait()


def corner_kernel(section, levels, codes, plane_in, matrices, partial, far, near, *rest):
    if section == LEVELS - 1:
        result_in, plane, result, sems = rest
    else:
        plane, tx_out, tx_in, ty_out, ty_in = rest
    out_x, in_x, out_y, in_y = edges()
    for at, (x, y) in enumerate(CORNERS):
        side = jnp.where(out_x == x, 0, 1)
        code = 2 * x + 2 * y // 3 + 9 * (section > 0)
        late = (PLANE if section else 0) + (x // 3) * 5 * GRID + (y // 3) * 5
        outward = out_y == y

        def block():
            return jnp.where(outward, far[side], near[side])

        if section == 0:
            plane[late] = block()

        @pl.when(levels[x, y] == section)
        def _():
            for k in range(8):

                @pl.when(codes[x, y, k] == code)
                def _():
                    summed = partial[at] + jnp.dot(
                        block(), matrices[x, y, 128 * k : 128 * (k + 1)], preferred_element_type=jnp.float32
                    )
                    plane[PLANE + (x + 1) * GRID + y + 1] = summed.astype(jnp.bfloat16)

    if section == LEVELS - 1:
        copies = [
            pltpu.make_async_copy(plane.at[PLANE + (x + 1) * GRID + y + 1], result.at[x, y], sems.at[at])
            for at, (x, y) in enumerate(CORNERS)
        ]
        for copy in copies:
            copy.start()
        for copy in copies:
            copy.wait()
    else:
        for i in range(SIDE):
            tx_out[i] = plane[PLANE + (out_x + 1) * GRID + i + 1]
            tx_in[i] = plane[PLANE + (in_x + 1) * GRID + i + 1]
            ty_out[i] = plane[PLANE + (i + 1) * GRID + out_y + 1]
            ty_in[i] = plane[PLANE + (i + 1) * GRID + in_y + 1]


def local(earlier, innovation, conditioner, chol_factor, block_level, neighbours):
    block = earlier.shape[2:]
    odd_y = lax.rem(lax.axis_index("ty"), 2) == 1
    edge = jax.ShapeDtypeStruct((SIDE, *block), jnp.bfloat16)
    plane_shape = jax.ShapeDtypeStruct((BLANK + 1, *block), jnp.bfloat16)
    whole = jax.ShapeDtypeStruct(earlier.shape, jnp.bfloat16)
    sends = pl.pallas_call(
        pack_kernel,
        out_shape=[edge] * 4,
        in_specs=[ANY],
        out_specs=[VMEM] * 4,
        scratch_shapes=[pltpu.SemaphoreType.DMA((4,))],
        compiler_params=PARAMS,
        name="pack",
    )(earlier)
    plane, matrices, noise = pl.pallas_call(
        load_kernel,
        out_shape=[
            plane_shape,
            jax.ShapeDtypeStruct(conditioner.shape, jnp.bfloat16),
            jax.ShapeDtypeStruct((SIDE * SIDE, *block), jnp.float32),
        ],
        in_specs=[ANY] * 4,
        out_specs=[VMEM] * 3,
        scratch_shapes=[
            pltpu.VMEM(innovation.shape, jnp.bfloat16),
            pltpu.VMEM(chol_factor.shape, jnp.bfloat16),
            pltpu.SemaphoreType.DMA((7,)),
        ],
        compiler_params=PARAMS,
        cost_estimate=pl.CostEstimate(flops=2 * 16 * 256 * 128 * 128, bytes_accessed=14 << 20, transcendentals=0),
        name="load",
    )(earlier, innovation, conditioner, chol_factor)
    for section in range(LEVELS):
        final = section == LEVELS - 1
        halo = exchange_edges(sends)
        far, near = exchange_corners(halo, odd_y)
        plane, partial, *result = pl.pallas_call(
            functools.partial(main_kernel, section),
            out_shape=[plane_shape, jax.ShapeDtypeStruct((4, *block), jnp.float32)] + [whole] * final,
            in_specs=[SMEM] * 2 + [VMEM] * 7,
            out_specs=[VMEM] * 2 + [ANY] * final,
            scratch_shapes=[pltpu.SemaphoreType.DMA((4,))] * final,
            input_output_aliases={2: 0},
            compiler_params=PARAMS,
            cost_estimate=pl.CostEstimate(flops=8 * 2 * 256 * 1024 * 128, bytes_accessed=4 << 20, transcendentals=0),
            name=f"main_{section}",
        )(block_level, neighbours, plane, matrices, noise, *halo)
        plane, *sends = pl.pallas_call(
            functools.partial(corner_kernel, section),
            out_shape=[plane_shape] + ([whole] if final else [edge] * 4),
            in_specs=[SMEM] * 2 + [VMEM] * 5 + [ANY] * final,
            out_specs=[VMEM] + ([ANY] if final else [VMEM] * 4),
            scratch_shapes=[pltpu.SemaphoreType.DMA((4,))] * final,
            input_output_aliases={2: 0, 7: 1} if final else {2: 0},
            compiler_params=PARAMS,
            cost_estimate=pl.CostEstimate(flops=2 * 256 * 128 * 128, bytes_accessed=1 << 20, transcendentals=0),
            name=f"corner_{section}",
        )(block_level, neighbours, plane, matrices, partial, far, near, *result)
    return sends[0]


def solution(mesh):
    placed = (
        P("tx", "ty", None, None),
        P("tx", "ty", None, None),
        P("tx", "ty", None, None),
        P("tx", "ty", None, None),
        P("tx", "ty"),
        P("tx", "ty", None),
    )
    return jax.shard_map(
        local, mesh=mesh, in_specs=placed, out_specs=P("tx", "ty", None, None), check_vma=False
    )
```

```python
import functools

import jax
import jax.numpy as jnp
from jax import lax
from jax.experimental import pallas as pl
from jax.experimental.pallas import tpu as pltpu
from jax.sharding import PartitionSpec as P

LEVELS = 4
BOTH = ("tx", "ty")
SIDE = 4
GRID = 6
PLANE = GRID * GRID
BLANK = 2 * PLANE
ROWS = 256
LANES = 128
MARK = 16
EXTRA = 2 * (LANES + MARK)
CORNERS = ((0, 0), (0, 3), (3, 0), (3, 3))
VMEM = pl.BlockSpec(memory_space=pltpu.VMEM)
SMEM = pl.BlockSpec(memory_space=pltpu.SMEM)
HBM = pl.BlockSpec(memory_space=pltpu.HBM)
PARAMS = pltpu.CompilerParams(vmem_limit_bytes=20 * 1024 * 1024)


def partner(at, size, kind):
    if kind == "in":
        return at ^ 1
    if kind == "out":
        return (at + 1) % size if at % 2 else (at - 1) % size
    return at


def swap(value, along_x, along_y):
    size_x, size_y = lax.axis_size("tx"), lax.axis_size("ty")
    pairs = [
        (x * size_y + y, partner(x, size_x, along_x) * size_y + partner(y, size_y, along_y))
        for x in range(size_x)
        for y in range(size_y)
    ]
    return lax.ppermute(value, BOTH, pairs)


def exchange(sends):
    tx_out, tx_in, ty_out, ty_in = sends
    return swap(tx_out, "out", None), swap(tx_in, "in", None), swap(ty_out, None, "out"), swap(ty_in, None, "in")


def forward_corners(halo, odd_y):
    blocks = [piece[: SIDE * ROWS].reshape(SIDE, ROWS, LANES) for piece in halo[:2]]
    first = jnp.stack([piece[0] for piece in blocks]).reshape(2 * ROWS, LANES)
    last = jnp.stack([piece[3] for piece in blocks]).reshape(2 * ROWS, LANES)
    return swap(jnp.where(odd_y, last, first), None, "out"), swap(jnp.where(odd_y, first, last), None, "in")


def edges():
    odd_x = lax.rem(lax.axis_index("tx"), 2)
    odd_y = lax.rem(lax.axis_index("ty"), 2)
    return 3 * odd_x, 3 - 3 * odd_x, 3 * odd_y, 3 - 3 * odd_y


def beyond(edge):
    return (edge // 3) * 5


def own_slot(x, y):
    return PLANE + (x + 1) * GRID + y + 1


def piece(ref, at):
    return ref[at * ROWS : (at + 1) * ROWS]


def pack_kernel(earlier, tx_out, tx_in, ty_out, ty_in, sems):
    out_x, in_x, out_y, in_y = edges()
    copies = [
        pltpu.make_async_copy(earlier.at[out_x], tx_out, sems.at[0]),
        pltpu.make_async_copy(earlier.at[in_x], tx_in, sems.at[1]),
        pltpu.make_async_copy(earlier.at[:, out_y], ty_out, sems.at[2]),
        pltpu.make_async_copy(earlier.at[:, in_y], ty_in, sems.at[3]),
    ]
    for copy in copies:
        copy.start()
    for copy in copies:
        copy.wait()


def load_kernel(
    levels, codes, earlier, innovation, conditioner, chol_factor, plane, matrices, noise, late, *rest
):
    extras = rest[:4]
    shocks, factors, sems = rest[4:]
    copies = [
        pltpu.make_async_copy(innovation, shocks, sems.at[0]),
        pltpu.make_async_copy(chol_factor, factors, sems.at[1]),
        pltpu.make_async_copy(conditioner, matrices, sems.at[2]),
    ]
    copies += [
        pltpu.make_async_copy(earlier.at[x], plane.at[pl.ds((x + 1) * GRID + 1, SIDE)], sems.at[3 + x])
        for x in range(SIDE)
    ]
    for copy in copies:
        copy.start()

    def clear(at, carry):
        plane[at] = jnp.zeros(plane.shape[1:], plane.dtype)
        return carry

    lax.fori_loop(PLANE, BLANK + 1, clear, 0)
    rows = lax.broadcasted_iota(jnp.int32, factors.shape[2:], 0)
    columns = lax.broadcasted_iota(jnp.int32, factors.shape[2:], 1)
    upper = rows <= columns
    copies[0].wait()
    copies[1].wait()

    def one_cell(cell, carry):
        x, y = cell // SIDE, cell % SIDE
        factor = jnp.where(upper, factors[x, y].astype(jnp.float32), 0.0).astype(jnp.bfloat16)
        noise[cell] = jnp.dot(shocks[x, y], factor, preferred_element_type=jnp.float32)
        return carry

    lax.fori_loop(0, SIDE * SIDE, one_cell, 0)
    for copy in copies[2:]:
        copy.wait()
    out_x, in_x, out_y, in_y = edges()
    for at, (x, y) in enumerate(CORNERS):
        level = levels[x, y]
        code = 2 * x + 2 * y // 3 + jnp.where(level > 0, 9, 0)
        found = jnp.int32(-1)
        for k in range(8):
            found = jnp.where(codes[x, y, k] == code, k, found)
        late[at] = found
        mark = jnp.full((MARK, LANES), jnp.where(found >= 0, level, -1).astype(jnp.float32)).astype(jnp.bfloat16)
        start = pl.multiple_of(LANES * jnp.maximum(found, 0), LANES)
        matrix = matrices[x, y, pl.ds(start, LANES)]
        for ref, facing, place in (
            (extras[0], out_x == x, y // 3),
            (extras[1], in_x == x, y // 3),
            (extras[2], out_y == y, x // 3),
            (extras[3], in_y == y, x // 3),
        ):

            @pl.when(facing)
            def _(ref=ref, place=place, matrix=matrix, mark=mark):
                ref[place * LANES : (place + 1) * LANES] = matrix
                ref[2 * LANES + place * MARK : 2 * LANES + (place + 1) * MARK] = mark


def slot_of(code, x, y):
    old = (code >= 9).astype(jnp.int32)
    offset = code - 9 * old
    down = (offset >= 3).astype(jnp.int32) + (offset >= 6).astype(jnp.int32)
    return (x + down) * GRID + y + (offset - 3 * down) + PLANE * old


def store_halo(base, plane, halo):
    tx_out, tx_in, ty_out, ty_in = halo
    out_x, in_x, out_y, in_y = edges()
    for i in range(SIDE):
        plane[base + beyond(out_x) * GRID + i + 1] = piece(tx_out, i)
        plane[base + beyond(in_x) * GRID + i + 1] = piece(tx_in, i)
        plane[base + (i + 1) * GRID + beyond(out_y)] = piece(ty_out, i)
        plane[base + (i + 1) * GRID + beyond(in_y)] = piece(ty_in, i)


def complete_halo(recent, plane, extras):
    out_x, in_x, out_y, in_y = edges()
    source = PLANE if recent else 0

    def complete(cell, other, extra, place):
        mark = extra[2 * LANES + place * MARK : 2 * LANES + place * MARK + 1].astype(jnp.float32)
        product = jnp.dot(
            plane[source + other], extra[place * LANES : (place + 1) * LANES], preferred_element_type=jnp.float32
        )
        product *= jnp.where(mark == recent, 1.0, 0.0)
        plane[PLANE + cell] = (plane[PLANE + cell].astype(jnp.float32) + product).astype(jnp.bfloat16)

    for side_x, extra_x in ((out_x, extras[0]), (in_x, extras[1])):
        for place in (0, 1):
            complete(beyond(side_x) * GRID + 1 + 3 * place, (side_x + 1) * GRID + 5 * place, extra_x, place)
    for side_y, extra_y in ((out_y, extras[2]), (in_y, extras[3])):
        for place in (0, 1):
            complete((1 + 3 * place) * GRID + beyond(side_y), 5 * place * GRID + side_y + 1, extra_y, place)


def finish_corners(recent, levels, late, plane, matrices, partial, far, near):
    out_x, _, out_y, _ = edges()
    for at, (x, y) in enumerate(CORNERS):
        start = jnp.where(out_x == x, 0, ROWS)
        outward = out_y == y

        @pl.when((levels[x, y] == recent) & (late[at] >= 0))
        def _(at=at, x=x, y=y, start=start, outward=outward):
            rows = pl.ds(pl.multiple_of(start, ROWS), ROWS)
            block = jnp.where(outward, far[rows], near[rows])
            matrix = matrices[x, y, pl.ds(pl.multiple_of(LANES * late[at], LANES), LANES)]
            summed = partial[at] + jnp.dot(block, matrix, preferred_element_type=jnp.float32)
            plane[own_slot(x, y)] = summed.astype(jnp.bfloat16)


def store_corners(plane, far, near):
    out_x, _, out_y, _ = edges()
    for x, y in CORNERS:
        rows = pl.ds(pl.multiple_of(jnp.where(out_x == x, 0, ROWS), ROWS), ROWS)
        plane[beyond(x) * GRID + beyond(y)] = jnp.where(out_y == y, far[rows], near[rows])


def main_kernel(section, levels, codes, late, plane_in, partial_in, matrices, noise, *rest):
    halo, rest = rest[:4], rest[4:]
    extras = halo
    if section != 1:
        extras, rest = rest[:4], rest[4:]
    if section:
        extras = [ref.at[pl.ds(ref.shape[0] - EXTRA, EXTRA)] for ref in extras]
    plane, partial, *rest = rest
    base = PLANE if section else 0
    out_x, in_x, out_y, in_y = edges()
    store_halo(base, plane, halo)
    if section:
        corners = [ref.at[pl.ds(SIDE * ROWS, 2 * ROWS)] for ref in halo[2:]]
        if section == 1:
            store_corners(plane, *corners)
        complete_halo(section - 1, plane, extras)
        finish_corners(section - 1, levels, late, plane, matrices, partial, *corners)
    waiting = tuple(base + row * GRID + column for row in (0, 5) for column in (0, 5))

    def one_cell(cell, carry):
        x, y = cell // SIDE, cell % SIDE

        @pl.when(levels[x, y] == section)
        def _():
            parts = []
            for k in range(8):
                slot = slot_of(codes[x, y, k], x, y)
                for corner in waiting:
                    slot = jnp.where(slot == corner, BLANK, slot)
                parts.append(plane[slot])
            summed = noise[cell] + jnp.dot(
                jnp.concatenate(parts, axis=1), matrices[x, y], preferred_element_type=jnp.float32
            )
            plane[own_slot(x, y)] = summed.astype(jnp.bfloat16)
            at_corner = ((x == 0) | (x == 3)) & ((y == 0) | (y == 3))

            @pl.when(at_corner)
            def _():
                partial[(x // 3) * 2 + y // 3] = summed

        return carry

    lax.fori_loop(0, SIDE * SIDE, one_cell, 0)
    if section == LEVELS - 1:
        result, sems = rest
        copies = [
            pltpu.make_async_copy(plane.at[pl.ds(own_slot(x, 0), SIDE)], result.at[x], sems.at[x])
            for x in range(SIDE)
        ]
        for copy in copies:
            copy.start()
        for copy in copies:
            copy.wait()
    else:
        tx_out, tx_in, ty_out, ty_in = rest
        for i in range(SIDE):
            rows = pl.ds(i * ROWS, ROWS)
            tx_out[rows] = plane[own_slot(out_x, i)]
            tx_in[rows] = plane[own_slot(in_x, i)]
            ty_out[rows] = plane[own_slot(i, out_y)]
            ty_in[rows] = plane[own_slot(i, in_y)]
        for i, side in enumerate((out_x, in_x)):
            rows = pl.ds((SIDE + i) * ROWS, ROWS)
            ty_out[rows] = plane[base + beyond(side) * GRID + out_y + 1]
            ty_in[rows] = plane[base + beyond(side) * GRID + in_y + 1]
        if section == 0:
            for ref, extra in zip(rest, extras, strict=True):
                ref[ref.shape[0] - EXTRA :] = extra[...]


def corner_kernel(levels, late, plane_in, matrices, partial, far, near, result_in, plane, result, sems):
    finish_corners(LEVELS - 1, levels, late, plane, matrices, partial, far, near)
    copies = [
        pltpu.make_async_copy(plane.at[own_slot(x, y)], result.at[x, y], sems.at[at])
        for at, (x, y) in enumerate(CORNERS)
    ]
    for copy in copies:
        copy.start()
    for copy in copies:
        copy.wait()


def rows_of(rows):
    return jax.ShapeDtypeStruct((rows, LANES), jnp.bfloat16)


def local(earlier, innovation, conditioner, chol_factor, block_level, neighbours):
    block = earlier.shape[2:]
    odd_y = lax.rem(lax.axis_index("ty"), 2) == 1
    in_hbm = lambda value: pltpu.with_memory_space_constraint(value, pltpu.HBM)
    plane_shape = jax.ShapeDtypeStruct((BLANK + 1, *block), jnp.bfloat16)
    whole = jax.ShapeDtypeStruct(earlier.shape, jnp.bfloat16)
    partial_shape = jax.ShapeDtypeStruct((len(CORNERS), *block), jnp.float32)
    late_shape = jax.ShapeDtypeStruct((len(CORNERS),), jnp.int32)
    sends = pl.pallas_call(
        pack_kernel,
        out_shape=[jax.ShapeDtypeStruct((SIDE, *block), jnp.bfloat16)] * 4,
        in_specs=[HBM],
        out_specs=[VMEM] * 4,
        scratch_shapes=[pltpu.SemaphoreType.DMA((4,))],
        compiler_params=PARAMS,
        name="pack",
    )(in_hbm(earlier))
    sends = [send.reshape(SIDE * ROWS, LANES) for send in sends]
    plane, matrices, noise, late, *extras = pl.pallas_call(
        load_kernel,
        out_shape=[
            plane_shape,
            jax.ShapeDtypeStruct(conditioner.shape, jnp.bfloat16),
            jax.ShapeDtypeStruct((SIDE * SIDE, *block), jnp.float32),
            late_shape,
        ]
        + [rows_of(EXTRA)] * 4,
        in_specs=[SMEM] * 2 + [HBM] * 4,
        out_specs=[VMEM] * 3 + [SMEM] + [VMEM] * 4,
        scratch_shapes=[
            pltpu.VMEM(innovation.shape, jnp.bfloat16),
            pltpu.VMEM(chol_factor.shape, jnp.bfloat16),
            pltpu.SemaphoreType.DMA((7,)),
        ],
        compiler_params=PARAMS,
        cost_estimate=pl.CostEstimate(flops=2 * 16 * 256 * 128 * 128, bytes_accessed=14 << 20, transcendentals=0),
        name="load",
    )(block_level, neighbours, in_hbm(earlier), in_hbm(innovation), in_hbm(conditioner), in_hbm(chol_factor))
    partial = jnp.zeros(partial_shape.shape, partial_shape.dtype)
    for section in range(LEVELS):
        final = section == LEVELS - 1
        halo = exchange(sends)
        if section == 1:
            extras = halo
        if final:
            far, near = forward_corners(halo, odd_y)
        tail = EXTRA if section == 0 else 0
        send_rows = [SIDE * ROWS + tail] * 2 + [(SIDE + 2) * ROWS + tail] * 2
        plane, partial, *sends = pl.pallas_call(
            functools.partial(main_kernel, section),
            out_shape=[plane_shape, partial_shape] + ([whole] if final else [rows_of(rows) for rows in send_rows]),
            in_specs=[SMEM] * 3 + [VMEM] * (8 if section == 1 else 12),
            out_specs=[VMEM] * 2 + ([HBM] if final else [VMEM] * 4),
            scratch_shapes=[pltpu.SemaphoreType.DMA((4,))] * final,
            input_output_aliases={3: 0, 4: 1},
            compiler_params=PARAMS,
            cost_estimate=pl.CostEstimate(flops=8 * 2 * 256 * 1024 * 128, bytes_accessed=4 << 20, transcendentals=0),
            name=f"main_{section}",
        )(block_level, neighbours, late, plane, partial, matrices, noise, *halo, *([] if section == 1 else extras))
    _, result = pl.pallas_call(
        corner_kernel,
        out_shape=[plane_shape, whole],
        in_specs=[SMEM] * 2 + [VMEM] * 5 + [HBM],
        out_specs=[VMEM, HBM],
        scratch_shapes=[pltpu.SemaphoreType.DMA((4,))],
        input_output_aliases={2: 0, 7: 1},
        compiler_params=PARAMS,
        cost_estimate=pl.CostEstimate(flops=2 * 256 * 128 * 128, bytes_accessed=1 << 20, transcendentals=0),
        name="last_corners",
    )(block_level, late, plane, matrices, partial, far, near, sends[0])
    return result


def solution(mesh):
    placed = (
        P("tx", "ty", None, None),
        P("tx", "ty", None, None),
        P("tx", "ty", None, None),
        P("tx", "ty", None, None),
        P("tx", "ty"),
        P("tx", "ty", None),
    )
    return jax.shard_map(
        local, mesh=mesh, in_specs=placed, out_specs=P("tx", "ty", None, None), check_vma=False
    )
```

```python
import functools

import jax
import jax.numpy as jnp
from jax import lax
from jax.experimental import pallas as pl
from jax.experimental.pallas import tpu as pltpu
from jax.sharding import PartitionSpec as P

LEVELS = 4
BOTH = ("tx", "ty")
SIDE = 4
GRID = 6
PLANE = GRID * GRID
BLANK = 2 * PLANE
ROWS = 256
LANES = 128
MARK = 16
EXTRA = 2 * (LANES + MARK)
DEPTH = 9 * LANES
ALL, SETTLED, ORDER, FIRST, LATE, TABLE = 0, 128, 256, 280, 288, 296
ITEMS = 66
CORNERS = ((0, 0), (0, 3), (3, 0), (3, 3))
VMEM = pl.BlockSpec(memory_space=pltpu.VMEM)
SMEM = pl.BlockSpec(memory_space=pltpu.SMEM)
HBM = pl.BlockSpec(memory_space=pltpu.HBM)
PARAMS = pltpu.CompilerParams(vmem_limit_bytes=8 * 1024 * 1024)


def partner(at, size, kind):
    if kind == "in":
        return at ^ 1
    if kind == "out":
        return (at + 1) % size if at % 2 else (at - 1) % size
    return at


def swap(value, along_x, along_y):
    size_x, size_y = lax.axis_size("tx"), lax.axis_size("ty")
    pairs = [
        (x * size_y + y, partner(x, size_x, along_x) * size_y + partner(y, size_y, along_y))
        for x in range(size_x)
        for y in range(size_y)
    ]
    return lax.ppermute(value, BOTH, pairs)


def exchange(sends):
    tx_out, tx_in, ty_out, ty_in = sends
    return swap(tx_out, "out", None), swap(tx_in, "in", None), swap(ty_out, None, "out"), swap(ty_in, None, "in")


def edges():
    odd_x = lax.rem(lax.axis_index("tx"), 2)
    odd_y = lax.rem(lax.axis_index("ty"), 2)
    return 3 * odd_x, 3 - 3 * odd_x, 3 * odd_y, 3 - 3 * odd_y


def beyond(edge):
    return (edge // 3) * 5


def own_slot(x, y):
    return PLANE + (x + 1) * GRID + y + 1


def piece(ref, at):
    return ref[at * ROWS : (at + 1) * ROWS]


def forward_kernel(tx_out, tx_in, far, near):
    _, _, out_y, in_y = edges()
    for i, ref in enumerate((tx_out, tx_in)):
        far[i * ROWS : (i + 1) * ROWS] = ref[pl.ds(pl.multiple_of(out_y * ROWS, ROWS), ROWS)]
        near[i * ROWS : (i + 1) * ROWS] = ref[pl.ds(pl.multiple_of(in_y * ROWS, ROWS), ROWS)]


def pack_kernel(earlier, tx_out, tx_in, ty_out, ty_in, sems):
    out_x, in_x, out_y, in_y = edges()
    copies = [
        pltpu.make_async_copy(earlier.at[out_x], tx_out, sems.at[0]),
        pltpu.make_async_copy(earlier.at[in_x], tx_in, sems.at[1]),
        pltpu.make_async_copy(earlier.at[:, out_y], ty_out, sems.at[2]),
        pltpu.make_async_copy(earlier.at[:, in_y], ty_in, sems.at[3]),
    ]
    for copy in copies:
        copy.start()
    for copy in copies:
        copy.wait()


def fill_table(levels, codes, table):
    def one_cell(cell, carry):
        x, y = cell // SIDE, cell % SIDE
        level = levels[x, y]
        for k in range(8):
            code = codes[x, y, k]
            old = code >= 9
            offset = jnp.where(old, code - 9, code)
            down = (offset >= 3).astype(jnp.int32) + (offset >= 6).astype(jnp.int32)
            row, column = x + down, y + offset - 3 * down
            slot = row * GRID + column + jnp.where(old, PLANE, 0)
            edge_row, edge_column = (row == 0) | (row == 5), (column == 0) | (column == 5)
            outer = edge_row & edge_column
            own_corner = ((row == 1) | (row == 4)) & ((column == 1) | (column == 4))
            waits = outer & (old == (level > 0))
            open_ = (old & (edge_row | edge_column | own_corner)) | outer
            table[ALL + 8 * cell + k] = jnp.where(waits, BLANK, slot)
            table[SETTLED + 8 * cell + k] = jnp.where(open_, BLANK, slot)
        return carry

    lax.fori_loop(0, SIDE * SIDE, one_cell, 0)
    at = jnp.int32(0)
    for level in range(LEVELS):
        table[FIRST + level] = at

        def one_place(cell, at, level=level):
            table[ORDER + at] = cell
            return at + (levels[cell // SIDE, cell % SIDE] == level).astype(jnp.int32)

        at = lax.fori_loop(0, SIDE * SIDE, one_place, at)
    table[FIRST + LEVELS] = at
    for at, (x, y) in enumerate(CORNERS):
        code = 2 * x + 2 * y // 3 + jnp.where(levels[x, y] > 0, 9, 0)
        found = jnp.int32(-1)
        for k in range(8):
            found = jnp.where(codes[x, y, k] == code, k, found)
        table[LATE + at] = found


def load_kernel(levels, codes, earlier, innovation, conditioner, chol_factor, plane, matrices, noise, sums, table, *rest):
    extras = rest[:4]
    factors, sems = rest[4:]
    copies = [
        pltpu.make_async_copy(chol_factor, factors, sems.at[0]),
        pltpu.make_async_copy(conditioner, matrices.at[:, pl.ds(0, 8 * LANES)], sems.at[1]),
        pltpu.make_async_copy(innovation, noise, sems.at[2]),
    ]
    copies += [
        pltpu.make_async_copy(
            earlier.at[pl.ds(x * SIDE, SIDE)], plane.at[pl.ds((x + 1) * GRID + 1, SIDE)], sems.at[3 + x]
        )
        for x in range(SIDE)
    ]
    for copy in copies:
        copy.start()

    def clear(at, carry):
        plane[at] = jnp.zeros(plane.shape[1:], plane.dtype)
        return carry

    lax.fori_loop(PLANE, BLANK + 1, clear, 0)
    fill_table(levels, codes, table)
    rows = lax.broadcasted_iota(jnp.int32, (LANES, LANES), 0)
    columns = lax.broadcasted_iota(jnp.int32, (LANES, LANES), 1)
    upper = rows <= columns
    copies[0].wait()

    def one_cell(cell, carry):
        factor = jnp.where(upper, factors[cell].astype(jnp.float32), 0.0)
        matrices[cell, 8 * LANES :] = factor.astype(jnp.bfloat16)
        return carry

    lax.fori_loop(0, SIDE * SIDE, one_cell, 0)
    for copy in copies[1:]:
        copy.wait()
    out_x, in_x, out_y, in_y = edges()
    for at, (x, y) in enumerate(CORNERS):
        found = table[LATE + at]
        mark = jnp.full((MARK, LANES), jnp.where(found >= 0, levels[x, y], -1).astype(jnp.float32)).astype(jnp.bfloat16)
        start = pl.multiple_of(LANES * jnp.maximum(found, 0), LANES)
        matrix = matrices[SIDE * x + y, pl.ds(start, LANES)]
        for ref, facing, place in (
            (extras[0], out_x == x, y // 3),
            (extras[1], in_x == x, y // 3),
            (extras[2], out_y == y, x // 3),
            (extras[3], in_y == y, x // 3),
        ):

            @pl.when(facing)
            def _(ref=ref, place=place, matrix=matrix, mark=mark):
                ref[place * LANES : (place + 1) * LANES] = matrix
                ref[2 * LANES + place * MARK : 2 * LANES + (place + 1) * MARK] = mark


def complete_halo(recent, plane, extras):
    out_x, in_x, out_y, in_y = edges()
    source = PLANE if recent else 0
    todo = []
    for side_x, extra_x in ((out_x, extras[0]), (in_x, extras[1])):
        for place in (0, 1):
            todo.append((beyond(side_x) * GRID + 1 + 3 * place, (side_x + 1) * GRID + 5 * place, extra_x, place))
    for side_y, extra_y in ((out_y, extras[2]), (in_y, extras[3])):
        for place in (0, 1):
            todo.append(((1 + 3 * place) * GRID + beyond(side_y), 5 * place * GRID + side_y + 1, extra_y, place))
    marks = [
        jnp.max(extra[2 * LANES + place * MARK : 2 * LANES + (place + 1) * MARK].astype(jnp.float32))
        for _, _, extra, place in todo
    ]
    for (cell, other, extra, place), mark in zip(todo, marks, strict=True):

        @pl.when(mark == recent)
        def _(cell=cell, other=other, extra=extra, place=place):
            product = jnp.dot(
                plane[source + other], extra[place * LANES : (place + 1) * LANES], preferred_element_type=jnp.float32
            )
            plane[PLANE + cell] = (plane[PLANE + cell].astype(jnp.float32) + product).astype(jnp.bfloat16)


def finish_corners(recent, table, plane, matrices, sums, levels, far, near):
    out_x, _, out_y, _ = edges()
    for at, (x, y) in enumerate(CORNERS):
        cell = SIDE * x + y

        @pl.when((levels[x, y] == recent) & (table[LATE + at] >= 0))
        def _(at=at, x=x, y=y, cell=cell):
            rows = pl.ds(pl.multiple_of(jnp.where(out_x == x, 0, ROWS), ROWS), ROWS)
            block = jnp.where(out_y == y, far[rows], near[rows])
            matrix = matrices[cell, pl.ds(pl.multiple_of(LANES * table[LATE + at], LANES), LANES)]
            summed = sums[cell] + jnp.dot(block, matrix, preferred_element_type=jnp.float32)
            plane[own_slot(x, y)] = summed.astype(jnp.bfloat16)


def store_corners(plane, far, near):
    out_x, _, out_y, _ = edges()
    for x, y in CORNERS:
        rows = pl.ds(pl.multiple_of(jnp.where(out_x == x, 0, ROWS), ROWS), ROWS)
        plane[beyond(x) * GRID + beyond(y)] = jnp.where(out_y == y, far[rows], near[rows])


def gather_product(which, cell, table, plane, matrices, noise):
    parts = [plane[table[which + 8 * cell + k]] for k in range(8)] + [noise[cell]]
    return jnp.dot(jnp.concatenate(parts, axis=1), matrices[cell], preferred_element_type=jnp.float32)


def settled_kernel(section, table, plane_in, sums_in, matrices, noise, plane, sums, items):
    def one_cell(at, count):
        cell = table[ORDER + at]
        sums[cell] = gather_product(SETTLED, cell, table, plane, matrices, noise)
        for k in range(8):
            items[1 + count] = 8 * cell + k
            count += (table[ALL + 8 * cell + k] != table[SETTLED + 8 * cell + k]).astype(jnp.int32)
        return count

    items[0] = lax.fori_loop(table[FIRST + section], table[FIRST + section + 1], one_cell, jnp.int32(0))


def store_rows(base, plane, tx_out, tx_in):
    out_x, in_x, _, _ = edges()
    for i in range(SIDE):
        plane[base + beyond(out_x) * GRID + i + 1] = piece(tx_out, i)
        plane[base + beyond(in_x) * GRID + i + 1] = piece(tx_in, i)


def rows_kernel(plane_in, tx_out, tx_in, plane):
    store_rows(PLANE, plane, tx_out, tx_in)


def store_columns(base, plane, ty_out, ty_in):
    _, _, out_y, in_y = edges()
    for i in range(SIDE):
        plane[base + (i + 1) * GRID + beyond(out_y)] = piece(ty_out, i)
        plane[base + (i + 1) * GRID + beyond(in_y)] = piece(ty_in, i)


def pack_sends(base, plane, sends):
    tx_out, tx_in, ty_out, ty_in = sends
    out_x, in_x, out_y, in_y = edges()
    for i in range(SIDE):
        rows = pl.ds(i * ROWS, ROWS)
        tx_out[rows] = plane[own_slot(out_x, i)]
        tx_in[rows] = plane[own_slot(in_x, i)]
        ty_out[rows] = plane[own_slot(i, out_y)]
        ty_in[rows] = plane[own_slot(i, in_y)]
    for i, side in enumerate((out_x, in_x)):
        rows = pl.ds((SIDE + i) * ROWS, ROWS)
        ty_out[rows] = plane[base + beyond(side) * GRID + out_y + 1]
        ty_in[rows] = plane[base + beyond(side) * GRID + in_y + 1]


def first_kernel(table, plane_in, sums_in, matrices, noise, *rest):
    halo, extras, (plane, sums, *sends) = rest[:4], rest[4:8], rest[8:]
    store_rows(0, plane, *halo[:2])
    store_columns(0, plane, *halo[2:])

    def one_cell(at, carry):
        cell = table[ORDER + at]
        summed = gather_product(ALL, cell, table, plane, matrices, noise)
        sums[cell] = summed
        plane[own_slot(cell // SIDE, cell % SIDE)] = summed.astype(jnp.bfloat16)
        return carry

    lax.fori_loop(table[FIRST], table[FIRST + 1], one_cell, 0)
    pack_sends(0, plane, sends)
    for ref, extra in zip(sends, extras, strict=True):
        ref[ref.shape[0] - EXTRA :] = extra[...]


def main_kernel(section, levels, table, items, plane_in, sums_in, matrices, ty_out, ty_in, *rest):
    extras, (plane, sums, *rest) = rest[:4], rest[4:]
    extras = [ref.at[pl.ds(ref.shape[0] - EXTRA, EXTRA)] for ref in extras]
    corners = [ref.at[pl.ds(SIDE * ROWS, 2 * ROWS)] for ref in (ty_out, ty_in)]
    store_columns(PLANE, plane, ty_out, ty_in)
    if section == 1:
        store_corners(plane, *corners)
    complete_halo(section - 1, plane, extras)
    finish_corners(section - 1, table, plane, matrices, sums, levels, *corners)

    def one_item(at, carry):
        item = items[1 + at]
        cell, k = item // 8, item % 8
        matrix = matrices[cell, pl.ds(pl.multiple_of(k * LANES, LANES), LANES)]
        sums[cell] += jnp.dot(plane[table[ALL + item]], matrix, preferred_element_type=jnp.float32)
        return carry

    lax.fori_loop(0, items[0], one_item, 0)

    def one_cell(at, carry):
        cell = table[ORDER + at]
        plane[own_slot(cell // SIDE, cell % SIDE)] = sums[cell].astype(jnp.bfloat16)
        return carry

    lax.fori_loop(table[FIRST + section], table[FIRST + section + 1], one_cell, 0)
    if section < LEVELS - 1:
        pack_sends(PLANE, plane, rest)
    else:
        result, sems = rest
        copies = [
            pltpu.make_async_copy(
                plane.at[pl.ds(own_slot(x, 0), SIDE)], result.at[pl.ds(x * SIDE, SIDE)], sems.at[x]
            )
            for x in range(SIDE)
        ]
        for copy in copies:
            copy.start()
        for copy in copies:
            copy.wait()


def corner_kernel(levels, table, plane_in, matrices, sums, far, near, result_in, plane, result, sems):
    finish_corners(LEVELS - 1, table, plane, matrices, sums, levels, far, near)
    copies = [
        pltpu.make_async_copy(plane.at[own_slot(x, y)], result.at[SIDE * x + y], sems.at[at])
        for at, (x, y) in enumerate(CORNERS)
    ]
    for copy in copies:
        copy.start()
    for copy in copies:
        copy.wait()


def cost(products, depth):
    flops = products * 2 * ROWS * depth * LANES
    return pl.CostEstimate(flops=flops, bytes_accessed=4 << 20, transcendentals=0)


def rows_of(rows):
    return jax.ShapeDtypeStruct((rows, LANES), jnp.bfloat16)


def local(earlier, innovation, conditioner, chol_factor, block_level, neighbours):
    block = earlier.shape[2:]
    tile = SIDE * SIDE
    in_hbm = lambda value: pltpu.with_memory_space_constraint(
        value.reshape(tile, *value.shape[2:]), pltpu.HBM
    )
    edge = jax.ShapeDtypeStruct((SIDE, *block), jnp.bfloat16)
    plane_shape = jax.ShapeDtypeStruct((BLANK + 1, *block), jnp.bfloat16)
    sums_shape = jax.ShapeDtypeStruct((tile, *block), jnp.float32)
    whole = jax.ShapeDtypeStruct((tile, *block), jnp.bfloat16)
    sends = pl.pallas_call(
        pack_kernel,
        out_shape=[edge] * 4,
        in_specs=[HBM],
        out_specs=[VMEM] * 4,
        scratch_shapes=[pltpu.SemaphoreType.DMA((4,))],
        compiler_params=PARAMS,
        name="pack",
    )(pltpu.with_memory_space_constraint(earlier, pltpu.HBM))
    sends = [send.reshape(SIDE * ROWS, LANES) for send in sends]
    plane, matrices, noise, sums, table, *extras = pl.pallas_call(
        load_kernel,
        out_shape=[
            plane_shape,
            jax.ShapeDtypeStruct((tile, DEPTH, LANES), jnp.bfloat16),
            whole,
            sums_shape,
            jax.ShapeDtypeStruct((TABLE,), jnp.int32),
        ]
        + [rows_of(EXTRA)] * 4,
        in_specs=[SMEM] * 2 + [HBM] * 4,
        out_specs=[VMEM] * 4 + [SMEM] + [VMEM] * 4,
        scratch_shapes=[pltpu.VMEM((tile, *chol_factor.shape[2:]), jnp.bfloat16), pltpu.SemaphoreType.DMA((7,))],
        compiler_params=PARAMS,
        cost_estimate=pl.CostEstimate(flops=0, bytes_accessed=14 << 20, transcendentals=0),
        name="load",
    )(block_level, neighbours, in_hbm(earlier), in_hbm(innovation), in_hbm(conditioner), in_hbm(chol_factor))
    halo = exchange(sends)
    plane, sums, *sends = pl.pallas_call(
        first_kernel,
        out_shape=[plane_shape, sums_shape]
        + [rows_of(SIDE * ROWS + EXTRA)] * 2
        + [rows_of((SIDE + 2) * ROWS + EXTRA)] * 2,
        in_specs=[SMEM] + [VMEM] * 12,
        out_specs=[VMEM] * 6,
        input_output_aliases={1: 0, 2: 1},
        compiler_params=PARAMS,
        cost_estimate=cost(8, DEPTH),
        name="level_0",
    )(table, plane, sums, matrices, noise, *halo, *extras)
    for section in range(1, LEVELS):
        final = section == LEVELS - 1
        halo = exchange(sends)
        if section == 1:
            extras = halo
        plane, sums, items = pl.pallas_call(
            functools.partial(settled_kernel, section),
            out_shape=[plane_shape, sums_shape, jax.ShapeDtypeStruct((ITEMS,), jnp.int32)],
            in_specs=[SMEM] + [VMEM] * 4,
            out_specs=[VMEM] * 2 + [SMEM],
            input_output_aliases={1: 0, 2: 1},
            compiler_params=PARAMS,
            cost_estimate=cost(8, DEPTH),
            name=f"settled_{section}",
        )(table, plane, sums, matrices, noise)
        if final:
            far, near = pl.pallas_call(
                forward_kernel,
                out_shape=[rows_of(2 * ROWS)] * 2,
                in_specs=[VMEM] * 2,
                out_specs=[VMEM] * 2,
                compiler_params=PARAMS,
                cost_estimate=cost(0, 0),
                name="forward",
            )(*halo[:2])
            far, near = swap(far, None, "out"), swap(near, None, "in")
        plane = pl.pallas_call(
            rows_kernel,
            out_shape=plane_shape,
            in_specs=[VMEM] * 3,
            out_specs=VMEM,
            input_output_aliases={0: 0},
            compiler_params=PARAMS,
            cost_estimate=cost(2, LANES),
            name=f"rows_{section}",
        )(plane, *halo[:2])
        plane, sums, *sends = pl.pallas_call(
            functools.partial(main_kernel, section),
            out_shape=[plane_shape, sums_shape]
            + ([whole] if final else [rows_of(SIDE * ROWS)] * 2 + [rows_of((SIDE + 2) * ROWS)] * 2),
            in_specs=[SMEM] * 3 + [VMEM] * 9,
            out_specs=[VMEM] * 2 + ([HBM] if final else [VMEM] * 4),
            scratch_shapes=[pltpu.SemaphoreType.DMA((4,))] * final,
            input_output_aliases={3: 0, 4: 1},
            compiler_params=PARAMS,
            cost_estimate=cost(16, LANES),
            name=f"level_{section}",
        )(block_level, table, items, plane, sums, matrices, *halo[2:], *extras)
    _, result = pl.pallas_call(
        corner_kernel,
        out_shape=[plane_shape, whole],
        in_specs=[SMEM] * 2 + [VMEM] * 5 + [HBM],
        out_specs=[VMEM, HBM],
        scratch_shapes=[pltpu.SemaphoreType.DMA((4,))],
        input_output_aliases={2: 0, 7: 1},
        compiler_params=PARAMS,
        cost_estimate=cost(4, LANES),
        name="last_corners",
    )(block_level, table, plane, matrices, sums, far, near, sends[0])
    return result.reshape(earlier.shape)


def solution(mesh):
    placed = (
        P("tx", "ty", None, None),
        P("tx", "ty", None, None),
        P("tx", "ty", None, None),
        P("tx", "ty", None, None),
        P("tx", "ty"),
        P("tx", "ty", None),
    )
    return jax.shard_map(
        local, mesh=mesh, in_specs=placed, out_specs=P("tx", "ty", None, None), check_vma=False
    )
```

```python
import functools

import jax
import jax.numpy as jnp
from jax import lax
from jax.experimental import pallas as pl
from jax.experimental.pallas import tpu as pltpu
from jax.sharding import PartitionSpec as P

LEVELS = 4
BOTH = ("tx", "ty")
SIDE = 4
GRID = 6
PLANE = GRID * GRID
BLANK = 2 * PLANE
ROWS = 256
LANES = 128
MARK = 16
EXTRA = 2 * (LANES + MARK)
DEPTH = 9 * LANES
LEVEL, LATE, SLOT, ITEM, MARKS, COUNT, TABLE = 0, 16, 20, 148, 220, 228, 229
GROUP = 4
CORNERS = ((0, 0), (0, 3), (3, 0), (3, 3))
VMEM = pl.BlockSpec(memory_space=pltpu.VMEM)
SMEM = pl.BlockSpec(memory_space=pltpu.SMEM)
HBM = pl.BlockSpec(memory_space=pltpu.HBM)
PARAMS = pltpu.CompilerParams(vmem_limit_bytes=8 * 1024 * 1024)


def partner(at, size, kind):
    if kind == "in":
        return at ^ 1
    if kind == "out":
        return (at + 1) % size if at % 2 else (at - 1) % size
    return at


def swap(value, along_x, along_y):
    size_x, size_y = lax.axis_size("tx"), lax.axis_size("ty")
    pairs = [
        (x * size_y + y, partner(x, size_x, along_x) * size_y + partner(y, size_y, along_y))
        for x in range(size_x)
        for y in range(size_y)
    ]
    return lax.ppermute(value, BOTH, pairs)


def exchange(sends):
    tx_out, tx_in, *ty_out, ty_in = sends
    halo = [swap(tx_out, "out", None), swap(tx_in, "in", None)]
    return halo + [swap(part, None, "out") for part in ty_out] + [swap(ty_in, None, "in")]


def edges():
    odd_x = lax.rem(lax.axis_index("tx"), 2)
    odd_y = lax.rem(lax.axis_index("ty"), 2)
    return 3 * odd_x, 3 - 3 * odd_x, 3 * odd_y, 3 - 3 * odd_y


def beyond(edge):
    return (edge // 3) * 5


def own_slot(x, y):
    return PLANE + (x + 1) * GRID + y + 1


def piece(ref, at):
    return ref[at * ROWS : (at + 1) * ROWS]


def forward_kernel(plane, far, near):
    out_x, in_x, out_y, in_y = edges()
    for i, side in enumerate((out_x, in_x)):
        far[i * ROWS : (i + 1) * ROWS] = plane[PLANE + beyond(side) * GRID + out_y + 1]
        near[i * ROWS : (i + 1) * ROWS] = plane[PLANE + beyond(side) * GRID + in_y + 1]


def pack_kernel(earlier, tx_out, tx_in, ty_out, ty_in, sems):
    out_x, in_x, out_y, in_y = edges()
    copies = [
        pltpu.make_async_copy(earlier.at[out_x], tx_out, sems.at[0]),
        pltpu.make_async_copy(earlier.at[in_x], tx_in, sems.at[1]),
        pltpu.make_async_copy(earlier.at[:, out_y], ty_out, sems.at[2]),
        pltpu.make_async_copy(earlier.at[:, in_y], ty_in, sems.at[3]),
    ]
    for copy in copies:
        copy.start()
    for copy in copies:
        copy.wait()


def late_code(levels, codes, x, y):
    code = 2 * x + 2 * y // 3 + jnp.where(levels[x, y] > 0, 9, 0)
    found = jnp.int32(-1)
    for k in range(8):
        found = jnp.where(codes[x, y, k] == code, k, found)
    return found


def fill_slots(cell, level, codes, every, settled):
    x, y = cell // SIDE, cell % SIDE
    for k in range(8):
        code = codes[x, y, k]
        old = code >= 9
        offset = jnp.where(old, code - 9, code)
        down = (offset >= 3).astype(jnp.int32) + (offset >= 6).astype(jnp.int32)
        row, column = x + down, y + offset - 3 * down
        slot = row * GRID + column + jnp.where(old, PLANE, 0)
        edge_row, edge_column = (row == 0) | (row == 5), (column == 0) | (column == 5)
        outer = edge_row & edge_column
        waits = outer & (old == (level > 0))
        every[SLOT + 8 * cell + k] = jnp.where(waits, BLANK, slot)
        if settled is not None:
            own_corner = ((row == 1) | (row == 4)) & ((column == 1) | (column == 4))
            open_ = (old & (edge_row | edge_column | own_corner)) | outer
            settled[8 * cell + k] = jnp.where(open_, BLANK, slot)


def cells_of(section, table, body):
    def one_cell(cell, carry):
        @pl.when(table[LEVEL + cell] == section)
        def _():
            body(cell)

        return carry

    lax.fori_loop(0, SIDE * SIDE, one_cell, 0)


def cell_copies(cell, sources, targets, sems):
    innovation, conditioner, chol_factor = sources
    noise, matrices, factors = targets
    return (
        pltpu.make_async_copy(chol_factor.at[cell], factors.at[cell], sems.at[0, cell]),
        pltpu.make_async_copy(innovation.at[cell], noise.at[cell], sems.at[1, cell]),
        pltpu.make_async_copy(conditioner.at[cell], matrices.at[cell, pl.ds(0, 8 * LANES)], sems.at[2, cell]),
    )


def start_cell(cell, sources, targets, sems):
    for copy in cell_copies(cell, sources, targets, sems):
        copy.start()


def finish_cell(cell, sources, targets, sems):
    _, matrices, factors = targets
    copies = cell_copies(cell, sources, targets, sems)
    copies[0].wait()
    rows = lax.broadcasted_iota(jnp.int32, (LANES, LANES), 0)
    columns = lax.broadcasted_iota(jnp.int32, (LANES, LANES), 1)
    upper = jnp.where(rows <= columns, factors[cell].astype(jnp.float32), 0.0)
    matrices[cell, 8 * LANES :] = upper.astype(jnp.bfloat16)
    copies[1].wait()
    copies[2].wait()


def load_kernel(
    block_level, neighbours, earlier, innovation, conditioner, chol_factor, plane, matrices, noise, sums, table, codes, extras, *rest
):
    levels, factors, sems, more_sems = rest
    scalars = [
        pltpu.make_async_copy(block_level, levels, more_sems.at[12]),
        pltpu.make_async_copy(neighbours, codes, more_sems.at[13]),
    ]
    copies = [
        pltpu.make_async_copy(
            earlier.at[pl.ds(x * SIDE, SIDE)], plane.at[pl.ds((x + 1) * GRID + 1, SIDE)], more_sems.at[x]
        )
        for x in range(SIDE)
    ]
    for copy in scalars + copies:
        copy.start()

    def clear(at, carry):
        plane[at] = jnp.zeros(plane.shape[1:], plane.dtype)
        return carry

    lax.fori_loop(PLANE, BLANK + 1, clear, 0)
    for copy in scalars:
        copy.wait()
    for cell in range(SIDE * SIDE):
        table[LEVEL + cell] = levels[cell // SIDE, cell % SIDE]
    sources, targets = (innovation, conditioner, chol_factor), (noise, matrices, factors)
    cells_of(0, table, lambda cell: start_cell(cell, sources, targets, sems))
    out_x, _, out_y, _ = edges()
    for at, (x, y) in enumerate(CORNERS):
        late = late_code(levels, codes, x, y)
        table[LATE + at] = late
        mark = jnp.full((MARK, LANES), jnp.where(late >= 0, levels[x, y], -1).astype(jnp.float32)).astype(jnp.bfloat16)
        start = pl.multiple_of(LANES * jnp.maximum(late, 0), LANES)
        matrix = conditioner.at[SIDE * x + y, pl.ds(start, LANES)]
        for way, (side, place) in enumerate(((jnp.where(out_x == x, 0, 1), y // 3), (jnp.where(out_y == y, 2, 3), x // 3))):
            copy = pltpu.make_async_copy(
                matrix, extras.at[side, pl.ds(place * LANES, LANES)], more_sems.at[4 + 2 * at + way]
            )
            copy.start()
            copies.append(copy)
            extras[side, 2 * LANES + place * MARK : 2 * LANES + (place + 1) * MARK] = mark
    cells_of(0, table, lambda cell: fill_slots(cell, 0, codes, table, None))
    cells_of(0, table, lambda cell: finish_cell(cell, sources, targets, sems))
    for copy in copies:
        copy.wait()


def read_marks(extras):
    return [
        jnp.max(extra[2 * LANES + place * MARK : 2 * LANES + (place + 1) * MARK].astype(jnp.float32)).astype(jnp.int32)
        for extra in extras
        for place in (0, 1)
    ]


def complete_halo(recent, plane, extras, marks):
    out_x, in_x, out_y, in_y = edges()
    source = PLANE if recent else 0
    todo = []
    for side in (out_x, in_x):
        for place in (0, 1):
            todo.append((beyond(side) * GRID + 1 + 3 * place, (side + 1) * GRID + 5 * place))
    for side in (out_y, in_y):
        for place in (0, 1):
            todo.append(((1 + 3 * place) * GRID + beyond(side), 5 * place * GRID + side + 1))
    for at, (cell, other) in enumerate(todo):

        @pl.when(marks[at] == recent)
        def _(cell=cell, other=other, extra=extras[at // 2], place=at % 2):
            product = jnp.dot(
                plane[source + other], extra[place * LANES : (place + 1) * LANES], preferred_element_type=jnp.float32
            )
            plane[PLANE + cell] = (plane[PLANE + cell].astype(jnp.float32) + product).astype(jnp.bfloat16)


def finish_corners(recent, table, plane, matrices, sums, far, near):
    out_x, _, out_y, _ = edges()
    for at, (x, y) in enumerate(CORNERS):
        cell = SIDE * x + y

        @pl.when((table[LEVEL + cell] == recent) & (table[LATE + at] >= 0))
        def _(at=at, x=x, y=y, cell=cell):
            side = jnp.where(out_x == x, 0, 1)
            block = jnp.where(out_y == y, far(side), near(side))
            matrix = matrices[cell, pl.ds(pl.multiple_of(LANES * table[LATE + at], LANES), LANES)]
            summed = sums[cell] + jnp.dot(block, matrix, preferred_element_type=jnp.float32)
            plane[own_slot(x, y)] = summed.astype(jnp.bfloat16)


def block_of(ref, first):
    return lambda at: ref[pl.ds(pl.multiple_of((first + at) * ROWS, ROWS), ROWS)]


def store_corners(plane, far, near):
    out_x, _, out_y, _ = edges()
    for x, y in CORNERS:
        side = jnp.where(out_x == x, 0, 1)
        plane[beyond(x) * GRID + beyond(y)] = jnp.where(out_y == y, far(side), near(side))


def gather_product(cell, slots, first, plane, matrices, noise):
    parts = [plane[slots[first + 8 * cell + k]] for k in range(8)] + [noise[cell]]
    return jnp.dot(jnp.concatenate(parts, axis=1), matrices[cell], preferred_element_type=jnp.float32)


def settled_kernel(section, codes, table_in, plane_in, sums_in, matrices_in, noise_in, *rest):
    sources, rest = rest[:3], rest[3:]
    extras = rest[:-8]
    plane, sums, matrices, noise, table, settled, factors, sems = rest[-8:]
    targets = noise, matrices, factors
    cells_of(section, table_in, lambda cell: start_cell(cell, sources, targets, sems))
    for at in range(SLOT):
        table[at] = table_in[at]
    marks = read_marks([ref.at[pl.ds(ref.shape[0] - EXTRA, EXTRA)] for ref in extras])
    for at, mark in enumerate(marks):
        table[MARKS + at] = mark

    def one_cell(cell, count):
        def collect():
            fill_slots(cell, section, codes, table, settled)
            found = count
            for k in range(8):
                table[ITEM + found] = 8 * cell + k
                found += (table[SLOT + 8 * cell + k] != settled[8 * cell + k]).astype(jnp.int32)
            return found

        return lax.cond(table_in[LEVEL + cell] == section, collect, lambda: count)

    count = lax.fori_loop(0, SIDE * SIDE, one_cell, jnp.int32(0))
    table[COUNT] = count

    def product(cell):
        finish_cell(cell, sources, targets, sems)
        sums[cell] = gather_product(cell, settled, 0, plane, matrices, noise)

    cells_of(section, table_in, product)


def store_rows(base, plane, tx_out, tx_in):
    out_x, in_x, _, _ = edges()
    for i in range(SIDE):
        plane[base + beyond(out_x) * GRID + i + 1] = piece(tx_out, i)
        plane[base + beyond(in_x) * GRID + i + 1] = piece(tx_in, i)


def rows_kernel(plane_in, tx_out, tx_in, plane):
    store_rows(PLANE, plane, tx_out, tx_in)


def store_columns(base, plane, out_blocks, ty_in):
    _, _, out_y, in_y = edges()
    for i in range(SIDE):
        plane[base + (i + 1) * GRID + beyond(out_y)] = out_blocks[i]
        plane[base + (i + 1) * GRID + beyond(in_y)] = piece(ty_in, i)


def pack_sends(base, plane, sends):
    tx_out, tx_in, ty_out, ty_more, ty_in = sends
    out_x, in_x, out_y, in_y = edges()
    for i in range(SIDE):
        rows = pl.ds(i * ROWS, ROWS)
        tx_out[rows] = plane[own_slot(out_x, i)]
        tx_in[rows] = plane[own_slot(in_x, i)]
        ty_in[rows] = plane[own_slot(i, in_y)]
        if i < 3:
            ty_out[rows] = plane[own_slot(i, out_y)]
        else:
            ty_more[pl.ds(0, ROWS)] = plane[own_slot(i, out_y)]
    for i, side in enumerate((out_x, in_x)):
        ty_more[pl.ds((1 + i) * ROWS, ROWS)] = plane[base + beyond(side) * GRID + out_y + 1]
        ty_in[pl.ds((SIDE + i) * ROWS, ROWS)] = plane[base + beyond(side) * GRID + in_y + 1]


def first_kernel(table, plane_in, sums_in, matrices_in, noise_in, *rest):
    halo, extras, (plane, sums, matrices, noise, *sends) = rest[:4], rest[4], rest[5:]
    store_rows(0, plane, *halo[:2])
    store_columns(0, plane, [piece(halo[2], i) for i in range(SIDE)], halo[3])

    def one_cell(cell):
        summed = gather_product(cell, table, SLOT, plane, matrices, noise)
        sums[cell] = summed
        plane[own_slot(cell // SIDE, cell % SIDE)] = summed.astype(jnp.bfloat16)

    cells_of(0, table, one_cell)
    pack_sends(0, plane, sends)
    for at, ref in enumerate((sends[0], sends[1], sends[3], sends[4])):
        ref[ref.shape[0] - EXTRA :] = extras[at]


def main_kernel(section, table, plane_in, sums_in, matrices, ty_out, ty_more, ty_in, *rest):
    extras, (plane, sums, *rest) = rest[:4], rest[4:]
    extras = [ref.at[pl.ds(ref.shape[0] - EXTRA, EXTRA)] for ref in extras]
    marks = read_marks(extras) if section == 1 else [table[MARKS + at] for at in range(8)]
    corners = block_of(ty_more, 1), block_of(ty_in, SIDE)
    store_columns(PLANE, plane, [piece(ty_out, i) for i in range(3)] + [piece(ty_more, 0)], ty_in)
    if section == 1:
        store_corners(plane, *corners)
    complete_halo(section - 1, plane, extras, marks)
    finish_corners(section - 1, table, plane, matrices, sums, *corners)
    count = table[COUNT]

    def one_group(group, carry):
        products = []
        for i in range(GROUP):
            item = table[ITEM + jnp.minimum(group * GROUP + i, count - 1)]
            slot = jnp.where(group * GROUP + i < count, table[SLOT + item], BLANK)
            matrix = matrices[item // 8, pl.ds(pl.multiple_of((item % 8) * LANES, LANES), LANES)]
            products.append((item // 8, jnp.dot(plane[slot], matrix, preferred_element_type=jnp.float32)))
        for cell, product in products:
            sums[cell] += product
        return carry

    lax.fori_loop(0, (count + GROUP - 1) // GROUP, one_group, 0)

    def one_cell(cell):
        plane[own_slot(cell // SIDE, cell % SIDE)] = sums[cell].astype(jnp.bfloat16)

    cells_of(section, table, one_cell)
    if section < LEVELS - 1:
        pack_sends(PLANE, plane, rest)
    else:
        result, sems = rest
        copies = [
            pltpu.make_async_copy(
                plane.at[pl.ds(own_slot(x, 0), SIDE)], result.at[pl.ds(x * SIDE, SIDE)], sems.at[x]
            )
            for x in range(SIDE)
        ]
        for copy in copies:
            copy.start()
        for copy in copies:
            copy.wait()


def corner_kernel(table, plane_in, matrices, sums, far, near, result_in, plane, result, sems):
    finish_corners(LEVELS - 1, table, plane, matrices, sums, block_of(far, 0), block_of(near, 0))
    copies = [
        pltpu.make_async_copy(plane.at[own_slot(x, y)], result.at[SIDE * x + y], sems.at[at])
        for at, (x, y) in enumerate(CORNERS)
    ]
    for copy in copies:
        copy.start()
    for copy in copies:
        copy.wait()


def cost(products, depth):
    flops = products * 2 * ROWS * depth * LANES
    return pl.CostEstimate(flops=flops, bytes_accessed=4 << 20, transcendentals=0)


def rows_of(rows):
    return jax.ShapeDtypeStruct((rows, LANES), jnp.bfloat16)


def local(earlier, innovation, conditioner, chol_factor, block_level, neighbours):
    block = earlier.shape[2:]
    tile = SIDE * SIDE
    keep = lambda value: pltpu.with_memory_space_constraint(value, pltpu.HBM)
    flat = lambda value: keep(value.reshape(tile, *value.shape[2:]))
    edge = jax.ShapeDtypeStruct((SIDE, *block), jnp.bfloat16)
    plane_shape = jax.ShapeDtypeStruct((BLANK + 1, *block), jnp.bfloat16)
    sums_shape = jax.ShapeDtypeStruct((tile, *block), jnp.float32)
    whole = jax.ShapeDtypeStruct((tile, *block), jnp.bfloat16)
    matrices_shape = jax.ShapeDtypeStruct((tile, DEPTH, LANES), jnp.bfloat16)
    table_shape = jax.ShapeDtypeStruct((TABLE,), jnp.int32)
    factors = pltpu.VMEM((tile, *chol_factor.shape[2:]), jnp.bfloat16)
    sends = pl.pallas_call(
        pack_kernel,
        out_shape=[edge] * 4,
        in_specs=[HBM],
        out_specs=[VMEM] * 4,
        scratch_shapes=[pltpu.SemaphoreType.DMA((4,))],
        compiler_params=PARAMS,
        name="pack",
    )(keep(earlier))
    sends = [send.reshape(SIDE * ROWS, LANES) for send in sends]
    sources = flat(innovation), flat(conditioner), flat(chol_factor)
    plane, matrices, noise, sums, table, codes, extras = pl.pallas_call(
        load_kernel,
        out_shape=[
            plane_shape,
            matrices_shape,
            whole,
            sums_shape,
            table_shape,
            jax.ShapeDtypeStruct(neighbours.shape, jnp.int32),
            jax.ShapeDtypeStruct((4, EXTRA, LANES), jnp.bfloat16),
        ],
        in_specs=[HBM] * 6,
        out_specs=[VMEM] * 4 + [SMEM] * 2 + [VMEM],
        scratch_shapes=[
            pltpu.SMEM(block_level.shape, jnp.int32),
            factors,
            pltpu.SemaphoreType.DMA((3, tile)),
            pltpu.SemaphoreType.DMA((14,)),
        ],
        compiler_params=PARAMS,
        cost_estimate=pl.CostEstimate(flops=0, bytes_accessed=10 << 20, transcendentals=0),
        name="load",
    )(keep(block_level), keep(neighbours), flat(earlier), *sources)
    halo = exchange(sends)
    send_rows = lambda extra: [
        rows_of(rows)
        for rows in (4 * ROWS + extra, 4 * ROWS + extra, 3 * ROWS, 3 * ROWS + extra, 6 * ROWS + extra)
    ]
    plane, sums, matrices, noise, *sends = pl.pallas_call(
        first_kernel,
        out_shape=[plane_shape, sums_shape, matrices_shape, whole, *send_rows(EXTRA)],
        in_specs=[SMEM] + [VMEM] * 9,
        out_specs=[VMEM] * 9,
        input_output_aliases={1: 0, 2: 1, 3: 2, 4: 3},
        compiler_params=PARAMS,
        cost_estimate=cost(8, DEPTH),
        name="level_0",
    )(table, plane, sums, matrices, noise, *halo, extras)
    for section in range(1, LEVELS):
        final = section == LEVELS - 1
        halo = exchange(sends)
        if section == 1:
            extras = [halo[0], halo[1], halo[3], halo[4]]
        marks_from = extras if section > 1 else []
        plane, sums, matrices, noise, items = pl.pallas_call(
            functools.partial(settled_kernel, section),
            out_shape=[plane_shape, sums_shape, matrices_shape, whole, table_shape],
            in_specs=[SMEM] * 2 + [VMEM] * 4 + [HBM] * 3 + [VMEM] * len(marks_from),
            out_specs=[VMEM] * 4 + [SMEM],
            scratch_shapes=[
                pltpu.SMEM((8 * tile,), jnp.int32),
                factors,
                pltpu.SemaphoreType.DMA((3, tile)),
            ],
            input_output_aliases={2: 0, 3: 1, 4: 2, 5: 3},
            compiler_params=PARAMS,
            cost_estimate=cost(8, DEPTH),
            name=f"settled_{section}",
        )(codes, table, plane, sums, matrices, noise, *sources, *marks_from)
        plane = pl.pallas_call(
            rows_kernel,
            out_shape=plane_shape,
            in_specs=[VMEM] * 3,
            out_specs=VMEM,
            input_output_aliases={0: 0},
            compiler_params=PARAMS,
            cost_estimate=cost(2, LANES),
            name=f"rows_{section}",
        )(plane, *halo[:2])
        if final:
            far, near = pl.pallas_call(
                forward_kernel,
                out_shape=[rows_of(2 * ROWS)] * 2,
                in_specs=[VMEM],
                out_specs=[VMEM] * 2,
                compiler_params=PARAMS,
                cost_estimate=cost(0, 0),
                name="forward",
            )(plane)
            far, near = swap(far, None, "out"), swap(near, None, "in")
        plane, sums, *sends = pl.pallas_call(
            functools.partial(main_kernel, section),
            out_shape=[plane_shape, sums_shape] + ([whole] if final else send_rows(0)),
            in_specs=[SMEM] + [VMEM] * 10,
            out_specs=[VMEM] * 2 + ([HBM] if final else [VMEM] * 5),
            scratch_shapes=[pltpu.SemaphoreType.DMA((4,))] * final,
            input_output_aliases={1: 0, 2: 1},
            compiler_params=PARAMS,
            cost_estimate=cost(16, LANES),
            name=f"level_{section}",
        )(items, plane, sums, matrices, *halo[2:], *extras)
    _, result = pl.pallas_call(
        corner_kernel,
        out_shape=[plane_shape, whole],
        in_specs=[SMEM] + [VMEM] * 5 + [HBM],
        out_specs=[VMEM, HBM],
        scratch_shapes=[pltpu.SemaphoreType.DMA((4,))],
        input_output_aliases={1: 0, 6: 1},
        compiler_params=PARAMS,
        cost_estimate=cost(4, LANES),
        name="last_corners",
    )(items, plane, matrices, sums, far, near, sends[0])
    return result.reshape(earlier.shape)


def solution(mesh):
    placed = (
        P("tx", "ty", None, None),
        P("tx", "ty", None, None),
        P("tx", "ty", None, None),
        P("tx", "ty", None, None),
        P("tx", "ty"),
        P("tx", "ty", None),
    )
    return jax.shard_map(
        local, mesh=mesh, in_specs=placed, out_specs=P("tx", "ty", None, None), check_vma=False
    )
```

```python
import functools

import jax
import jax.numpy as jnp
from jax import lax
from jax.experimental import pallas as pl
from jax.experimental.pallas import tpu as pltpu
from jax.sharding import PartitionSpec as P

LEVELS = 4
BOTH = ("tx", "ty")
SIDE = 4
GRID = 6
PLANE = GRID * GRID
BLANK = 2 * PLANE
ROWS = 256
LANES = 128
MARK = 16
EXTRA = 2 * (LANES + MARK)
DEPTH = 9 * LANES
LEVEL, SLOT, ITEM, CELLS, COUNT, CHOSEN, TABLE = 0, 16, 144, 216, 236, 237, 238
GROUP = 4
CORNERS = ((0, 0), (0, 3), (3, 0), (3, 3))
VMEM = pl.BlockSpec(memory_space=pltpu.VMEM)
SMEM = pl.BlockSpec(memory_space=pltpu.SMEM)
HBM = pl.BlockSpec(memory_space=pltpu.HBM)
PARAMS = pltpu.CompilerParams(vmem_limit_bytes=8 * 1024 * 1024)


def partner(at, size, kind):
    if kind == "in":
        return at ^ 1
    if kind == "out":
        return (at + 1) % size if at % 2 else (at - 1) % size
    return at


def swap(value, along_x, along_y):
    size_x, size_y = lax.axis_size("tx"), lax.axis_size("ty")
    pairs = [
        (x * size_y + y, partner(x, size_x, along_x) * size_y + partner(y, size_y, along_y))
        for x in range(size_x)
        for y in range(size_y)
    ]
    return lax.ppermute(value, BOTH, pairs)


def exchange(sends):
    tx_out, tx_in, *ty_out, ty_in = sends
    halo = [swap(tx_out, "out", None), swap(tx_in, "in", None)]
    return halo + [swap(part, None, "out") for part in ty_out] + [swap(ty_in, None, "in")]


def edges():
    odd_x = lax.rem(lax.axis_index("tx"), 2)
    odd_y = lax.rem(lax.axis_index("ty"), 2)
    return 3 * odd_x, 3 - 3 * odd_x, 3 * odd_y, 3 - 3 * odd_y


def beyond(edge):
    return (edge // 3) * 5


def own_slot(x, y):
    return PLANE + (x + 1) * GRID + y + 1


def piece(ref, at):
    return ref[at * ROWS : (at + 1) * ROWS]


def forward_kernel(plane, far, near):
    out_x, in_x, out_y, in_y = edges()
    for i, side in enumerate((out_x, in_x)):
        far[i * ROWS : (i + 1) * ROWS] = plane[PLANE + beyond(side) * GRID + out_y + 1]
        near[i * ROWS : (i + 1) * ROWS] = plane[PLANE + beyond(side) * GRID + in_y + 1]


def pack_kernel(earlier, tx_out, tx_in, ty_out, ty_in, sems):
    out_x, in_x, out_y, in_y = edges()
    copies = [
        pltpu.make_async_copy(earlier.at[out_x], tx_out, sems.at[0]),
        pltpu.make_async_copy(earlier.at[in_x], tx_in, sems.at[1]),
        pltpu.make_async_copy(earlier.at[:, out_y], ty_out, sems.at[2]),
        pltpu.make_async_copy(earlier.at[:, in_y], ty_in, sems.at[3]),
    ]
    for copy in copies:
        copy.start()
    for copy in copies:
        copy.wait()


def late_code(levels, codes, x, y):
    code = 2 * x + 2 * y // 3 + jnp.where(levels[x, y] > 0, 9, 0)
    found = jnp.int32(-1)
    for k in range(8):
        found = jnp.where(codes[x, y, k] == code, k, found)
    return found


def fill_slots(cell, level, codes, every, settled):
    x, y = cell // SIDE, cell % SIDE
    for k in range(8):
        code = codes[x, y, k]
        old = code >= 9
        offset = jnp.where(old, code - 9, code)
        down = (offset >= 3).astype(jnp.int32) + (offset >= 6).astype(jnp.int32)
        row, column = x + down, y + offset - 3 * down
        slot = row * GRID + column + jnp.where(old, PLANE, 0)
        edge_row, edge_column = (row == 0) | (row == 5), (column == 0) | (column == 5)
        outer = edge_row & edge_column
        waits = outer & (old == (level > 0))
        every[SLOT + 8 * cell + k] = jnp.where(waits, BLANK, slot)
        if settled is not None:
            own_corner = ((row == 1) | (row == 4)) & ((column == 1) | (column == 4))
            open_ = (old & (edge_row | edge_column | own_corner)) | outer
            settled[8 * cell + k] = jnp.where(open_, BLANK, slot)


def choose(section, levels, table):
    def one_cell(cell, at):
        table[CELLS + at] = cell
        return at + (levels[LEVEL + cell] == section).astype(jnp.int32)

    table[CHOSEN] = lax.fori_loop(0, SIDE * SIDE, one_cell, jnp.int32(0))


def each_cell(table, body):
    def one_cell(at, carry):
        body(table[CELLS + at])
        return carry

    lax.fori_loop(0, table[CHOSEN], one_cell, 0)


def each_pair(table, body):
    count = table[CHOSEN]

    def one_pair(pair, carry):
        second = jnp.minimum(2 * pair + 1, count - 1)
        body(table[CELLS + 2 * pair], table[CELLS + second], 2 * pair + 1 < count)
        return carry

    lax.fori_loop(0, (count + 1) // 2, one_pair, 0)


def cell_copies(cell, sources, targets, sems):
    innovation, conditioner, chol_factor = sources
    noise, matrices, factors = targets
    return (
        pltpu.make_async_copy(chol_factor.at[cell], factors.at[cell], sems.at[0, cell]),
        pltpu.make_async_copy(innovation.at[cell], noise.at[cell], sems.at[1, cell]),
        pltpu.make_async_copy(conditioner.at[cell], matrices.at[cell, pl.ds(0, 8 * LANES)], sems.at[2, cell]),
    )


def start_cell(cell, sources, targets, sems):
    for copy in cell_copies(cell, sources, targets, sems):
        copy.start()


def finish_cell(cell, sources, targets, sems):
    _, matrices, factors = targets
    copies = cell_copies(cell, sources, targets, sems)
    copies[0].wait()
    rows = lax.broadcasted_iota(jnp.int32, (LANES, LANES), 0)
    columns = lax.broadcasted_iota(jnp.int32, (LANES, LANES), 1)
    upper = jnp.where(rows <= columns, factors[cell].astype(jnp.float32), 0.0)
    matrices[cell, 8 * LANES :] = upper.astype(jnp.bfloat16)
    copies[1].wait()
    copies[2].wait()


def load_kernel(
    block_level, neighbours, earlier, innovation, conditioner, chol_factor, plane, matrices, noise, sums, table, codes, extras, *rest
):
    levels, factors, sems, more_sems = rest
    scalars = [
        pltpu.make_async_copy(block_level, levels, more_sems.at[12]),
        pltpu.make_async_copy(neighbours, codes, more_sems.at[13]),
    ]
    copies = [
        pltpu.make_async_copy(
            earlier.at[pl.ds(x * SIDE, SIDE)], plane.at[pl.ds((x + 1) * GRID + 1, SIDE)], more_sems.at[x]
        )
        for x in range(SIDE)
    ]
    for copy in scalars + copies:
        copy.start()

    def clear(at, carry):
        plane[at] = jnp.zeros(plane.shape[1:], plane.dtype)
        return carry

    lax.fori_loop(PLANE, BLANK + 1, clear, 0)
    for copy in scalars:
        copy.wait()
    for cell in range(SIDE * SIDE):
        table[LEVEL + cell] = levels[cell // SIDE, cell % SIDE]
    sources, targets = (innovation, conditioner, chol_factor), (noise, matrices, factors)
    choose(0, table, table)
    each_cell(table, lambda cell: start_cell(cell, sources, targets, sems))
    out_x, _, out_y, _ = edges()
    for at, (x, y) in enumerate(CORNERS):
        late = late_code(levels, codes, x, y)
        mark = jnp.full((MARK, LANES), jnp.where(late >= 0, levels[x, y], -1).astype(jnp.float32)).astype(jnp.bfloat16)
        start = pl.multiple_of(LANES * jnp.maximum(late, 0), LANES)
        matrix = conditioner.at[SIDE * x + y, pl.ds(start, LANES)]
        for way, (side, place) in enumerate(((jnp.where(out_x == x, 0, 1), y // 3), (jnp.where(out_y == y, 2, 3), x // 3))):
            copy = pltpu.make_async_copy(
                matrix, extras.at[side, pl.ds(place * LANES, LANES)], more_sems.at[4 + 2 * at + way]
            )
            copy.start()
            copies.append(copy)
            extras[side, 2 * LANES + place * MARK : 2 * LANES + (place + 1) * MARK] = mark
    each_cell(table, lambda cell: fill_slots(cell, 0, codes, table, None))
    each_cell(table, lambda cell: finish_cell(cell, sources, targets, sems))
    for copy in copies:
        copy.wait()


def read_mark(extra, place):
    return jnp.max(extra[2 * LANES + place * MARK : 2 * LANES + (place + 1) * MARK].astype(jnp.float32))


def complete_halo(recent, plane, extras):
    out_x, in_x, out_y, in_y = edges()
    source = PLANE if recent else 0
    todo = []
    for side in (out_x, in_x):
        for place in (0, 1):
            todo.append((beyond(side) * GRID + 1 + 3 * place, (side + 1) * GRID + 5 * place))
    for side in (out_y, in_y):
        for place in (0, 1):
            todo.append(((1 + 3 * place) * GRID + beyond(side), 5 * place * GRID + side + 1))
    marks = [read_mark(extra, place) for extra in extras for place in (0, 1)]
    for at, (cell, other) in enumerate(todo):

        @pl.when(marks[at] == recent)
        def _(cell=cell, other=other, extra=extras[at // 2], place=at % 2):
            product = jnp.dot(
                plane[source + other], extra[place * LANES : (place + 1) * LANES], preferred_element_type=jnp.float32
            )
            plane[PLANE + cell] = (plane[PLANE + cell].astype(jnp.float32) + product).astype(jnp.bfloat16)


def finish_corners(recent, extras, plane, sums, far, near):
    out_x, _, out_y, _ = edges()
    facing = [extras.at[jnp.where(out_y == y, 2, 3)] for _, y in CORNERS]
    places = [x // 3 for x, _ in CORNERS]
    marks = [read_mark(extra, place) for extra, place in zip(facing, places, strict=True)]
    for (x, y), extra, place, mark in zip(CORNERS, facing, places, marks, strict=True):

        @pl.when(mark == recent)
        def _(x=x, y=y, extra=extra, place=place):
            side = jnp.where(out_x == x, 0, 1)
            block = jnp.where(out_y == y, far(side), near(side))
            matrix = extra[place * LANES : (place + 1) * LANES]
            summed = sums[SIDE * x + y] + jnp.dot(block, matrix, preferred_element_type=jnp.float32)
            plane[own_slot(x, y)] = summed.astype(jnp.bfloat16)

    return [mark == recent for mark in marks]


def block_of(ref, first):
    return lambda at: ref[pl.ds(pl.multiple_of((first + at) * ROWS, ROWS), ROWS)]


def store_corners(plane, far, near):
    out_x, _, out_y, _ = edges()
    for x, y in CORNERS:
        side = jnp.where(out_x == x, 0, 1)
        plane[beyond(x) * GRID + beyond(y)] = jnp.where(out_y == y, far(side), near(side))


def gather_product(cell, slots, first, plane, matrices, noise):
    parts = [plane[slots[first + 8 * cell + k]] for k in range(8)] + [noise[cell]]
    return jnp.dot(jnp.concatenate(parts, axis=1), matrices[cell], preferred_element_type=jnp.float32)


def settled_kernel(section, codes, table_in, plane_in, sums_in, matrices_in, noise_in, *rest):
    sources, rest = rest[:3], rest[3:]
    plane, sums, matrices, noise, table, settled, factors, sems = rest
    targets = noise, matrices, factors
    choose(section, table_in, table)
    each_cell(table, lambda cell: start_cell(cell, sources, targets, sems))

    def one_cell(at, found):
        cell = table[CELLS + at]
        fill_slots(cell, section, codes, table, settled)
        for k in range(8):
            table[ITEM + found] = 8 * cell + k
            found += (table[SLOT + 8 * cell + k] != settled[8 * cell + k]).astype(jnp.int32)
        return found

    table[COUNT] = lax.fori_loop(0, table[CHOSEN], one_cell, jnp.int32(0))

    def products(first, second, fresh):
        finish_cell(first, sources, targets, sems)

        @pl.when(fresh)
        def _():
            finish_cell(second, sources, targets, sems)

        both = [gather_product(cell, settled, 0, plane, matrices, noise) for cell in (first, second)]
        sums[first] = both[0]
        sums[second] = both[1]

    each_pair(table, products)


def store_rows(base, plane, tx_out, tx_in):
    out_x, in_x, _, _ = edges()
    for i in range(SIDE):
        plane[base + beyond(out_x) * GRID + i + 1] = piece(tx_out, i)
        plane[base + beyond(in_x) * GRID + i + 1] = piece(tx_in, i)


def rows_kernel(plane_in, tx_out, tx_in, plane):
    store_rows(PLANE, plane, tx_out, tx_in)


def store_columns(base, plane, out_blocks, ty_in):
    _, _, out_y, in_y = edges()
    for i in range(SIDE):
        plane[base + (i + 1) * GRID + beyond(out_y)] = out_blocks[i]
        plane[base + (i + 1) * GRID + beyond(in_y)] = piece(ty_in, i)


def pack_sends(base, plane, sends):
    tx_out, tx_in, ty_out, ty_more, ty_in = sends
    out_x, in_x, out_y, in_y = edges()
    for i in range(SIDE):
        rows = pl.ds(i * ROWS, ROWS)
        tx_out[rows] = plane[own_slot(out_x, i)]
        tx_in[rows] = plane[own_slot(in_x, i)]
        ty_in[rows] = plane[own_slot(i, in_y)]
        if i < 3:
            ty_out[rows] = plane[own_slot(i, out_y)]
        else:
            ty_more[pl.ds(0, ROWS)] = plane[own_slot(i, out_y)]
    for i, side in enumerate((out_x, in_x)):
        ty_more[pl.ds((1 + i) * ROWS, ROWS)] = plane[base + beyond(side) * GRID + out_y + 1]
        ty_in[pl.ds((SIDE + i) * ROWS, ROWS)] = plane[base + beyond(side) * GRID + in_y + 1]


def fetch(table, scalars, sem):
    copy = pltpu.make_async_copy(table, scalars, sem)
    copy.start()
    return copy.wait


def first_kernel(table_in, plane_in, sums_in, matrices_in, noise_in, *rest):
    halo, extras, (plane, sums, matrices, noise, *sends) = rest[:4], rest[4], rest[5:-2]
    table, sem = rest[-2:]
    wait = fetch(table_in, table, sem)
    store_rows(0, plane, *halo[:2])
    store_columns(0, plane, [piece(halo[2], i) for i in range(SIDE)], halo[3])
    for at, ref in enumerate((sends[0], sends[1], sends[3], sends[4])):
        ref[ref.shape[0] - EXTRA :] = extras[at]
    wait()

    def products(first, second, fresh):
        cells = first, second
        both = [gather_product(cell, table, SLOT, plane, matrices, noise) for cell in cells]
        for cell, summed in zip(cells, both, strict=True):
            sums[cell] = summed
            plane[own_slot(cell // SIDE, cell % SIDE)] = summed.astype(jnp.bfloat16)

    each_pair(table, products)
    pack_sends(0, plane, sends)


def main_kernel(section, table_in, plane_in, sums_in, matrices, own, ty_out, ty_more, ty_in, *rest):
    extras, rest = rest[:4], rest[4:]
    plane, sums, *rest, table, sem = rest
    wait = fetch(table_in, table, sem)
    extras = [ref.at[pl.ds(ref.shape[0] - EXTRA, EXTRA)] for ref in extras]
    corners = block_of(ty_more, 1), block_of(ty_in, SIDE)
    store_columns(PLANE, plane, [piece(ty_out, i) for i in range(3)] + [piece(ty_more, 0)], ty_in)
    if section == 1:
        store_corners(plane, *corners)
    complete_halo(section - 1, plane, extras)
    finish_corners(section - 1, own, plane, sums, *corners)
    wait()
    count = table[COUNT]

    def one_group(group, carry):
        products = []
        for i in range(GROUP):
            item = table[ITEM + jnp.minimum(group * GROUP + i, count - 1)]
            slot = jnp.where(group * GROUP + i < count, table[SLOT + item], BLANK)
            matrix = matrices[item // 8, pl.ds(pl.multiple_of((item % 8) * LANES, LANES), LANES)]
            products.append((item // 8, jnp.dot(plane[slot], matrix, preferred_element_type=jnp.float32)))
        for cell, product in products:
            sums[cell] += product
        return carry

    lax.fori_loop(0, (count + GROUP - 1) // GROUP, one_group, 0)

    def one_cell(cell):
        plane[own_slot(cell // SIDE, cell % SIDE)] = sums[cell].astype(jnp.bfloat16)

    each_cell(table, one_cell)
    if section < LEVELS - 1:
        pack_sends(PLANE, plane, rest)
    else:
        result, sems = rest
        copies = [
            pltpu.make_async_copy(
                plane.at[pl.ds(own_slot(x, 0), SIDE)], result.at[pl.ds(x * SIDE, SIDE)], sems.at[x]
            )
            for x in range(SIDE)
        ]
        for copy in copies:
            copy.start()
        for copy in copies:
            copy.wait()


def corner_kernel(plane_in, own, sums, far, near, result_in, plane, result, sems):
    changed = finish_corners(LEVELS - 1, own, plane, sums, block_of(far, 0), block_of(near, 0))
    copies = [
        pltpu.make_async_copy(plane.at[own_slot(x, y)], result.at[SIDE * x + y], sems.at[at])
        for at, (x, y) in enumerate(CORNERS)
    ]
    for copy, needed in zip(copies, changed, strict=True):
        pl.when(needed)(copy.start)
    for copy, needed in zip(copies, changed, strict=True):
        pl.when(needed)(copy.wait)


def cost(products, depth):
    flops = products * 2 * ROWS * depth * LANES
    return pl.CostEstimate(flops=flops, bytes_accessed=4 << 20, transcendentals=0)


def rows_of(rows):
    return jax.ShapeDtypeStruct((rows, LANES), jnp.bfloat16)


def local(earlier, innovation, conditioner, chol_factor, block_level, neighbours):
    block = earlier.shape[2:]
    tile = SIDE * SIDE
    keep = lambda value: pltpu.with_memory_space_constraint(value, pltpu.HBM)
    flat = lambda value: keep(value.reshape(tile, *value.shape[2:]))
    edge = jax.ShapeDtypeStruct((SIDE, *block), jnp.bfloat16)
    plane_shape = jax.ShapeDtypeStruct((BLANK + 1, *block), jnp.bfloat16)
    sums_shape = jax.ShapeDtypeStruct((tile, *block), jnp.float32)
    whole = jax.ShapeDtypeStruct((tile, *block), jnp.bfloat16)
    matrices_shape = jax.ShapeDtypeStruct((tile, DEPTH, LANES), jnp.bfloat16)
    table_shape = jax.ShapeDtypeStruct((TABLE,), jnp.int32)
    scalars = [pltpu.SMEM((TABLE,), jnp.int32), pltpu.SemaphoreType.DMA]
    factors = pltpu.VMEM((tile, *chol_factor.shape[2:]), jnp.bfloat16)
    sends = pl.pallas_call(
        pack_kernel,
        out_shape=[edge] * 4,
        in_specs=[HBM],
        out_specs=[VMEM] * 4,
        scratch_shapes=[pltpu.SemaphoreType.DMA((4,))],
        compiler_params=PARAMS,
        name="pack",
    )(keep(earlier))
    sends = [send.reshape(SIDE * ROWS, LANES) for send in sends]
    sources = flat(innovation), flat(conditioner), flat(chol_factor)
    plane, matrices, noise, sums, table, codes, own = pl.pallas_call(
        load_kernel,
        out_shape=[
            plane_shape,
            matrices_shape,
            whole,
            sums_shape,
            table_shape,
            jax.ShapeDtypeStruct(neighbours.shape, jnp.int32),
            jax.ShapeDtypeStruct((4, EXTRA, LANES), jnp.bfloat16),
        ],
        in_specs=[HBM] * 6,
        out_specs=[VMEM] * 4 + [SMEM] * 2 + [VMEM],
        scratch_shapes=[
            pltpu.SMEM(block_level.shape, jnp.int32),
            factors,
            pltpu.SemaphoreType.DMA((3, tile)),
            pltpu.SemaphoreType.DMA((14,)),
        ],
        compiler_params=PARAMS,
        cost_estimate=pl.CostEstimate(flops=0, bytes_accessed=10 << 20, transcendentals=0),
        name="load",
    )(keep(block_level), keep(neighbours), flat(earlier), *sources)
    halo = exchange(sends)
    send_rows = lambda extra: [
        rows_of(rows)
        for rows in (4 * ROWS + extra, 4 * ROWS + extra, 3 * ROWS, 3 * ROWS + extra, 6 * ROWS + extra)
    ]
    plane, sums, matrices, noise, *sends = pl.pallas_call(
        first_kernel,
        out_shape=[plane_shape, sums_shape, matrices_shape, whole, *send_rows(EXTRA)],
        in_specs=[VMEM] * 10,
        out_specs=[VMEM] * 9,
        scratch_shapes=scalars,
        input_output_aliases={1: 0, 2: 1, 3: 2, 4: 3},
        compiler_params=PARAMS,
        cost_estimate=cost(8, DEPTH),
        name="level_0",
    )(table, plane, sums, matrices, noise, *halo, own)
    for section in range(1, LEVELS):
        final = section == LEVELS - 1
        halo = exchange(sends)
        if section == 1:
            extras = [halo[0], halo[1], halo[3], halo[4]]
        plane, sums, matrices, noise, items = pl.pallas_call(
            functools.partial(settled_kernel, section),
            out_shape=[plane_shape, sums_shape, matrices_shape, whole, table_shape],
            in_specs=[SMEM] * 2 + [VMEM] * 4 + [HBM] * 3,
            out_specs=[VMEM] * 4 + [SMEM],
            scratch_shapes=[
                pltpu.SMEM((8 * tile,), jnp.int32),
                factors,
                pltpu.SemaphoreType.DMA((3, tile)),
            ],
            input_output_aliases={2: 0, 3: 1, 4: 2, 5: 3},
            compiler_params=PARAMS,
            cost_estimate=cost(8, DEPTH),
            name=f"settled_{section}",
        )(codes, table, plane, sums, matrices, noise, *sources)
        plane = pl.pallas_call(
            rows_kernel,
            out_shape=plane_shape,
            in_specs=[VMEM] * 3,
            out_specs=VMEM,
            input_output_aliases={0: 0},
            compiler_params=PARAMS,
            cost_estimate=cost(2, LANES),
            name=f"rows_{section}",
        )(plane, *halo[:2])
        if final:
            far, near = pl.pallas_call(
                forward_kernel,
                out_shape=[rows_of(2 * ROWS)] * 2,
                in_specs=[VMEM],
                out_specs=[VMEM] * 2,
                compiler_params=PARAMS,
                cost_estimate=cost(0, 0),
                name="forward",
            )(plane)
            far, near = swap(far, None, "out"), swap(near, None, "in")
        plane, sums, *sends = pl.pallas_call(
            functools.partial(main_kernel, section),
            out_shape=[plane_shape, sums_shape] + ([whole] if final else send_rows(0)),
            in_specs=[VMEM] * 12,
            out_specs=[VMEM] * 2 + ([HBM] if final else [VMEM] * 5),
            scratch_shapes=[pltpu.SemaphoreType.DMA((4,))] * final + scalars,
            input_output_aliases={1: 0, 2: 1},
            compiler_params=PARAMS,
            cost_estimate=cost(16, LANES),
            name=f"level_{section}",
        )(items, plane, sums, matrices, own, *halo[2:], *extras)
    _, result = pl.pallas_call(
        corner_kernel,
        out_shape=[plane_shape, whole],
        in_specs=[VMEM] * 5 + [HBM],
        out_specs=[VMEM, HBM],
        scratch_shapes=[pltpu.SemaphoreType.DMA((4,))],
        input_output_aliases={0: 0, 5: 1},
        compiler_params=PARAMS,
        cost_estimate=cost(4, LANES),
        name="last_corners",
    )(plane, own, sums, far, near, sends[0])
    return result.reshape(earlier.shape)


def solution(mesh):
    placed = (
        P("tx", "ty", None, None),
        P("tx", "ty", None, None),
        P("tx", "ty", None, None),
        P("tx", "ty", None, None),
        P("tx", "ty"),
        P("tx", "ty", None),
    )
    return jax.shard_map(
        local, mesh=mesh, in_specs=placed, out_specs=P("tx", "ty", None, None), check_vma=False
    )
```

```python
import functools

import jax
import jax.numpy as jnp
from jax import lax
from jax.experimental import pallas as pl
from jax.experimental.pallas import tpu as pltpu
from jax.sharding import PartitionSpec as P

LEVELS = 4
BOTH = ("tx", "ty")
SIDE = 4
GRID = 6
PLANE = GRID * GRID
BLANK = 2 * PLANE
ROWS = 256
LANES = 128
MARK = 16
EXTRA = 2 * (LANES + MARK)
DEPTH = 9 * LANES
LEVEL, SLOT, ITEM, CELLS, COUNT, CHOSEN, TABLE = 0, 16, 144, 216, 236, 237, 238
GROUP = 4
CORNERS = ((0, 0), (0, 3), (3, 0), (3, 3))
VMEM = pl.BlockSpec(memory_space=pltpu.VMEM)
SMEM = pl.BlockSpec(memory_space=pltpu.SMEM)
HBM = pl.BlockSpec(memory_space=pltpu.HBM)
PARAMS = pltpu.CompilerParams(vmem_limit_bytes=8 * 1024 * 1024)


def partner(at, size, kind):
    if kind == "in":
        return at ^ 1
    if kind == "out":
        return (at + 1) % size if at % 2 else (at - 1) % size
    return at


def swap(value, along_x, along_y):
    size_x, size_y = lax.axis_size("tx"), lax.axis_size("ty")
    pairs = [
        (x * size_y + y, partner(x, size_x, along_x) * size_y + partner(y, size_y, along_y))
        for x in range(size_x)
        for y in range(size_y)
    ]
    return lax.ppermute(value, BOTH, pairs)


def exchange(sends):
    tx_out, tx_in, ty_out, ty_in = sends
    return swap(tx_out, "out", None), swap(tx_in, "in", None), swap(ty_out, None, "out"), swap(ty_in, None, "in")


def edges():
    odd_x = lax.rem(lax.axis_index("tx"), 2)
    odd_y = lax.rem(lax.axis_index("ty"), 2)
    return 3 * odd_x, 3 - 3 * odd_x, 3 * odd_y, 3 - 3 * odd_y


def beyond(edge):
    return (edge // 3) * 5


def own_slot(x, y):
    return PLANE + (x + 1) * GRID + y + 1


def piece(ref, at):
    return ref[at * ROWS : (at + 1) * ROWS]


def forward_kernel(plane, far, near):
    out_x, in_x, out_y, in_y = edges()
    for i, side in enumerate((out_x, in_x)):
        far[i * ROWS : (i + 1) * ROWS] = plane[PLANE + beyond(side) * GRID + out_y + 1]
        near[i * ROWS : (i + 1) * ROWS] = plane[PLANE + beyond(side) * GRID + in_y + 1]


def pack_kernel(earlier, tx_out, tx_in, ty_out, ty_in, sems):
    out_x, in_x, out_y, in_y = edges()
    copies = [
        pltpu.make_async_copy(earlier.at[out_x], tx_out, sems.at[0]),
        pltpu.make_async_copy(earlier.at[in_x], tx_in, sems.at[1]),
        pltpu.make_async_copy(earlier.at[:, out_y], ty_out, sems.at[2]),
        pltpu.make_async_copy(earlier.at[:, in_y], ty_in, sems.at[3]),
    ]
    for copy in copies:
        copy.start()
    for copy in copies:
        copy.wait()


def late_code(levels, codes, x, y):
    code = 2 * x + 2 * y // 3 + jnp.where(levels[x, y] > 0, 9, 0)
    found = jnp.int32(-1)
    for k in range(8):
        found = jnp.where(codes[x, y, k] == code, k, found)
    return found


def fill_slots(cell, level, codes, every, settled):
    x, y = cell // SIDE, cell % SIDE
    for k in range(8):
        code = codes[x, y, k]
        old = code >= 9
        offset = jnp.where(old, code - 9, code)
        down = (offset >= 3).astype(jnp.int32) + (offset >= 6).astype(jnp.int32)
        row, column = x + down, y + offset - 3 * down
        slot = row * GRID + column + jnp.where(old, PLANE, 0)
        edge_row, edge_column = (row == 0) | (row == 5), (column == 0) | (column == 5)
        outer = edge_row & edge_column
        waits = outer & (old == (level > 0))
        every[SLOT + 8 * cell + k] = jnp.where(waits, BLANK, slot)
        if settled is not None:
            own_corner = ((row == 1) | (row == 4)) & ((column == 1) | (column == 4))
            open_ = (old & (edge_row | edge_column | own_corner)) | outer
            settled[8 * cell + k] = jnp.where(open_, BLANK, slot)


def choose(section, levels, table):
    def one_cell(cell, at):
        table[CELLS + at] = cell
        return at + (levels[LEVEL + cell] == section).astype(jnp.int32)

    table[CHOSEN] = lax.fori_loop(0, SIDE * SIDE, one_cell, jnp.int32(0))


def each_cell(table, body):
    def one_cell(at, carry):
        body(table[CELLS + at])
        return carry

    lax.fori_loop(0, table[CHOSEN], one_cell, 0)


def each_pair(table, body):
    count = table[CHOSEN]

    def one_pair(pair, carry):
        second = jnp.minimum(2 * pair + 1, count - 1)
        body(table[CELLS + 2 * pair], table[CELLS + second], 2 * pair + 1 < count)
        return carry

    lax.fori_loop(0, (count + 1) // 2, one_pair, 0)


def cell_copies(cell, sources, targets, sems):
    innovation, conditioner, chol_factor = sources
    noise, matrices, factors = targets
    return (
        pltpu.make_async_copy(chol_factor.at[cell], factors.at[cell], sems.at[0, cell]),
        pltpu.make_async_copy(innovation.at[cell], noise.at[cell], sems.at[1, cell]),
        pltpu.make_async_copy(conditioner.at[cell], matrices.at[cell, pl.ds(0, 8 * LANES)], sems.at[2, cell]),
    )


def start_cell(cell, sources, targets, sems):
    for copy in cell_copies(cell, sources, targets, sems):
        copy.start()


def finish_cell(cell, sources, targets, sems):
    _, matrices, factors = targets
    copies = cell_copies(cell, sources, targets, sems)
    copies[0].wait()
    rows = lax.broadcasted_iota(jnp.int32, (LANES, LANES), 0)
    columns = lax.broadcasted_iota(jnp.int32, (LANES, LANES), 1)
    upper = jnp.where(rows <= columns, factors[cell].astype(jnp.float32), 0.0)
    matrices[cell, 8 * LANES :] = upper.astype(jnp.bfloat16)
    copies[1].wait()
    copies[2].wait()


def load_kernel(
    block_level, neighbours, earlier, innovation, conditioner, chol_factor, plane, matrices, noise, sums, table, codes, extras, *rest
):
    levels, factors, sems, more_sems = rest
    scalars = [
        pltpu.make_async_copy(block_level, levels, more_sems.at[12]),
        pltpu.make_async_copy(neighbours, codes, more_sems.at[13]),
    ]
    copies = [
        pltpu.make_async_copy(
            earlier.at[pl.ds(x * SIDE, SIDE)], plane.at[pl.ds((x + 1) * GRID + 1, SIDE)], more_sems.at[x]
        )
        for x in range(SIDE)
    ]
    for copy in scalars + copies:
        copy.start()

    def clear(at, carry):
        plane[at] = jnp.zeros(plane.shape[1:], plane.dtype)
        return carry

    lax.fori_loop(PLANE, BLANK + 1, clear, 0)
    for copy in scalars:
        copy.wait()
    for cell in range(SIDE * SIDE):
        table[LEVEL + cell] = levels[cell // SIDE, cell % SIDE]
    sources, targets = (innovation, conditioner, chol_factor), (noise, matrices, factors)
    choose(0, table, table)
    each_cell(table, lambda cell: start_cell(cell, sources, targets, sems))
    out_x, _, out_y, _ = edges()
    for at, (x, y) in enumerate(CORNERS):
        late = late_code(levels, codes, x, y)
        mark = jnp.full((MARK, LANES), jnp.where(late >= 0, levels[x, y], -1).astype(jnp.float32)).astype(jnp.bfloat16)
        start = pl.multiple_of(LANES * jnp.maximum(late, 0), LANES)
        matrix = conditioner.at[SIDE * x + y, pl.ds(start, LANES)]
        for way, (side, place) in enumerate(((jnp.where(out_x == x, 0, 1), y // 3), (jnp.where(out_y == y, 2, 3), x // 3))):
            copy = pltpu.make_async_copy(
                matrix, extras.at[side, pl.ds(place * LANES, LANES)], more_sems.at[4 + 2 * at + way]
            )
            copy.start()
            copies.append(copy)
            extras[side, 2 * LANES + place * MARK : 2 * LANES + (place + 1) * MARK] = mark
    each_cell(table, lambda cell: fill_slots(cell, 0, codes, table, None))
    each_cell(table, lambda cell: finish_cell(cell, sources, targets, sems))
    for copy in copies:
        copy.wait()


def read_mark(extra, place):
    return jnp.max(extra[2 * LANES + place * MARK : 2 * LANES + (place + 1) * MARK].astype(jnp.float32))


def complete_halo(recent, plane, extras):
    out_x, in_x, out_y, in_y = edges()
    source = PLANE if recent else 0
    todo = []
    for side in (out_x, in_x):
        for place in (0, 1):
            todo.append((beyond(side) * GRID + 1 + 3 * place, (side + 1) * GRID + 5 * place))
    for side in (out_y, in_y):
        for place in (0, 1):
            todo.append(((1 + 3 * place) * GRID + beyond(side), 5 * place * GRID + side + 1))
    marks = [read_mark(extra, place) for extra in extras for place in (0, 1)]
    for at, (cell, other) in enumerate(todo):

        @pl.when(marks[at] == recent)
        def _(cell=cell, other=other, extra=extras[at // 2], place=at % 2):
            product = jnp.dot(
                plane[source + other], extra[place * LANES : (place + 1) * LANES], preferred_element_type=jnp.float32
            )
            plane[PLANE + cell] = (plane[PLANE + cell].astype(jnp.float32) + product).astype(jnp.bfloat16)


def finish_corners(recent, extras, plane, sums, far, near):
    out_x, _, out_y, _ = edges()
    facing = [extras.at[jnp.where(out_y == y, 2, 3)] for _, y in CORNERS]
    places = [x // 3 for x, _ in CORNERS]
    marks = [read_mark(extra, place) for extra, place in zip(facing, places, strict=True)]
    for (x, y), extra, place, mark in zip(CORNERS, facing, places, marks, strict=True):

        @pl.when(mark == recent)
        def _(x=x, y=y, extra=extra, place=place):
            side = jnp.where(out_x == x, 0, 1)
            block = jnp.where(out_y == y, far(side), near(side))
            matrix = extra[place * LANES : (place + 1) * LANES]
            summed = sums[SIDE * x + y] + jnp.dot(block, matrix, preferred_element_type=jnp.float32)
            plane[own_slot(x, y)] = summed.astype(jnp.bfloat16)

    return [mark == recent for mark in marks]


def block_of(ref, first):
    return lambda at: ref[pl.ds(pl.multiple_of((first + at) * ROWS, ROWS), ROWS)]


def store_corners(plane, far, near):
    out_x, _, out_y, _ = edges()
    for x, y in CORNERS:
        side = jnp.where(out_x == x, 0, 1)
        plane[beyond(x) * GRID + beyond(y)] = jnp.where(out_y == y, far(side), near(side))


def gather_product(cell, slots, first, plane, matrices, noise):
    parts = [plane[slots[first + 8 * cell + k]] for k in range(8)] + [noise[cell]]
    return jnp.dot(jnp.concatenate(parts, axis=1), matrices[cell], preferred_element_type=jnp.float32)


def settled_kernel(section, codes, table_in, plane_in, sums_in, matrices_in, noise_in, *rest):
    sources, rest = rest[:3], rest[3:]
    plane, sums, matrices, noise, table, settled, factors, sems = rest
    targets = noise, matrices, factors
    choose(section, table_in, table)
    each_cell(table, lambda cell: start_cell(cell, sources, targets, sems))

    def one_cell(at, found):
        cell = table[CELLS + at]
        fill_slots(cell, section, codes, table, settled)
        for k in range(8):
            table[ITEM + found] = 8 * cell + k
            found += (table[SLOT + 8 * cell + k] != settled[8 * cell + k]).astype(jnp.int32)
        return found

    table[COUNT] = lax.fori_loop(0, table[CHOSEN], one_cell, jnp.int32(0))

    def products(first, second, fresh):
        finish_cell(first, sources, targets, sems)

        @pl.when(fresh)
        def _():
            finish_cell(second, sources, targets, sems)

        both = [gather_product(cell, settled, 0, plane, matrices, noise) for cell in (first, second)]
        sums[first] = both[0]
        sums[second] = both[1]

    each_pair(table, products)


def rows_kernel(base, outward, plane_in, halo, plane):
    out_x, in_x, _, _ = edges()
    row = beyond(out_x if outward else in_x)
    for i in range(SIDE):
        plane[base + row * GRID + i + 1] = piece(halo, i)


def take_rows(base, plane, halo, name):
    for outward, part, products in ((True, halo[0], 16), (False, halo[1], 64)):
        plane = pl.pallas_call(
            functools.partial(rows_kernel, base, outward),
            out_shape=jax.ShapeDtypeStruct(plane.shape, plane.dtype),
            in_specs=[VMEM] * 2,
            out_specs=VMEM,
            input_output_aliases={0: 0},
            compiler_params=PARAMS,
            cost_estimate=cost(products, DEPTH),
            name=f"{name}_{'out' if outward else 'in'}",
        )(plane, part)
    return plane


def store_columns(base, plane, ty_out, ty_in):
    _, _, out_y, in_y = edges()
    for i in range(SIDE):
        plane[base + (i + 1) * GRID + beyond(out_y)] = piece(ty_out, i)
        plane[base + (i + 1) * GRID + beyond(in_y)] = piece(ty_in, i)


def pack_sends(base, plane, sends):
    tx_out, tx_in, ty_out, ty_in = sends
    out_x, in_x, out_y, in_y = edges()
    for i in range(SIDE):
        rows = pl.ds(i * ROWS, ROWS)
        tx_out[rows] = plane[own_slot(out_x, i)]
        tx_in[rows] = plane[own_slot(in_x, i)]
        ty_out[rows] = plane[own_slot(i, out_y)]
        ty_in[rows] = plane[own_slot(i, in_y)]
    for i, side in enumerate((out_x, in_x)):
        rows = pl.ds((SIDE + i) * ROWS, ROWS)
        ty_out[rows] = plane[base + beyond(side) * GRID + out_y + 1]
        ty_in[rows] = plane[base + beyond(side) * GRID + in_y + 1]


def fetch(table, scalars, sem):
    copy = pltpu.make_async_copy(table, scalars, sem)
    copy.start()
    return copy.wait


def first_kernel(table_in, plane_in, sums_in, matrices_in, noise_in, *rest):
    halo, extras, (plane, sums, matrices, noise, *sends) = rest[:2], rest[2], rest[3:-2]
    table, sem = rest[-2:]
    wait = fetch(table_in, table, sem)
    store_columns(0, plane, *halo)
    for at, ref in enumerate(sends):
        ref[ref.shape[0] - EXTRA :] = extras[at]
    wait()

    def products(first, second, fresh):
        cells = first, second
        both = [gather_product(cell, table, SLOT, plane, matrices, noise) for cell in cells]
        for cell, summed in zip(cells, both, strict=True):
            sums[cell] = summed
            plane[own_slot(cell // SIDE, cell % SIDE)] = summed.astype(jnp.bfloat16)

    each_pair(table, products)
    pack_sends(0, plane, sends)


def main_kernel(section, table_in, plane_in, sums_in, matrices, own, ty_out, ty_in, *rest):
    extras, rest = rest[:4], rest[4:]
    plane, sums, *rest, table, sem = rest
    wait = fetch(table_in, table, sem)
    extras = [ref.at[pl.ds(ref.shape[0] - EXTRA, EXTRA)] for ref in extras]
    corners = block_of(ty_out, SIDE), block_of(ty_in, SIDE)
    store_columns(PLANE, plane, ty_out, ty_in)
    if section == 1:
        store_corners(plane, *corners)
    complete_halo(section - 1, plane, extras)
    finish_corners(section - 1, own, plane, sums, *corners)
    wait()
    count = table[COUNT]

    def one_group(group, carry):
        products = []
        for i in range(GROUP):
            item = table[ITEM + jnp.minimum(group * GROUP + i, count - 1)]
            slot = jnp.where(group * GROUP + i < count, table[SLOT + item], BLANK)
            matrix = matrices[item // 8, pl.ds(pl.multiple_of((item % 8) * LANES, LANES), LANES)]
            products.append((item // 8, jnp.dot(plane[slot], matrix, preferred_element_type=jnp.float32)))
        for cell, product in products:
            sums[cell] += product
        return carry

    lax.fori_loop(0, (count + GROUP - 1) // GROUP, one_group, 0)

    def one_cell(cell):
        plane[own_slot(cell // SIDE, cell % SIDE)] = sums[cell].astype(jnp.bfloat16)

    each_cell(table, one_cell)
    if section < LEVELS - 1:
        pack_sends(PLANE, plane, rest)
    else:
        result, sems = rest
        copies = [
            pltpu.make_async_copy(
                plane.at[pl.ds(own_slot(x, 0), SIDE)], result.at[pl.ds(x * SIDE, SIDE)], sems.at[x]
            )
            for x in range(SIDE)
        ]
        for copy in copies:
            copy.start()
        for copy in copies:
            copy.wait()


def corner_kernel(plane_in, own, sums, far, near, result_in, plane, result, sems):
    changed = finish_corners(LEVELS - 1, own, plane, sums, block_of(far, 0), block_of(near, 0))
    copies = [
        pltpu.make_async_copy(plane.at[own_slot(x, y)], result.at[SIDE * x + y], sems.at[at])
        for at, (x, y) in enumerate(CORNERS)
    ]
    for copy, needed in zip(copies, changed, strict=True):
        pl.when(needed)(copy.start)
    for copy, needed in zip(copies, changed, strict=True):
        pl.when(needed)(copy.wait)


def cost(products, depth):
    flops = products * 2 * ROWS * depth * LANES
    return pl.CostEstimate(flops=flops, bytes_accessed=4 << 20, transcendentals=0)


def rows_of(rows):
    return jax.ShapeDtypeStruct((rows, LANES), jnp.bfloat16)


def local(earlier, innovation, conditioner, chol_factor, block_level, neighbours):
    block = earlier.shape[2:]
    tile = SIDE * SIDE
    keep = lambda value: pltpu.with_memory_space_constraint(value, pltpu.HBM)
    flat = lambda value: keep(value.reshape(tile, *value.shape[2:]))
    edge = jax.ShapeDtypeStruct((SIDE, *block), jnp.bfloat16)
    plane_shape = jax.ShapeDtypeStruct((BLANK + 1, *block), jnp.bfloat16)
    sums_shape = jax.ShapeDtypeStruct((tile, *block), jnp.float32)
    whole = jax.ShapeDtypeStruct((tile, *block), jnp.bfloat16)
    matrices_shape = jax.ShapeDtypeStruct((tile, DEPTH, LANES), jnp.bfloat16)
    table_shape = jax.ShapeDtypeStruct((TABLE,), jnp.int32)
    scalars = [pltpu.SMEM((TABLE,), jnp.int32), pltpu.SemaphoreType.DMA]
    factors = pltpu.VMEM((tile, *chol_factor.shape[2:]), jnp.bfloat16)
    sends = pl.pallas_call(
        pack_kernel,
        out_shape=[edge] * 4,
        in_specs=[HBM],
        out_specs=[VMEM] * 4,
        scratch_shapes=[pltpu.SemaphoreType.DMA((4,))],
        compiler_params=PARAMS,
        name="pack",
    )(keep(earlier))
    sends = [send.reshape(SIDE * ROWS, LANES) for send in sends]
    sources = flat(innovation), flat(conditioner), flat(chol_factor)
    plane, matrices, noise, sums, table, codes, own = pl.pallas_call(
        load_kernel,
        out_shape=[
            plane_shape,
            matrices_shape,
            whole,
            sums_shape,
            table_shape,
            jax.ShapeDtypeStruct(neighbours.shape, jnp.int32),
            jax.ShapeDtypeStruct((4, EXTRA, LANES), jnp.bfloat16),
        ],
        in_specs=[HBM] * 6,
        out_specs=[VMEM] * 4 + [SMEM] * 2 + [VMEM],
        scratch_shapes=[
            pltpu.SMEM(block_level.shape, jnp.int32),
            factors,
            pltpu.SemaphoreType.DMA((3, tile)),
            pltpu.SemaphoreType.DMA((14,)),
        ],
        compiler_params=PARAMS,
        cost_estimate=pl.CostEstimate(flops=0, bytes_accessed=10 << 20, transcendentals=0),
        name="load",
    )(keep(block_level), keep(neighbours), flat(earlier), *sources)
    halo = exchange(sends)
    plane = take_rows(0, plane, halo, "rows_0")
    send_rows = lambda extra: [rows_of(4 * ROWS + extra)] * 2 + [rows_of(6 * ROWS + extra)] * 2
    plane, sums, matrices, noise, *sends = pl.pallas_call(
        first_kernel,
        out_shape=[plane_shape, sums_shape, matrices_shape, whole, *send_rows(EXTRA)],
        in_specs=[VMEM] * 8,
        out_specs=[VMEM] * 8,
        scratch_shapes=scalars,
        input_output_aliases={1: 0, 2: 1, 3: 2, 4: 3},
        compiler_params=PARAMS,
        cost_estimate=cost(8, DEPTH),
        name="level_0",
    )(table, plane, sums, matrices, noise, *halo[2:], own)
    for section in range(1, LEVELS):
        final = section == LEVELS - 1
        halo = exchange(sends)
        if section == 1:
            extras = halo
        plane, sums, matrices, noise, items = pl.pallas_call(
            functools.partial(settled_kernel, section),
            out_shape=[plane_shape, sums_shape, matrices_shape, whole, table_shape],
            in_specs=[SMEM] * 2 + [VMEM] * 4 + [HBM] * 3,
            out_specs=[VMEM] * 4 + [SMEM],
            scratch_shapes=[
                pltpu.SMEM((8 * tile,), jnp.int32),
                factors,
                pltpu.SemaphoreType.DMA((3, tile)),
            ],
            input_output_aliases={2: 0, 3: 1, 4: 2, 5: 3},
            compiler_params=PARAMS,
            cost_estimate=cost(8, DEPTH),
            name=f"settled_{section}",
        )(codes, table, plane, sums, matrices, noise, *sources)
        plane = take_rows(PLANE, plane, halo, f"rows_{section}")
        if final:
            far, near = pl.pallas_call(
                forward_kernel,
                out_shape=[rows_of(2 * ROWS)] * 2,
                in_specs=[VMEM],
                out_specs=[VMEM] * 2,
                compiler_params=PARAMS,
                cost_estimate=cost(0, 0),
                name="forward",
            )(plane)
            far, near = swap(far, None, "out"), swap(near, None, "in")
        plane, sums, *sends = pl.pallas_call(
            functools.partial(main_kernel, section),
            out_shape=[plane_shape, sums_shape] + ([whole] if final else send_rows(0)),
            in_specs=[VMEM] * 11,
            out_specs=[VMEM] * 2 + ([HBM] if final else [VMEM] * 4),
            scratch_shapes=[pltpu.SemaphoreType.DMA((4,))] * final + scalars,
            input_output_aliases={1: 0, 2: 1},
            compiler_params=PARAMS,
            cost_estimate=cost(16, LANES),
            name=f"level_{section}",
        )(items, plane, sums, matrices, own, *halo[2:], *extras)
    _, result = pl.pallas_call(
        corner_kernel,
        out_shape=[plane_shape, whole],
        in_specs=[VMEM] * 5 + [HBM],
        out_specs=[VMEM, HBM],
        scratch_shapes=[pltpu.SemaphoreType.DMA((4,))],
        input_output_aliases={0: 0, 5: 1},
        compiler_params=PARAMS,
        cost_estimate=cost(4, LANES),
        name="last_corners",
    )(plane, own, sums, far, near, sends[0])
    return result.reshape(earlier.shape)


def solution(mesh):
    placed = (
        P("tx", "ty", None, None),
        P("tx", "ty", None, None),
        P("tx", "ty", None, None),
        P("tx", "ty", None, None),
        P("tx", "ty"),
        P("tx", "ty", None),
    )
    return jax.shard_map(
        local, mesh=mesh, in_specs=placed, out_specs=P("tx", "ty", None, None), check_vma=False
    )
```

```python
import functools

import jax
import jax.numpy as jnp
from jax import lax
from jax.experimental import pallas as pl
from jax.experimental.pallas import tpu as pltpu
from jax.sharding import PartitionSpec as P

LEVELS = 4
BOTH = ("tx", "ty")
SIDE = 4
GRID = 6
PLANE = GRID * GRID
BLANK = 2 * PLANE
ROWS = 256
LANES = 128
MARK = 16
EXTRA = 2 * (LANES + MARK)
DEPTH = 9 * LANES
LEVEL, SLOT, ITEM, CELLS, COUNT, CHOSEN, TABLE = 0, 16, 144, 216, 236, 237, 238
GROUP = 4
CORNERS = ((0, 0), (0, 3), (3, 0), (3, 3))
VMEM = pl.BlockSpec(memory_space=pltpu.VMEM)
SMEM = pl.BlockSpec(memory_space=pltpu.SMEM)
HBM = pl.BlockSpec(memory_space=pltpu.HBM)
PARAMS = pltpu.CompilerParams(vmem_limit_bytes=8 * 1024 * 1024)


def partner(at, size, kind):
    if kind == "in":
        return at ^ 1
    if kind == "out":
        return (at + 1) % size if at % 2 else (at - 1) % size
    return at


def swap(value, along_x, along_y):
    size_x, size_y = lax.axis_size("tx"), lax.axis_size("ty")
    pairs = [
        (x * size_y + y, partner(x, size_x, along_x) * size_y + partner(y, size_y, along_y))
        for x in range(size_x)
        for y in range(size_y)
    ]
    return lax.ppermute(value, BOTH, pairs)


def exchange(sends):
    tx_out, tx_in, ty_out, ty_in = sends
    return swap(tx_out, "out", None), swap(tx_in, "in", None), swap(ty_out, None, "out"), swap(ty_in, None, "in")


def edges():
    odd_x = lax.rem(lax.axis_index("tx"), 2)
    odd_y = lax.rem(lax.axis_index("ty"), 2)
    return 3 * odd_x, 3 - 3 * odd_x, 3 * odd_y, 3 - 3 * odd_y


def beyond(edge):
    return (edge // 3) * 5


def own_slot(x, y):
    return PLANE + (x + 1) * GRID + y + 1


def piece(ref, at):
    return ref[at * ROWS : (at + 1) * ROWS]


def forward_kernel(plane, far, near):
    out_x, in_x, out_y, in_y = edges()
    for i, side in enumerate((out_x, in_x)):
        far[i * ROWS : (i + 1) * ROWS] = plane[PLANE + beyond(side) * GRID + out_y + 1]
        near[i * ROWS : (i + 1) * ROWS] = plane[PLANE + beyond(side) * GRID + in_y + 1]


def pack_kernel(earlier, tx_out, tx_in, ty_out, ty_in, sems):
    out_x, in_x, out_y, in_y = edges()
    copies = [
        pltpu.make_async_copy(earlier.at[out_x], tx_out, sems.at[0]),
        pltpu.make_async_copy(earlier.at[in_x], tx_in, sems.at[1]),
        pltpu.make_async_copy(earlier.at[:, out_y], ty_out, sems.at[2]),
        pltpu.make_async_copy(earlier.at[:, in_y], ty_in, sems.at[3]),
    ]
    for copy in copies:
        copy.start()
    for copy in copies:
        copy.wait()


def late_code(levels, codes, x, y):
    code = 2 * x + 2 * y // 3 + jnp.where(levels[x, y] > 0, 9, 0)
    found = jnp.int32(-1)
    for k in range(8):
        found = jnp.where(codes[x, y, k] == code, k, found)
    return found


def fill_slots(cell, level, codes, every, settled):
    x, y = cell // SIDE, cell % SIDE
    for k in range(8):
        code = codes[x, y, k]
        old = code >= 9
        offset = jnp.where(old, code - 9, code)
        down = (offset >= 3).astype(jnp.int32) + (offset >= 6).astype(jnp.int32)
        row, column = x + down, y + offset - 3 * down
        slot = row * GRID + column + jnp.where(old, PLANE, 0)
        edge_row, edge_column = (row == 0) | (row == 5), (column == 0) | (column == 5)
        outer = edge_row & edge_column
        waits = outer & (old == (level > 0))
        every[SLOT + 8 * cell + k] = jnp.where(waits, BLANK, slot)
        if settled is not None:
            own_corner = ((row == 1) | (row == 4)) & ((column == 1) | (column == 4))
            open_ = (old & (edge_row | edge_column | own_corner)) | outer
            settled[8 * cell + k] = jnp.where(open_, BLANK, slot)


def cells_of(section, table, body):
    def one_cell(cell, carry):
        @pl.when(table[LEVEL + cell] == section)
        def _():
            body(cell)

        return carry

    lax.fori_loop(0, SIDE * SIDE, one_cell, 0)


def choose(section, levels, table):
    def one_cell(cell, at):
        table[CELLS + at] = cell
        return at + (levels[LEVEL + cell] == section).astype(jnp.int32)

    table[CHOSEN] = lax.fori_loop(0, SIDE * SIDE, one_cell, jnp.int32(0))


def each_cell(table, body):
    def one_cell(at, carry):
        body(table[CELLS + at])
        return carry

    lax.fori_loop(0, table[CHOSEN], one_cell, 0)


def each_group(table, body):
    count = table[CHOSEN]

    def one_group(group, carry):
        first = group * GROUP
        body([table[CELLS + jnp.minimum(first + i, count - 1)] for i in range(GROUP)], count - first)
        return carry

    lax.fori_loop(0, (count + GROUP - 1) // GROUP, one_group, 0)


def cell_copies(cell, sources, targets, sems):
    innovation, conditioner, chol_factor = sources
    noise, matrices, factors = targets
    return (
        pltpu.make_async_copy(chol_factor.at[cell], factors.at[cell], sems.at[0, cell]),
        pltpu.make_async_copy(innovation.at[cell], noise.at[cell], sems.at[1, cell]),
        pltpu.make_async_copy(conditioner.at[cell], matrices.at[cell, pl.ds(0, 8 * LANES)], sems.at[2, cell]),
    )


def start_cell(cell, sources, targets, sems):
    for copy in cell_copies(cell, sources, targets, sems):
        copy.start()


def finish_cell(cell, sources, targets, sems):
    _, matrices, factors = targets
    copies = cell_copies(cell, sources, targets, sems)
    copies[0].wait()
    rows = lax.broadcasted_iota(jnp.int32, (LANES, LANES), 0)
    columns = lax.broadcasted_iota(jnp.int32, (LANES, LANES), 1)
    upper = jnp.where(rows <= columns, factors[cell].astype(jnp.float32), 0.0)
    matrices[cell, 8 * LANES :] = upper.astype(jnp.bfloat16)
    copies[1].wait()
    copies[2].wait()


def load_kernel(
    block_level, neighbours, earlier, innovation, conditioner, chol_factor, plane, matrices, noise, sums, table, codes, extras, *rest
):
    levels, factors, sems, more_sems = rest
    scalars = [
        pltpu.make_async_copy(block_level, levels, more_sems.at[12]),
        pltpu.make_async_copy(neighbours, codes, more_sems.at[13]),
    ]
    copies = [
        pltpu.make_async_copy(
            earlier.at[pl.ds(x * SIDE, SIDE)], plane.at[pl.ds((x + 1) * GRID + 1, SIDE)], more_sems.at[x]
        )
        for x in range(SIDE)
    ]
    for copy in scalars + copies:
        copy.start()

    def clear(at, carry):
        plane[at] = jnp.zeros(plane.shape[1:], plane.dtype)
        return carry

    lax.fori_loop(PLANE, BLANK + 1, clear, 0)
    for copy in scalars:
        copy.wait()
    for cell in range(SIDE * SIDE):
        table[LEVEL + cell] = levels[cell // SIDE, cell % SIDE]
    sources, targets = (innovation, conditioner, chol_factor), (noise, matrices, factors)
    choose(0, table, table)
    each_cell(table, lambda cell: start_cell(cell, sources, targets, sems))
    out_x, _, out_y, _ = edges()
    for at, (x, y) in enumerate(CORNERS):
        late = late_code(levels, codes, x, y)
        mark = jnp.full((MARK, LANES), jnp.where(late >= 0, levels[x, y], -1).astype(jnp.float32)).astype(jnp.bfloat16)
        start = pl.multiple_of(LANES * jnp.maximum(late, 0), LANES)
        matrix = conditioner.at[SIDE * x + y, pl.ds(start, LANES)]
        for way, (side, place) in enumerate(((jnp.where(out_x == x, 0, 1), y // 3), (jnp.where(out_y == y, 2, 3), x // 3))):
            copy = pltpu.make_async_copy(
                matrix, extras.at[side, pl.ds(place * LANES, LANES)], more_sems.at[4 + 2 * at + way]
            )
            copy.start()
            copies.append(copy)
            extras[side, 2 * LANES + place * MARK : 2 * LANES + (place + 1) * MARK] = mark
    each_cell(table, lambda cell: fill_slots(cell, 0, codes, table, None))
    each_cell(table, lambda cell: finish_cell(cell, sources, targets, sems))
    for copy in copies:
        copy.wait()


def read_mark(extra, place):
    return jnp.max(extra[2 * LANES + place * MARK : 2 * LANES + (place + 1) * MARK].astype(jnp.float32))


def complete_halo(recent, plane, extras):
    out_x, in_x, out_y, in_y = edges()
    source = PLANE if recent else 0
    todo = []
    for side in (out_x, in_x):
        for place in (0, 1):
            todo.append((beyond(side) * GRID + 1 + 3 * place, (side + 1) * GRID + 5 * place))
    for side in (out_y, in_y):
        for place in (0, 1):
            todo.append(((1 + 3 * place) * GRID + beyond(side), 5 * place * GRID + side + 1))
    marks = [read_mark(extra, place) for extra in extras for place in (0, 1)]
    for at, (cell, other) in enumerate(todo):

        @pl.when(marks[at] == recent)
        def _(cell=cell, other=other, extra=extras[at // 2], place=at % 2):
            product = jnp.dot(
                plane[source + other], extra[place * LANES : (place + 1) * LANES], preferred_element_type=jnp.float32
            )
            plane[PLANE + cell] = (plane[PLANE + cell].astype(jnp.float32) + product).astype(jnp.bfloat16)


def finish_corners(recent, extras, plane, sums, far, near):
    out_x, _, out_y, _ = edges()
    facing = [extras.at[jnp.where(out_y == y, 2, 3)] for _, y in CORNERS]
    places = [x // 3 for x, _ in CORNERS]
    marks = [read_mark(extra, place) for extra, place in zip(facing, places, strict=True)]
    for (x, y), extra, place, mark in zip(CORNERS, facing, places, marks, strict=True):

        @pl.when(mark == recent)
        def _(x=x, y=y, extra=extra, place=place):
            side = jnp.where(out_x == x, 0, 1)
            block = jnp.where(out_y == y, far(side), near(side))
            matrix = extra[place * LANES : (place + 1) * LANES]
            summed = sums[SIDE * x + y] + jnp.dot(block, matrix, preferred_element_type=jnp.float32)
            plane[own_slot(x, y)] = summed.astype(jnp.bfloat16)

    return [mark == recent for mark in marks]


def block_of(ref, first):
    return lambda at: ref[pl.ds(pl.multiple_of((first + at) * ROWS, ROWS), ROWS)]


def store_corners(plane, far, near):
    out_x, _, out_y, _ = edges()
    for x, y in CORNERS:
        side = jnp.where(out_x == x, 0, 1)
        plane[beyond(x) * GRID + beyond(y)] = jnp.where(out_y == y, far(side), near(side))


def gather_product(cell, slots, first, plane, matrices, noise):
    parts = [plane[slots[first + 8 * cell + k]] for k in range(8)] + [noise[cell]]
    return jnp.dot(jnp.concatenate(parts, axis=1), matrices[cell], preferred_element_type=jnp.float32)


def settled_kernel(section, codes, table_in, plane_in, sums_in, matrices_in, noise_in, *rest):
    sources, rest = rest[:3], rest[3:]
    plane, sums, matrices, noise, table, settled, factors, sems = rest
    targets = noise, matrices, factors
    choose(section, table_in, table)
    if section == 1:
        each_cell(table, lambda cell: start_cell(cell, sources, targets, sems))
    if section + 1 < LEVELS:
        cells_of(section + 1, table_in, lambda cell: start_cell(cell, sources, targets, sems))

    def one_cell(at, found):
        cell = table[CELLS + at]
        fill_slots(cell, section, codes, table, settled)
        for k in range(8):
            table[ITEM + found] = 8 * cell + k
            found += (table[SLOT + 8 * cell + k] != settled[8 * cell + k]).astype(jnp.int32)
        return found

    table[COUNT] = lax.fori_loop(0, table[CHOSEN], one_cell, jnp.int32(0))

    def products(cells, fresh):
        if section == 1:
            for i, cell in enumerate(cells):

                @pl.when(i < fresh)
                def _(cell=cell):
                    finish_cell(cell, sources, targets, sems)

        results = [gather_product(cell, settled, 0, plane, matrices, noise) for cell in cells]
        for cell, summed in zip(cells, results, strict=True):
            sums[cell] = summed

    each_group(table, products)
    if section + 1 < LEVELS:
        cells_of(section + 1, table_in, lambda cell: finish_cell(cell, sources, targets, sems))


def rows_kernel(base, outward, plane_in, halo, plane):
    out_x, in_x, _, _ = edges()
    row = beyond(out_x if outward else in_x)
    for i in range(SIDE):
        plane[base + row * GRID + i + 1] = piece(halo, i)


def take_rows(base, plane, halo, name):
    for outward, part, products in ((True, halo[0], 16), (False, halo[1], 64)):
        plane = pl.pallas_call(
            functools.partial(rows_kernel, base, outward),
            out_shape=jax.ShapeDtypeStruct(plane.shape, plane.dtype),
            in_specs=[VMEM] * 2,
            out_specs=VMEM,
            input_output_aliases={0: 0},
            compiler_params=PARAMS,
            cost_estimate=cost(products, DEPTH),
            name=f"{name}_{'out' if outward else 'in'}",
        )(plane, part)
    return plane


def store_columns(base, plane, ty_out, ty_in):
    _, _, out_y, in_y = edges()
    for i in range(SIDE):
        plane[base + (i + 1) * GRID + beyond(out_y)] = piece(ty_out, i)
        plane[base + (i + 1) * GRID + beyond(in_y)] = piece(ty_in, i)


def pack_sends(base, plane, sends):
    tx_out, tx_in, ty_out, ty_in = sends
    out_x, in_x, out_y, in_y = edges()
    for i in range(SIDE):
        rows = pl.ds(i * ROWS, ROWS)
        tx_out[rows] = plane[own_slot(out_x, i)]
        tx_in[rows] = plane[own_slot(in_x, i)]
        ty_out[rows] = plane[own_slot(i, out_y)]
        ty_in[rows] = plane[own_slot(i, in_y)]
    for i, side in enumerate((out_x, in_x)):
        rows = pl.ds((SIDE + i) * ROWS, ROWS)
        ty_out[rows] = plane[base + beyond(side) * GRID + out_y + 1]
        ty_in[rows] = plane[base + beyond(side) * GRID + in_y + 1]


def fetch(table, scalars, sem):
    copy = pltpu.make_async_copy(table, scalars, sem)
    copy.start()
    return copy.wait


def first_kernel(table_in, plane_in, sums_in, matrices_in, noise_in, *rest):
    halo, extras, (plane, sums, matrices, noise, *sends) = rest[:2], rest[2], rest[3:-2]
    table, sem = rest[-2:]
    wait = fetch(table_in, table, sem)
    store_columns(0, plane, *halo)
    for at, ref in enumerate(sends):
        ref[ref.shape[0] - EXTRA :] = extras[at]
    wait()

    def products(cells, fresh):
        results = [gather_product(cell, table, SLOT, plane, matrices, noise) for cell in cells]
        for cell, summed in zip(cells, results, strict=True):
            sums[cell] = summed
            plane[own_slot(cell // SIDE, cell % SIDE)] = summed.astype(jnp.bfloat16)

    each_group(table, products)
    pack_sends(0, plane, sends)


def main_kernel(section, table_in, plane_in, sums_in, matrices, own, ty_out, ty_in, *rest):
    extras, rest = rest[:4], rest[4:]
    plane, sums, *rest, table, sem = rest
    wait = fetch(table_in, table, sem)
    extras = [ref.at[pl.ds(ref.shape[0] - EXTRA, EXTRA)] for ref in extras]
    corners = block_of(ty_out, SIDE), block_of(ty_in, SIDE)
    store_columns(PLANE, plane, ty_out, ty_in)
    if section == 1:
        store_corners(plane, *corners)
    complete_halo(section - 1, plane, extras)
    finish_corners(section - 1, own, plane, sums, *corners)
    wait()
    count = table[COUNT]

    def one_group(group, carry):
        products = []
        for i in range(GROUP):
            item = table[ITEM + jnp.minimum(group * GROUP + i, count - 1)]
            slot = jnp.where(group * GROUP + i < count, table[SLOT + item], BLANK)
            matrix = matrices[item // 8, pl.ds(pl.multiple_of((item % 8) * LANES, LANES), LANES)]
            products.append((item // 8, jnp.dot(plane[slot], matrix, preferred_element_type=jnp.float32)))
        for cell, product in products:
            sums[cell] += product
        return carry

    lax.fori_loop(0, (count + GROUP - 1) // GROUP, one_group, 0)

    def one_cell(cell):
        plane[own_slot(cell // SIDE, cell % SIDE)] = sums[cell].astype(jnp.bfloat16)

    each_cell(table, one_cell)
    if section < LEVELS - 1:
        pack_sends(PLANE, plane, rest)
    else:
        result, sems = rest
        copies = [
            pltpu.make_async_copy(
                plane.at[pl.ds(own_slot(x, 0), SIDE)], result.at[pl.ds(x * SIDE, SIDE)], sems.at[x]
            )
            for x in range(SIDE)
        ]
        for copy in copies:
            copy.start()
        for copy in copies:
            copy.wait()


def corner_kernel(plane_in, own, sums, far, near, result_in, plane, result, sems):
    changed = finish_corners(LEVELS - 1, own, plane, sums, block_of(far, 0), block_of(near, 0))
    copies = [
        pltpu.make_async_copy(plane.at[own_slot(x, y)], result.at[SIDE * x + y], sems.at[at])
        for at, (x, y) in enumerate(CORNERS)
    ]
    for copy, needed in zip(copies, changed, strict=True):
        pl.when(needed)(copy.start)
    for copy, needed in zip(copies, changed, strict=True):
        pl.when(needed)(copy.wait)


def cost(products, depth):
    flops = products * 2 * ROWS * depth * LANES
    return pl.CostEstimate(flops=flops, bytes_accessed=4 << 20, transcendentals=0)


def rows_of(rows):
    return jax.ShapeDtypeStruct((rows, LANES), jnp.bfloat16)


def local(earlier, innovation, conditioner, chol_factor, block_level, neighbours):
    block = earlier.shape[2:]
    tile = SIDE * SIDE
    keep = lambda value: pltpu.with_memory_space_constraint(value, pltpu.HBM)
    flat = lambda value: keep(value.reshape(tile, *value.shape[2:]))
    edge = jax.ShapeDtypeStruct((SIDE, *block), jnp.bfloat16)
    plane_shape = jax.ShapeDtypeStruct((BLANK + 1, *block), jnp.bfloat16)
    sums_shape = jax.ShapeDtypeStruct((tile, *block), jnp.float32)
    whole = jax.ShapeDtypeStruct((tile, *block), jnp.bfloat16)
    matrices_shape = jax.ShapeDtypeStruct((tile, DEPTH, LANES), jnp.bfloat16)
    table_shape = jax.ShapeDtypeStruct((TABLE,), jnp.int32)
    scalars = [pltpu.SMEM((TABLE,), jnp.int32), pltpu.SemaphoreType.DMA]
    factors = pltpu.VMEM((tile, *chol_factor.shape[2:]), jnp.bfloat16)
    sends = pl.pallas_call(
        pack_kernel,
        out_shape=[edge] * 4,
        in_specs=[HBM],
        out_specs=[VMEM] * 4,
        scratch_shapes=[pltpu.SemaphoreType.DMA((4,))],
        compiler_params=PARAMS,
        name="pack",
    )(keep(earlier))
    sends = [send.reshape(SIDE * ROWS, LANES) for send in sends]
    sources = flat(innovation), flat(conditioner), flat(chol_factor)
    plane, matrices, noise, sums, table, codes, own = pl.pallas_call(
        load_kernel,
        out_shape=[
            plane_shape,
            matrices_shape,
            whole,
            sums_shape,
            table_shape,
            jax.ShapeDtypeStruct(neighbours.shape, jnp.int32),
            jax.ShapeDtypeStruct((4, EXTRA, LANES), jnp.bfloat16),
        ],
        in_specs=[HBM] * 6,
        out_specs=[VMEM] * 4 + [SMEM] * 2 + [VMEM],
        scratch_shapes=[
            pltpu.SMEM(block_level.shape, jnp.int32),
            factors,
            pltpu.SemaphoreType.DMA((3, tile)),
            pltpu.SemaphoreType.DMA((14,)),
        ],
        compiler_params=PARAMS,
        cost_estimate=pl.CostEstimate(flops=0, bytes_accessed=10 << 20, transcendentals=0),
        name="load",
    )(keep(block_level), keep(neighbours), flat(earlier), *sources)
    halo = exchange(sends)
    plane = take_rows(0, plane, halo, "rows_0")
    send_rows = lambda extra: [rows_of(4 * ROWS + extra)] * 2 + [rows_of(6 * ROWS + extra)] * 2
    plane, sums, matrices, noise, *sends = pl.pallas_call(
        first_kernel,
        out_shape=[plane_shape, sums_shape, matrices_shape, whole, *send_rows(EXTRA)],
        in_specs=[VMEM] * 8,
        out_specs=[VMEM] * 8,
        scratch_shapes=scalars,
        input_output_aliases={1: 0, 2: 1, 3: 2, 4: 3},
        compiler_params=PARAMS,
        cost_estimate=cost(8, DEPTH),
        name="level_0",
    )(table, plane, sums, matrices, noise, *halo[2:], own)
    for section in range(1, LEVELS):
        final = section == LEVELS - 1
        halo = exchange(sends)
        if section == 1:
            extras = halo
        plane, sums, matrices, noise, items = pl.pallas_call(
            functools.partial(settled_kernel, section),
            out_shape=[plane_shape, sums_shape, matrices_shape, whole, table_shape],
            in_specs=[SMEM] * 2 + [VMEM] * 4 + [HBM] * 3,
            out_specs=[VMEM] * 4 + [SMEM],
            scratch_shapes=[
                pltpu.SMEM((8 * tile,), jnp.int32),
                factors,
                pltpu.SemaphoreType.DMA((3, tile)),
            ],
            input_output_aliases={2: 0, 3: 1, 4: 2, 5: 3},
            compiler_params=PARAMS,
            cost_estimate=cost(8, DEPTH),
            name=f"settled_{section}",
        )(codes, table, plane, sums, matrices, noise, *sources)
        plane = take_rows(PLANE, plane, halo, f"rows_{section}")
        if final:
            far, near = pl.pallas_call(
                forward_kernel,
                out_shape=[rows_of(2 * ROWS)] * 2,
                in_specs=[VMEM],
                out_specs=[VMEM] * 2,
                compiler_params=PARAMS,
                cost_estimate=cost(0, 0),
                name="forward",
            )(plane)
            far, near = swap(far, None, "out"), swap(near, None, "in")
        plane, sums, *sends = pl.pallas_call(
            functools.partial(main_kernel, section),
            out_shape=[plane_shape, sums_shape] + ([whole] if final else send_rows(0)),
            in_specs=[VMEM] * 11,
            out_specs=[VMEM] * 2 + ([HBM] if final else [VMEM] * 4),
            scratch_shapes=[pltpu.SemaphoreType.DMA((4,))] * final + scalars,
            input_output_aliases={1: 0, 2: 1},
            compiler_params=PARAMS,
            cost_estimate=cost(16, LANES),
            name=f"level_{section}",
        )(items, plane, sums, matrices, own, *halo[2:], *extras)
    _, result = pl.pallas_call(
        corner_kernel,
        out_shape=[plane_shape, whole],
        in_specs=[VMEM] * 5 + [HBM],
        out_specs=[VMEM, HBM],
        scratch_shapes=[pltpu.SemaphoreType.DMA((4,))],
        input_output_aliases={0: 0, 5: 1},
        compiler_params=PARAMS,
        cost_estimate=cost(4, LANES),
        name="last_corners",
    )(plane, own, sums, far, near, sends[0])
    return result.reshape(earlier.shape)


def solution(mesh):
    placed = (
        P("tx", "ty", None, None),
        P("tx", "ty", None, None),
        P("tx", "ty", None, None),
        P("tx", "ty", None, None),
        P("tx", "ty"),
        P("tx", "ty", None),
    )
    return jax.shard_map(
        local, mesh=mesh, in_specs=placed, out_specs=P("tx", "ty", None, None), check_vma=False
    )
```

```python
import functools

import jax
import jax.numpy as jnp
from jax import lax
from jax.experimental import pallas as pl
from jax.experimental.pallas import tpu as pltpu
from jax.sharding import PartitionSpec as P

LEVELS = 4
BOTH = ("tx", "ty")
SIDE = 4
GRID = 6
PLANE = GRID * GRID
BLANK = 2 * PLANE
ROWS = 256
LANES = 128
MARK = 16
EXTRA = 2 * (LANES + MARK)
DEPTH = 9 * LANES
LEVEL, SLOT, ITEM, CELLS, COUNT, CHOSEN, TABLE = 0, 16, 144, 216, 236, 237, 238
GROUP = 4
CORNERS = ((0, 0), (0, 3), (3, 0), (3, 3))
VMEM = pl.BlockSpec(memory_space=pltpu.VMEM)
SMEM = pl.BlockSpec(memory_space=pltpu.SMEM)
HBM = pl.BlockSpec(memory_space=pltpu.HBM)
PARAMS = pltpu.CompilerParams(vmem_limit_bytes=8 * 1024 * 1024)


def partner(at, size, kind):
    if kind == "in":
        return at ^ 1
    if kind == "out":
        return (at + 1) % size if at % 2 else (at - 1) % size
    return at


def swap(value, along_x, along_y):
    size_x, size_y = lax.axis_size("tx"), lax.axis_size("ty")
    pairs = [
        (x * size_y + y, partner(x, size_x, along_x) * size_y + partner(y, size_y, along_y))
        for x in range(size_x)
        for y in range(size_y)
    ]
    return lax.ppermute(value, BOTH, pairs)


def exchange(sends):
    tx_out, tx_in, ty_out, ty_in = sends
    return swap(tx_out, "out", None), swap(tx_in, "in", None), swap(ty_out, None, "out"), swap(ty_in, None, "in")


def edges():
    odd_x = lax.rem(lax.axis_index("tx"), 2)
    odd_y = lax.rem(lax.axis_index("ty"), 2)
    return 3 * odd_x, 3 - 3 * odd_x, 3 * odd_y, 3 - 3 * odd_y


def beyond(edge):
    return (edge // 3) * 5


def own_slot(x, y):
    return PLANE + (x + 1) * GRID + y + 1


def piece(ref, at):
    return ref[at * ROWS : (at + 1) * ROWS]


def forward_kernel(plane, far, near):
    out_x, in_x, out_y, in_y = edges()
    for i, side in enumerate((out_x, in_x)):
        far[i * ROWS : (i + 1) * ROWS] = plane[PLANE + beyond(side) * GRID + out_y + 1]
        near[i * ROWS : (i + 1) * ROWS] = plane[PLANE + beyond(side) * GRID + in_y + 1]


def pack_kernel(earlier, tx_out, tx_in, ty_out, ty_in, sems):
    out_x, in_x, out_y, in_y = edges()
    copies = [
        pltpu.make_async_copy(earlier.at[out_x], tx_out, sems.at[0]),
        pltpu.make_async_copy(earlier.at[in_x], tx_in, sems.at[1]),
        pltpu.make_async_copy(earlier.at[:, out_y], ty_out, sems.at[2]),
        pltpu.make_async_copy(earlier.at[:, in_y], ty_in, sems.at[3]),
    ]
    for copy in copies:
        copy.start()
    for copy in copies:
        copy.wait()


def late_code(levels, codes, x, y):
    code = 2 * x + 2 * y // 3 + jnp.where(levels[x, y] > 0, 9, 0)
    found = jnp.int32(-1)
    for k in range(8):
        found = jnp.where(codes[x, y, k] == code, k, found)
    return found


def fill_slots(cell, level, codes, every, settled):
    x, y = cell // SIDE, cell % SIDE
    for k in range(8):
        code = codes[x, y, k]
        old = code >= 9
        offset = jnp.where(old, code - 9, code)
        down = (offset >= 3).astype(jnp.int32) + (offset >= 6).astype(jnp.int32)
        row, column = x + down, y + offset - 3 * down
        slot = row * GRID + column + jnp.where(old, PLANE, 0)
        edge_row, edge_column = (row == 0) | (row == 5), (column == 0) | (column == 5)
        outer = edge_row & edge_column
        waits = outer & (old == (level > 0))
        every[SLOT + 8 * cell + k] = jnp.where(waits, BLANK, slot)
        if settled is not None:
            own_corner = ((row == 1) | (row == 4)) & ((column == 1) | (column == 4))
            open_ = (old & (edge_row | edge_column | own_corner)) | outer
            settled[8 * cell + k] = jnp.where(open_, BLANK, slot)


def choose(section, levels, table):
    def one_cell(cell, at):
        table[CELLS + at] = cell
        return at + (levels[LEVEL + cell] == section).astype(jnp.int32)

    table[CHOSEN] = lax.fori_loop(0, SIDE * SIDE, one_cell, jnp.int32(0))


def each_cell(table, body):
    def one_cell(at, carry):
        body(table[CELLS + at])
        return carry

    lax.fori_loop(0, table[CHOSEN], one_cell, 0)


def each_pair(table, body):
    count = table[CHOSEN]

    def one_pair(pair, carry):
        second = jnp.minimum(2 * pair + 1, count - 1)
        body(table[CELLS + 2 * pair], table[CELLS + second], 2 * pair + 1 < count)
        return carry

    lax.fori_loop(0, (count + 1) // 2, one_pair, 0)


def cell_copies(cell, sources, targets, sems):
    innovation, conditioner, chol_factor = sources
    noise, matrices, factors = targets
    return (
        pltpu.make_async_copy(chol_factor.at[cell], factors.at[cell], sems.at[0, cell]),
        pltpu.make_async_copy(innovation.at[cell], noise.at[cell], sems.at[1, cell]),
        pltpu.make_async_copy(conditioner.at[cell], matrices.at[cell, pl.ds(0, 8 * LANES)], sems.at[2, cell]),
    )


def start_cell(cell, sources, targets, sems):
    for copy in cell_copies(cell, sources, targets, sems):
        copy.start()


def finish_cell(cell, sources, targets, sems):
    _, matrices, factors = targets
    copies = cell_copies(cell, sources, targets, sems)
    copies[0].wait()
    rows = lax.broadcasted_iota(jnp.int32, (LANES, LANES), 0)
    columns = lax.broadcasted_iota(jnp.int32, (LANES, LANES), 1)
    upper = jnp.where(rows <= columns, factors[cell].astype(jnp.float32), 0.0)
    matrices[cell, 8 * LANES :] = upper.astype(jnp.bfloat16)
    copies[1].wait()
    copies[2].wait()


def load_kernel(
    block_level, neighbours, earlier, innovation, conditioner, chol_factor, plane, matrices, noise, sums, table, codes, extras, *rest
):
    levels, factors, sems, more_sems = rest
    scalars = [
        pltpu.make_async_copy(block_level, levels, more_sems.at[12]),
        pltpu.make_async_copy(neighbours, codes, more_sems.at[13]),
    ]
    copies = [
        pltpu.make_async_copy(
            earlier.at[pl.ds(x * SIDE, SIDE)], plane.at[pl.ds((x + 1) * GRID + 1, SIDE)], more_sems.at[x]
        )
        for x in range(SIDE)
    ]
    for copy in scalars + copies:
        copy.start()

    plane[BLANK] = jnp.zeros(plane.shape[1:], plane.dtype)
    for copy in scalars:
        copy.wait()
    for cell in range(SIDE * SIDE):
        table[LEVEL + cell] = levels[cell // SIDE, cell % SIDE]
    sources, targets = (innovation, conditioner, chol_factor), (noise, matrices, factors)
    choose(0, table, table)
    each_cell(table, lambda cell: start_cell(cell, sources, targets, sems))
    out_x, _, out_y, _ = edges()
    for at, (x, y) in enumerate(CORNERS):
        late = late_code(levels, codes, x, y)
        mark = jnp.full((MARK, LANES), jnp.where(late >= 0, levels[x, y], -1).astype(jnp.float32)).astype(jnp.bfloat16)
        start = pl.multiple_of(LANES * jnp.maximum(late, 0), LANES)
        matrix = conditioner.at[SIDE * x + y, pl.ds(start, LANES)]
        for way, (side, place) in enumerate(((jnp.where(out_x == x, 0, 1), y // 3), (jnp.where(out_y == y, 2, 3), x // 3))):
            copy = pltpu.make_async_copy(
                matrix, extras.at[side, pl.ds(place * LANES, LANES)], more_sems.at[4 + 2 * at + way]
            )
            copy.start()
            copies.append(copy)
            extras[side, 2 * LANES + place * MARK : 2 * LANES + (place + 1) * MARK] = mark
    each_cell(table, lambda cell: fill_slots(cell, 0, codes, table, None))
    each_cell(table, lambda cell: finish_cell(cell, sources, targets, sems))
    for copy in copies:
        copy.wait()


def read_mark(extra, place):
    return jnp.max(extra[2 * LANES + place * MARK : 2 * LANES + (place + 1) * MARK].astype(jnp.float32))


def complete_halo(recent, plane, extras):
    out_x, in_x, out_y, in_y = edges()
    source = PLANE if recent else 0
    todo = []
    for side in (out_x, in_x):
        for place in (0, 1):
            todo.append((beyond(side) * GRID + 1 + 3 * place, (side + 1) * GRID + 5 * place))
    for side in (out_y, in_y):
        for place in (0, 1):
            todo.append(((1 + 3 * place) * GRID + beyond(side), 5 * place * GRID + side + 1))
    marks = [read_mark(extra, place) for extra in extras for place in (0, 1)]
    for at, (cell, other) in enumerate(todo):

        @pl.when(marks[at] == recent)
        def _(cell=cell, other=other, extra=extras[at // 2], place=at % 2):
            product = jnp.dot(
                plane[source + other], extra[place * LANES : (place + 1) * LANES], preferred_element_type=jnp.float32
            )
            plane[PLANE + cell] = (plane[PLANE + cell].astype(jnp.float32) + product).astype(jnp.bfloat16)


def finish_corners(recent, extras, plane, sums, far, near):
    out_x, _, out_y, _ = edges()
    facing = [extras.at[jnp.where(out_y == y, 2, 3)] for _, y in CORNERS]
    places = [x // 3 for x, _ in CORNERS]
    marks = [read_mark(extra, place) for extra, place in zip(facing, places, strict=True)]
    for (x, y), extra, place, mark in zip(CORNERS, facing, places, marks, strict=True):

        @pl.when(mark == recent)
        def _(x=x, y=y, extra=extra, place=place):
            side = jnp.where(out_x == x, 0, 1)
            block = jnp.where(out_y == y, far(side), near(side))
            matrix = extra[place * LANES : (place + 1) * LANES]
            summed = sums[SIDE * x + y] + jnp.dot(block, matrix, preferred_element_type=jnp.float32)
            plane[own_slot(x, y)] = summed.astype(jnp.bfloat16)

    return [mark == recent for mark in marks]


def block_of(ref, first):
    return lambda at: ref[pl.ds(pl.multiple_of((first + at) * ROWS, ROWS), ROWS)]


def store_corners(plane, far, near):
    out_x, _, out_y, _ = edges()
    for x, y in CORNERS:
        side = jnp.where(out_x == x, 0, 1)
        plane[beyond(x) * GRID + beyond(y)] = jnp.where(out_y == y, far(side), near(side))


def gather_product(cell, slots, first, plane, matrices, noise):
    parts = [plane[slots[first + 8 * cell + k]] for k in range(8)] + [noise[cell]]
    return jnp.dot(jnp.concatenate(parts, axis=1), matrices[cell], preferred_element_type=jnp.float32)


def settled_kernel(section, codes, table_in, plane_in, sums_in, matrices_in, noise_in, *rest):
    sources, rest = rest[:3], rest[3:]
    plane, sums, matrices, noise, table, settled, factors, sems = rest
    targets = noise, matrices, factors
    choose(section, table_in, table)
    each_cell(table, lambda cell: start_cell(cell, sources, targets, sems))

    def one_cell(at, found):
        cell = table[CELLS + at]
        fill_slots(cell, section, codes, table, settled)
        for k in range(8):
            table[ITEM + found] = 8 * cell + k
            found += (table[SLOT + 8 * cell + k] != settled[8 * cell + k]).astype(jnp.int32)
        return found

    table[COUNT] = lax.fori_loop(0, table[CHOSEN], one_cell, jnp.int32(0))

    def products(first, second, fresh):
        finish_cell(first, sources, targets, sems)

        @pl.when(fresh)
        def _():
            finish_cell(second, sources, targets, sems)

        both = [gather_product(cell, settled, 0, plane, matrices, noise) for cell in (first, second)]
        sums[first] = both[0]
        sums[second] = both[1]

    each_pair(table, products)


def rows_kernel(base, outward, plane_in, halo, plane):
    out_x, in_x, _, _ = edges()
    row = beyond(out_x if outward else in_x)
    for i in range(SIDE):
        plane[base + row * GRID + i + 1] = piece(halo, i)


def take_rows(base, plane, halo, name):
    for outward, part, products in ((True, halo[0], 16), (False, halo[1], 64)):
        plane = pl.pallas_call(
            functools.partial(rows_kernel, base, outward),
            out_shape=jax.ShapeDtypeStruct(plane.shape, plane.dtype),
            in_specs=[VMEM] * 2,
            out_specs=VMEM,
            input_output_aliases={0: 0},
            compiler_params=PARAMS,
            cost_estimate=cost(products, DEPTH),
            name=f"{name}_{'out' if outward else 'in'}",
        )(plane, part)
    return plane


def store_columns(base, plane, ty_out, ty_in):
    _, _, out_y, in_y = edges()
    for i in range(SIDE):
        plane[base + (i + 1) * GRID + beyond(out_y)] = piece(ty_out, i)
        plane[base + (i + 1) * GRID + beyond(in_y)] = piece(ty_in, i)


def pack_sends(base, plane, sends):
    tx_out, tx_in, ty_out, ty_in = sends
    out_x, in_x, out_y, in_y = edges()
    for i in range(SIDE):
        rows = pl.ds(i * ROWS, ROWS)
        tx_out[rows] = plane[own_slot(out_x, i)]
        tx_in[rows] = plane[own_slot(in_x, i)]
        ty_out[rows] = plane[own_slot(i, out_y)]
        ty_in[rows] = plane[own_slot(i, in_y)]
    for i, side in enumerate((out_x, in_x)):
        rows = pl.ds((SIDE + i) * ROWS, ROWS)
        ty_out[rows] = plane[base + beyond(side) * GRID + out_y + 1]
        ty_in[rows] = plane[base + beyond(side) * GRID + in_y + 1]


def fetch(table, scalars, sem):
    copy = pltpu.make_async_copy(table, scalars, sem)
    copy.start()
    return copy.wait


def first_kernel(table_in, plane_in, sums_in, matrices_in, noise_in, *rest):
    halo, extras, (plane, sums, matrices, noise, *sends) = rest[:2], rest[2], rest[3:-2]
    table, sem = rest[-2:]
    wait = fetch(table_in, table, sem)
    store_columns(0, plane, *halo)
    for at, ref in enumerate(sends):
        ref[ref.shape[0] - EXTRA :] = extras[at]
    wait()

    def products(first, second, fresh):
        cells = first, second
        both = [gather_product(cell, table, SLOT, plane, matrices, noise) for cell in cells]
        for cell, summed in zip(cells, both, strict=True):
            sums[cell] = summed
            plane[own_slot(cell // SIDE, cell % SIDE)] = summed.astype(jnp.bfloat16)

    each_pair(table, products)
    pack_sends(0, plane, sends)


def main_kernel(section, table_in, plane_in, sums_in, matrices, own, ty_out, ty_in, *rest):
    extras, rest = rest[:4], rest[4:]
    plane, sums, *rest, table, sem = rest
    wait = fetch(table_in, table, sem)
    extras = [ref.at[pl.ds(ref.shape[0] - EXTRA, EXTRA)] for ref in extras]
    corners = block_of(ty_out, SIDE), block_of(ty_in, SIDE)
    store_columns(PLANE, plane, ty_out, ty_in)
    if section == 1:
        store_corners(plane, *corners)
    complete_halo(section - 1, plane, extras)
    finish_corners(section - 1, own, plane, sums, *corners)
    wait()
    count = table[COUNT]

    def one_group(group, carry):
        products = []
        for i in range(GROUP):
            item = table[ITEM + jnp.minimum(group * GROUP + i, count - 1)]
            slot = jnp.where(group * GROUP + i < count, table[SLOT + item], BLANK)
            matrix = matrices[item // 8, pl.ds(pl.multiple_of((item % 8) * LANES, LANES), LANES)]
            products.append((item // 8, jnp.dot(plane[slot], matrix, preferred_element_type=jnp.float32)))
        for cell, product in products:
            sums[cell] += product
        return carry

    lax.fori_loop(0, (count + GROUP - 1) // GROUP, one_group, 0)

    def one_cell(cell):
        plane[own_slot(cell // SIDE, cell % SIDE)] = sums[cell].astype(jnp.bfloat16)

    each_cell(table, one_cell)
    if section < LEVELS - 1:
        pack_sends(PLANE, plane, rest)
    else:
        result, sems = rest
        copies = [
            pltpu.make_async_copy(
                plane.at[pl.ds(own_slot(x, 0), SIDE)], result.at[pl.ds(x * SIDE, SIDE)], sems.at[x]
            )
            for x in range(SIDE)
        ]
        for copy in copies:
            copy.start()
        for copy in copies:
            copy.wait()


def corner_kernel(plane_in, own, sums, far, near, result_in, plane, result, sems):
    changed = finish_corners(LEVELS - 1, own, plane, sums, block_of(far, 0), block_of(near, 0))
    copies = [
        pltpu.make_async_copy(plane.at[own_slot(x, y)], result.at[SIDE * x + y], sems.at[at])
        for at, (x, y) in enumerate(CORNERS)
    ]
    for copy, needed in zip(copies, changed, strict=True):
        pl.when(needed)(copy.start)
    for copy, needed in zip(copies, changed, strict=True):
        pl.when(needed)(copy.wait)


def cost(products, depth):
    flops = products * 2 * ROWS * depth * LANES
    return pl.CostEstimate(flops=flops, bytes_accessed=4 << 20, transcendentals=0)


def rows_of(rows):
    return jax.ShapeDtypeStruct((rows, LANES), jnp.bfloat16)


def local(earlier, innovation, conditioner, chol_factor, block_level, neighbours):
    block = earlier.shape[2:]
    tile = SIDE * SIDE
    keep = lambda value: pltpu.with_memory_space_constraint(value, pltpu.HBM)
    flat = lambda value: keep(value.reshape(tile, *value.shape[2:]))
    edge = jax.ShapeDtypeStruct((SIDE, *block), jnp.bfloat16)
    plane_shape = jax.ShapeDtypeStruct((BLANK + 1, *block), jnp.bfloat16)
    sums_shape = jax.ShapeDtypeStruct((tile, *block), jnp.float32)
    whole = jax.ShapeDtypeStruct((tile, *block), jnp.bfloat16)
    matrices_shape = jax.ShapeDtypeStruct((tile, DEPTH, LANES), jnp.bfloat16)
    table_shape = jax.ShapeDtypeStruct((TABLE,), jnp.int32)
    scalars = [pltpu.SMEM((TABLE,), jnp.int32), pltpu.SemaphoreType.DMA]
    factors = pltpu.VMEM((tile, *chol_factor.shape[2:]), jnp.bfloat16)
    sends = pl.pallas_call(
        pack_kernel,
        out_shape=[edge] * 4,
        in_specs=[HBM],
        out_specs=[VMEM] * 4,
        scratch_shapes=[pltpu.SemaphoreType.DMA((4,))],
        compiler_params=PARAMS,
        name="pack",
    )(keep(earlier))
    sends = [send.reshape(SIDE * ROWS, LANES) for send in sends]
    sources = flat(innovation), flat(conditioner), flat(chol_factor)
    plane, matrices, noise, sums, table, codes, own = pl.pallas_call(
        load_kernel,
        out_shape=[
            plane_shape,
            matrices_shape,
            whole,
            sums_shape,
            table_shape,
            jax.ShapeDtypeStruct(neighbours.shape, jnp.int32),
            jax.ShapeDtypeStruct((4, EXTRA, LANES), jnp.bfloat16),
        ],
        in_specs=[HBM] * 6,
        out_specs=[VMEM] * 4 + [SMEM] * 2 + [VMEM],
        scratch_shapes=[
            pltpu.SMEM(block_level.shape, jnp.int32),
            factors,
            pltpu.SemaphoreType.DMA((3, tile)),
            pltpu.SemaphoreType.DMA((14,)),
        ],
        compiler_params=PARAMS,
        cost_estimate=pl.CostEstimate(flops=0, bytes_accessed=10 << 20, transcendentals=0),
        name="load",
    )(keep(block_level), keep(neighbours), flat(earlier), *sources)
    halo = exchange(sends)
    plane = take_rows(0, plane, halo, "rows_0")
    send_rows = lambda extra: [rows_of(4 * ROWS + extra)] * 2 + [rows_of(6 * ROWS + extra)] * 2
    plane, sums, matrices, noise, *sends = pl.pallas_call(
        first_kernel,
        out_shape=[plane_shape, sums_shape, matrices_shape, whole, *send_rows(EXTRA)],
        in_specs=[VMEM] * 8,
        out_specs=[VMEM] * 8,
        scratch_shapes=scalars,
        input_output_aliases={1: 0, 2: 1, 3: 2, 4: 3},
        compiler_params=PARAMS,
        cost_estimate=cost(8, DEPTH),
        name="level_0",
    )(table, plane, sums, matrices, noise, *halo[2:], own)
    for section in range(1, LEVELS):
        final = section == LEVELS - 1
        halo = exchange(sends)
        if section == 1:
            extras = halo
        plane, sums, matrices, noise, items = pl.pallas_call(
            functools.partial(settled_kernel, section),
            out_shape=[plane_shape, sums_shape, matrices_shape, whole, table_shape],
            in_specs=[SMEM] * 2 + [VMEM] * 4 + [HBM] * 3,
            out_specs=[VMEM] * 4 + [SMEM],
            scratch_shapes=[
                pltpu.SMEM((8 * tile,), jnp.int32),
                factors,
                pltpu.SemaphoreType.DMA((3, tile)),
            ],
            input_output_aliases={2: 0, 3: 1, 4: 2, 5: 3},
            compiler_params=PARAMS,
            cost_estimate=cost(8, DEPTH),
            name=f"settled_{section}",
        )(codes, table, plane, sums, matrices, noise, *sources)
        plane = take_rows(PLANE, plane, halo, f"rows_{section}")
        if final:
            far, near = pl.pallas_call(
                forward_kernel,
                out_shape=[rows_of(2 * ROWS)] * 2,
                in_specs=[VMEM],
                out_specs=[VMEM] * 2,
                compiler_params=PARAMS,
                cost_estimate=cost(0, 0),
                name="forward",
            )(plane)
            far, near = swap(far, None, "out"), swap(near, None, "in")
        plane, sums, *sends = pl.pallas_call(
            functools.partial(main_kernel, section),
            out_shape=[plane_shape, sums_shape] + ([whole] if final else send_rows(0)),
            in_specs=[VMEM] * 11,
            out_specs=[VMEM] * 2 + ([HBM] if final else [VMEM] * 4),
            scratch_shapes=[pltpu.SemaphoreType.DMA((4,))] * final + scalars,
            input_output_aliases={1: 0, 2: 1},
            compiler_params=PARAMS,
            cost_estimate=cost(16, LANES),
            name=f"level_{section}",
        )(items, plane, sums, matrices, own, *halo[2:], *extras)
    _, result = pl.pallas_call(
        corner_kernel,
        out_shape=[plane_shape, whole],
        in_specs=[VMEM] * 5 + [HBM],
        out_specs=[VMEM, HBM],
        scratch_shapes=[pltpu.SemaphoreType.DMA((4,))],
        input_output_aliases={0: 0, 5: 1},
        compiler_params=PARAMS,
        cost_estimate=cost(4, LANES),
        name="last_corners",
    )(plane, own, sums, far, near, sends[0])
    return result.reshape(earlier.shape)


def solution(mesh):
    placed = (
        P("tx", "ty", None, None),
        P("tx", "ty", None, None),
        P("tx", "ty", None, None),
        P("tx", "ty", None, None),
        P("tx", "ty"),
        P("tx", "ty", None),
    )
    return jax.shard_map(
        local, mesh=mesh, in_specs=placed, out_specs=P("tx", "ty", None, None), check_vma=False
    )
```

```python
import functools

import jax
import jax.numpy as jnp
from jax import lax
from jax.experimental import pallas as pl
from jax.experimental.pallas import tpu as pltpu
from jax.sharding import PartitionSpec as P

LEVELS = 4
BOTH = ("tx", "ty")
SIDE = 4
GRID = 6
PLANE = GRID * GRID
BLANK = 2 * PLANE
ROWS = 256
LANES = 128
MARK = 16
EXTRA = 2 * (LANES + MARK)
DEPTH = 9 * LANES
LEVEL, SLOT, ITEM, CELLS, COUNT, CHOSEN, TABLE = 0, 16, 144, 216, 236, 237, 238
GROUP = 4
CORNERS = ((0, 0), (0, 3), (3, 0), (3, 3))
VMEM = pl.BlockSpec(memory_space=pltpu.VMEM)
SMEM = pl.BlockSpec(memory_space=pltpu.SMEM)
HBM = pl.BlockSpec(memory_space=pltpu.HBM)
PARAMS = pltpu.CompilerParams(vmem_limit_bytes=8 * 1024 * 1024)


def partner(at, size, kind):
    if kind == "in":
        return at ^ 1
    if kind == "out":
        return (at + 1) % size if at % 2 else (at - 1) % size
    return at


def swap(value, along_x, along_y):
    size_x, size_y = lax.axis_size("tx"), lax.axis_size("ty")
    pairs = [
        (x * size_y + y, partner(x, size_x, along_x) * size_y + partner(y, size_y, along_y))
        for x in range(size_x)
        for y in range(size_y)
    ]
    return lax.ppermute(value, BOTH, pairs)


def exchange(sends):
    tx_out, tx_in, ty_out, ty_in = sends
    return swap(tx_out, "out", None), swap(tx_in, "in", None), swap(ty_out, None, "out"), swap(ty_in, None, "in")


def edges():
    odd_x = lax.rem(lax.axis_index("tx"), 2)
    odd_y = lax.rem(lax.axis_index("ty"), 2)
    return 3 * odd_x, 3 - 3 * odd_x, 3 * odd_y, 3 - 3 * odd_y


def beyond(edge):
    return (edge // 3) * 5


def own_slot(x, y):
    return PLANE + (x + 1) * GRID + y + 1


def piece(ref, at):
    return ref[at * ROWS : (at + 1) * ROWS]


def forward_kernel(plane, far, near):
    out_x, in_x, out_y, in_y = edges()
    for i, side in enumerate((out_x, in_x)):
        far[i * ROWS : (i + 1) * ROWS] = plane[PLANE + beyond(side) * GRID + out_y + 1]
        near[i * ROWS : (i + 1) * ROWS] = plane[PLANE + beyond(side) * GRID + in_y + 1]


def pack_kernel(earlier, tx_out, tx_in, ty_out, ty_in, sems):
    out_x, in_x, out_y, in_y = edges()
    copies = [
        pltpu.make_async_copy(earlier.at[out_x], tx_out, sems.at[0]),
        pltpu.make_async_copy(earlier.at[in_x], tx_in, sems.at[1]),
        pltpu.make_async_copy(earlier.at[:, out_y], ty_out, sems.at[2]),
        pltpu.make_async_copy(earlier.at[:, in_y], ty_in, sems.at[3]),
    ]
    for copy in copies:
        copy.start()
    for copy in copies:
        copy.wait()


def late_code(levels, codes, x, y):
    code = 2 * x + 2 * y // 3 + jnp.where(levels[x, y] > 0, 9, 0)
    found = jnp.int32(-1)
    for k in range(8):
        found = jnp.where(codes[x, y, k] == code, k, found)
    return found


def fill_slots(cell, level, codes, every, settled):
    x, y = cell // SIDE, cell % SIDE
    for k in range(8):
        code = codes[x, y, k]
        old = code >= 9
        offset = jnp.where(old, code - 9, code)
        down = (offset >= 3).astype(jnp.int32) + (offset >= 6).astype(jnp.int32)
        row, column = x + down, y + offset - 3 * down
        slot = row * GRID + column + jnp.where(old, PLANE, 0)
        edge_row, edge_column = (row == 0) | (row == 5), (column == 0) | (column == 5)
        outer = edge_row & edge_column
        waits = outer & (old == (level > 0))
        every[SLOT + 8 * cell + k] = jnp.where(waits, BLANK, slot)
        if settled is not None:
            own_corner = ((row == 1) | (row == 4)) & ((column == 1) | (column == 4))
            open_ = (old & (edge_row | edge_column | own_corner)) | outer
            settled[8 * cell + k] = jnp.where(open_, BLANK, slot)


def choose(section, levels, table):
    def one_cell(cell, at):
        table[CELLS + at] = cell
        return at + (levels[LEVEL + cell] == section).astype(jnp.int32)

    table[CHOSEN] = lax.fori_loop(0, SIDE * SIDE, one_cell, jnp.int32(0))


def each_cell(table, body):
    def one_cell(at, carry):
        body(table[CELLS + at])
        return carry

    lax.fori_loop(0, table[CHOSEN], one_cell, 0)


def each_pair(table, body):
    count = table[CHOSEN]

    def one_pair(pair, carry):
        second = jnp.minimum(2 * pair + 1, count - 1)
        body(table[CELLS + 2 * pair], table[CELLS + second], 2 * pair + 1 < count)
        return carry

    lax.fori_loop(0, (count + 1) // 2, one_pair, 0)


def cell_copies(cell, sources, targets, sems):
    innovation, conditioner, chol_factor = sources
    noise, matrices, factors = targets
    return (
        pltpu.make_async_copy(chol_factor.at[cell], factors.at[cell], sems.at[0, cell]),
        pltpu.make_async_copy(innovation.at[cell], noise.at[cell], sems.at[1, cell]),
        pltpu.make_async_copy(conditioner.at[cell], matrices.at[cell, pl.ds(0, 8 * LANES)], sems.at[2, cell]),
    )


def start_cell(cell, sources, targets, sems):
    for copy in cell_copies(cell, sources, targets, sems):
        copy.start()


def finish_cell(cell, sources, targets, sems):
    _, matrices, factors = targets
    copies = cell_copies(cell, sources, targets, sems)
    copies[0].wait()
    rows = lax.broadcasted_iota(jnp.int32, (LANES, LANES), 0)
    columns = lax.broadcasted_iota(jnp.int32, (LANES, LANES), 1)
    upper = jnp.where(rows <= columns, factors[cell].astype(jnp.float32), 0.0)
    matrices[cell, 8 * LANES :] = upper.astype(jnp.bfloat16)
    copies[1].wait()
    copies[2].wait()


def load_kernel(
    block_level, neighbours, earlier, innovation, conditioner, chol_factor, plane, matrices, noise, sums, table, codes, extras, *rest
):
    levels, factors, sems, more_sems = rest
    scalars = [
        pltpu.make_async_copy(block_level, levels, more_sems.at[12]),
        pltpu.make_async_copy(neighbours, codes, more_sems.at[13]),
    ]
    copies = [
        pltpu.make_async_copy(
            earlier.at[pl.ds(x * SIDE, SIDE)], plane.at[pl.ds((x + 1) * GRID + 1, SIDE)], more_sems.at[x]
        )
        for x in range(SIDE)
    ]
    for copy in scalars + copies:
        copy.start()

    def clear(at, carry):
        plane[at] = jnp.zeros(plane.shape[1:], plane.dtype)
        return carry

    lax.fori_loop(PLANE, BLANK + 1, clear, 0)
    for copy in scalars:
        copy.wait()
    for cell in range(SIDE * SIDE):
        table[LEVEL + cell] = levels[cell // SIDE, cell % SIDE]
    sources, targets = (innovation, conditioner, chol_factor), (noise, matrices, factors)
    choose(0, table, table)
    each_cell(table, lambda cell: start_cell(cell, sources, targets, sems))
    out_x, _, out_y, _ = edges()
    for at, (x, y) in enumerate(CORNERS):
        late = late_code(levels, codes, x, y)
        mark = jnp.full((MARK, LANES), jnp.where(late >= 0, levels[x, y], -1).astype(jnp.float32)).astype(jnp.bfloat16)
        start = pl.multiple_of(LANES * jnp.maximum(late, 0), LANES)
        matrix = conditioner.at[SIDE * x + y, pl.ds(start, LANES)]
        for way, (side, place) in enumerate(((jnp.where(out_x == x, 0, 1), y // 3), (jnp.where(out_y == y, 2, 3), x // 3))):
            copy = pltpu.make_async_copy(
                matrix, extras.at[side, pl.ds(place * LANES, LANES)], more_sems.at[4 + 2 * at + way]
            )
            copy.start()
            copies.append(copy)
            extras[side, 2 * LANES + place * MARK : 2 * LANES + (place + 1) * MARK] = mark
    each_cell(table, lambda cell: fill_slots(cell, 0, codes, table, None))
    each_cell(table, lambda cell: finish_cell(cell, sources, targets, sems))
    for copy in copies:
        copy.wait()


def read_mark(extra, place):
    return jnp.max(extra[2 * LANES + place * MARK : 2 * LANES + (place + 1) * MARK].astype(jnp.float32))


def complete_halo(recent, plane, extras):
    out_x, in_x, out_y, in_y = edges()
    source = PLANE if recent else 0
    todo = []
    for side in (out_x, in_x):
        for place in (0, 1):
            todo.append((beyond(side) * GRID + 1 + 3 * place, (side + 1) * GRID + 5 * place))
    for side in (out_y, in_y):
        for place in (0, 1):
            todo.append(((1 + 3 * place) * GRID + beyond(side), 5 * place * GRID + side + 1))
    marks = [read_mark(extra, place) for extra in extras for place in (0, 1)]
    for at, (cell, other) in enumerate(todo):

        @pl.when(marks[at] == recent)
        def _(cell=cell, other=other, extra=extras[at // 2], place=at % 2):
            product = jnp.dot(
                plane[source + other], extra[place * LANES : (place + 1) * LANES], preferred_element_type=jnp.float32
            )
            plane[PLANE + cell] = (plane[PLANE + cell].astype(jnp.float32) + product).astype(jnp.bfloat16)


def finish_corners(recent, extras, plane, sums, far, near):
    out_x, _, out_y, _ = edges()
    facing = [extras.at[jnp.where(out_y == y, 2, 3)] for _, y in CORNERS]
    places = [x // 3 for x, _ in CORNERS]
    marks = [read_mark(extra, place) for extra, place in zip(facing, places, strict=True)]
    for (x, y), extra, place, mark in zip(CORNERS, facing, places, marks, strict=True):

        @pl.when(mark == recent)
        def _(x=x, y=y, extra=extra, place=place):
            side = jnp.where(out_x == x, 0, 1)
            block = jnp.where(out_y == y, far(side), near(side))
            matrix = extra[place * LANES : (place + 1) * LANES]
            summed = sums[SIDE * x + y] + jnp.dot(block, matrix, preferred_element_type=jnp.float32)
            plane[own_slot(x, y)] = summed.astype(jnp.bfloat16)

    return [mark == recent for mark in marks]


def block_of(ref, first):
    return lambda at: ref[pl.ds(pl.multiple_of((first + at) * ROWS, ROWS), ROWS)]


def store_corners(plane, far, near):
    out_x, _, out_y, _ = edges()
    for x, y in CORNERS:
        side = jnp.where(out_x == x, 0, 1)
        plane[beyond(x) * GRID + beyond(y)] = jnp.where(out_y == y, far(side), near(side))


def gather_product(cell, slots, first, plane, matrices, noise):
    parts = [plane[slots[first + 8 * cell + k]] for k in range(8)] + [noise[cell]]
    return jnp.dot(jnp.concatenate(parts, axis=1), matrices[cell], preferred_element_type=jnp.float32)


def settled_kernel(section, codes, table_in, plane_in, sums_in, matrices_in, noise_in, *rest):
    sources, rest = rest[:3], rest[3:]
    plane, sums, matrices, noise, table, settled, factors, sems = rest
    targets = noise, matrices, factors
    choose(section, table_in, table)
    each_cell(table, lambda cell: start_cell(cell, sources, targets, sems))

    def one_cell(at, found):
        cell = table[CELLS + at]
        fill_slots(cell, section, codes, table, settled)
        for k in range(8):
            table[ITEM + found] = 8 * cell + k
            found += (table[SLOT + 8 * cell + k] != settled[8 * cell + k]).astype(jnp.int32)
        return found

    table[COUNT] = lax.fori_loop(0, table[CHOSEN], one_cell, jnp.int32(0))

    def products(first, second, fresh):
        finish_cell(first, sources, targets, sems)

        @pl.when(fresh)
        def _():
            finish_cell(second, sources, targets, sems)

        both = [gather_product(cell, settled, 0, plane, matrices, noise) for cell in (first, second)]
        sums[first] = both[0]
        sums[second] = both[1]

    each_pair(table, products)


def rows_kernel(base, outward, plane_in, halo, plane):
    out_x, in_x, _, _ = edges()
    row = beyond(out_x if outward else in_x)
    for i in range(SIDE):
        plane[base + row * GRID + i + 1] = piece(halo, i)


def take_rows(base, plane, halo, name):
    for outward, part, products in ((True, halo[0], 16), (False, halo[1], 64)):
        plane = pl.pallas_call(
            functools.partial(rows_kernel, base, outward),
            out_shape=jax.ShapeDtypeStruct(plane.shape, plane.dtype),
            in_specs=[VMEM] * 2,
            out_specs=VMEM,
            input_output_aliases={0: 0},
            compiler_params=PARAMS,
            cost_estimate=cost(products, DEPTH),
            name=f"{name}_{'out' if outward else 'in'}",
        )(plane, part)
    return plane


def store_columns(base, plane, ty_out, ty_in):
    _, _, out_y, in_y = edges()
    for i in range(SIDE):
        plane[base + (i + 1) * GRID + beyond(out_y)] = piece(ty_out, i)
        plane[base + (i + 1) * GRID + beyond(in_y)] = piece(ty_in, i)


def pack_sends(base, plane, sends):
    tx_out, tx_in, ty_out, ty_in = sends
    out_x, in_x, out_y, in_y = edges()
    for i in range(SIDE):
        rows = pl.ds(i * ROWS, ROWS)
        tx_out[rows] = plane[own_slot(out_x, i)]
        tx_in[rows] = plane[own_slot(in_x, i)]
        ty_out[rows] = plane[own_slot(i, out_y)]
        ty_in[rows] = plane[own_slot(i, in_y)]
    for i, side in enumerate((out_x, in_x)):
        rows = pl.ds((SIDE + i) * ROWS, ROWS)
        ty_out[rows] = plane[base + beyond(side) * GRID + out_y + 1]
        ty_in[rows] = plane[base + beyond(side) * GRID + in_y + 1]


def fetch(table, scalars, sem):
    copy = pltpu.make_async_copy(table, scalars, sem)
    copy.start()
    return copy.wait


def first_kernel(table_in, plane_in, sums_in, matrices_in, noise_in, *rest):
    halo, extras, (plane, sums, matrices, noise, *sends) = rest[:2], rest[2], rest[3:-2]
    table, sem = rest[-2:]
    wait = fetch(table_in, table, sem)
    store_columns(0, plane, *halo)
    for at, ref in enumerate(sends):
        ref[ref.shape[0] - EXTRA :] = extras[at]
    wait()

    count = table[CHOSEN]

    def one_group(group, carry):
        cells = [table[CELLS + jnp.minimum(GROUP * group + i, count - 1)] for i in range(GROUP)]
        products = [gather_product(cell, table, SLOT, plane, matrices, noise) for cell in cells]
        for cell, summed in zip(cells, products, strict=True):
            sums[cell] = summed
            plane[own_slot(cell // SIDE, cell % SIDE)] = summed.astype(jnp.bfloat16)
        return carry

    lax.fori_loop(0, (count + GROUP - 1) // GROUP, one_group, 0)
    pack_sends(0, plane, sends)


def main_kernel(section, table_in, plane_in, sums_in, matrices, own, ty_out, ty_in, *rest):
    extras, rest = rest[:4], rest[4:]
    plane, sums, *rest, table, sem = rest
    wait = fetch(table_in, table, sem)
    extras = [ref.at[pl.ds(ref.shape[0] - EXTRA, EXTRA)] for ref in extras]
    corners = block_of(ty_out, SIDE), block_of(ty_in, SIDE)
    store_columns(PLANE, plane, ty_out, ty_in)
    if section == 1:
        store_corners(plane, *corners)
    complete_halo(section - 1, plane, extras)
    finish_corners(section - 1, own, plane, sums, *corners)
    wait()
    count = table[COUNT]

    def one_group(group, carry):
        products = []
        for i in range(GROUP):
            item = table[ITEM + jnp.minimum(group * GROUP + i, count - 1)]
            slot = jnp.where(group * GROUP + i < count, table[SLOT + item], BLANK)
            matrix = matrices[item // 8, pl.ds(pl.multiple_of((item % 8) * LANES, LANES), LANES)]
            products.append((item // 8, jnp.dot(plane[slot], matrix, preferred_element_type=jnp.float32)))
        for cell, product in products:
            sums[cell] += product
        return carry

    lax.fori_loop(0, (count + GROUP - 1) // GROUP, one_group, 0)

    def one_cell(cell):
        plane[own_slot(cell // SIDE, cell % SIDE)] = sums[cell].astype(jnp.bfloat16)

    each_cell(table, one_cell)
    if section < LEVELS - 1:
        pack_sends(PLANE, plane, rest)
    else:
        result, sems = rest
        copies = [
            pltpu.make_async_copy(
                plane.at[pl.ds(own_slot(x, 0), SIDE)], result.at[pl.ds(x * SIDE, SIDE)], sems.at[x]
            )
            for x in range(SIDE)
        ]
        for copy in copies:
            copy.start()
        for copy in copies:
            copy.wait()


def corner_kernel(plane_in, own, sums, far, near, result_in, plane, result, sems):
    changed = finish_corners(LEVELS - 1, own, plane, sums, block_of(far, 0), block_of(near, 0))
    copies = [
        pltpu.make_async_copy(plane.at[own_slot(x, y)], result.at[SIDE * x + y], sems.at[at])
        for at, (x, y) in enumerate(CORNERS)
    ]
    for copy, needed in zip(copies, changed, strict=True):
        pl.when(needed)(copy.start)
    for copy, needed in zip(copies, changed, strict=True):
        pl.when(needed)(copy.wait)


def cost(products, depth):
    flops = products * 2 * ROWS * depth * LANES
    return pl.CostEstimate(flops=flops, bytes_accessed=4 << 20, transcendentals=0)


def rows_of(rows):
    return jax.ShapeDtypeStruct((rows, LANES), jnp.bfloat16)


def local(earlier, innovation, conditioner, chol_factor, block_level, neighbours):
    block = earlier.shape[2:]
    tile = SIDE * SIDE
    keep = lambda value: pltpu.with_memory_space_constraint(value, pltpu.HBM)
    flat = lambda value: keep(value.reshape(tile, *value.shape[2:]))
    edge = jax.ShapeDtypeStruct((SIDE, *block), jnp.bfloat16)
    plane_shape = jax.ShapeDtypeStruct((BLANK + 1, *block), jnp.bfloat16)
    sums_shape = jax.ShapeDtypeStruct((tile, *block), jnp.float32)
    whole = jax.ShapeDtypeStruct((tile, *block), jnp.bfloat16)
    matrices_shape = jax.ShapeDtypeStruct((tile, DEPTH, LANES), jnp.bfloat16)
    table_shape = jax.ShapeDtypeStruct((TABLE,), jnp.int32)
    scalars = [pltpu.SMEM((TABLE,), jnp.int32), pltpu.SemaphoreType.DMA]
    factors = pltpu.VMEM((tile, *chol_factor.shape[2:]), jnp.bfloat16)
    sends = pl.pallas_call(
        pack_kernel,
        out_shape=[edge] * 4,
        in_specs=[HBM],
        out_specs=[VMEM] * 4,
        scratch_shapes=[pltpu.SemaphoreType.DMA((4,))],
        compiler_params=PARAMS,
        name="pack",
    )(keep(earlier))
    sends = [send.reshape(SIDE * ROWS, LANES) for send in sends]
    sources = flat(innovation), flat(conditioner), flat(chol_factor)
    plane, matrices, noise, sums, table, codes, own = pl.pallas_call(
        load_kernel,
        out_shape=[
            plane_shape,
            matrices_shape,
            whole,
            sums_shape,
            table_shape,
            jax.ShapeDtypeStruct(neighbours.shape, jnp.int32),
            jax.ShapeDtypeStruct((4, EXTRA, LANES), jnp.bfloat16),
        ],
        in_specs=[HBM] * 6,
        out_specs=[VMEM] * 4 + [SMEM] * 2 + [VMEM],
        scratch_shapes=[
            pltpu.SMEM(block_level.shape, jnp.int32),
            factors,
            pltpu.SemaphoreType.DMA((3, tile)),
            pltpu.SemaphoreType.DMA((14,)),
        ],
        compiler_params=PARAMS,
        cost_estimate=pl.CostEstimate(flops=0, bytes_accessed=10 << 20, transcendentals=0),
        name="load",
    )(keep(block_level), keep(neighbours), flat(earlier), *sources)
    halo = exchange(sends)
    plane = take_rows(0, plane, halo, "rows_0")
    send_rows = lambda extra: [rows_of(4 * ROWS + extra)] * 2 + [rows_of(6 * ROWS + extra)] * 2
    plane, sums, matrices, noise, *sends = pl.pallas_call(
        first_kernel,
        out_shape=[plane_shape, sums_shape, matrices_shape, whole, *send_rows(EXTRA)],
        in_specs=[VMEM] * 8,
        out_specs=[VMEM] * 8,
        scratch_shapes=scalars,
        input_output_aliases={1: 0, 2: 1, 3: 2, 4: 3},
        compiler_params=PARAMS,
        cost_estimate=cost(8, DEPTH),
        name="level_0",
    )(table, plane, sums, matrices, noise, *halo[2:], own)
    for section in range(1, LEVELS):
        final = section == LEVELS - 1
        halo = exchange(sends)
        if section == 1:
            extras = halo
        plane, sums, matrices, noise, items = pl.pallas_call(
            functools.partial(settled_kernel, section),
            out_shape=[plane_shape, sums_shape, matrices_shape, whole, table_shape],
            in_specs=[SMEM] * 2 + [VMEM] * 4 + [HBM] * 3,
            out_specs=[VMEM] * 4 + [SMEM],
            scratch_shapes=[
                pltpu.SMEM((8 * tile,), jnp.int32),
                factors,
                pltpu.SemaphoreType.DMA((3, tile)),
            ],
            input_output_aliases={2: 0, 3: 1, 4: 2, 5: 3},
            compiler_params=PARAMS,
            cost_estimate=cost(8, DEPTH),
            name=f"settled_{section}",
        )(codes, table, plane, sums, matrices, noise, *sources)
        plane = take_rows(PLANE, plane, halo, f"rows_{section}")
        if final:
            far, near = pl.pallas_call(
                forward_kernel,
                out_shape=[rows_of(2 * ROWS)] * 2,
                in_specs=[VMEM],
                out_specs=[VMEM] * 2,
                compiler_params=PARAMS,
                cost_estimate=cost(0, 0),
                name="forward",
            )(plane)
            far, near = swap(far, None, "out"), swap(near, None, "in")
        plane, sums, *sends = pl.pallas_call(
            functools.partial(main_kernel, section),
            out_shape=[plane_shape, sums_shape] + ([whole] if final else send_rows(0)),
            in_specs=[VMEM] * 11,
            out_specs=[VMEM] * 2 + ([HBM] if final else [VMEM] * 4),
            scratch_shapes=[pltpu.SemaphoreType.DMA((4,))] * final + scalars,
            input_output_aliases={1: 0, 2: 1},
            compiler_params=PARAMS,
            cost_estimate=cost(16, LANES),
            name=f"level_{section}",
        )(items, plane, sums, matrices, own, *halo[2:], *extras)
    _, result = pl.pallas_call(
        corner_kernel,
        out_shape=[plane_shape, whole],
        in_specs=[VMEM] * 5 + [HBM],
        out_specs=[VMEM, HBM],
        scratch_shapes=[pltpu.SemaphoreType.DMA((4,))],
        input_output_aliases={0: 0, 5: 1},
        compiler_params=PARAMS,
        cost_estimate=cost(4, LANES),
        name="last_corners",
    )(plane, own, sums, far, near, sends[0])
    return result.reshape(earlier.shape)


def solution(mesh):
    placed = (
        P("tx", "ty", None, None),
        P("tx", "ty", None, None),
        P("tx", "ty", None, None),
        P("tx", "ty", None, None),
        P("tx", "ty"),
        P("tx", "ty", None),
    )
    return jax.shard_map(
        local, mesh=mesh, in_specs=placed, out_specs=P("tx", "ty", None, None), check_vma=False
    )
```
